32 devices in a mesh: rows: 8 (over z, y), pair: 4 (over x, core).
Axes of the slice: x: 2, y: 2, z: 4, core: 2. Of those that a mesh axis runs over, the one named last changes fastest.
Arguments:
- a_tiles: bfloat16 [2048, 8, 4096], P(('rows', 'pair')), may hold values from -2.09375 to 2.09375
- p_tiles: bfloat16 [2048, 4096], P(('rows', 'pair')), may hold values from -0.75 to 0.75
- a_cols: int32 [2048, 8], P(('rows', 'pair')), may hold values from 0 to 2047, as said below
- tile_group: int32 [2048, 8], P(('rows', 'pair')), may hold values from 0 to 1
- coarse_slots: int32 [2048, 2], P(('rows', 'pair')), may hold values from 0 to 15
- aggregate: int32 [2048], P(('rows', 'pair')), may hold values from 0 to 127, as said below
Outputs:
- coarse_tiles: float32 [128, 16, 4096], P(('rows', 'pair'))
The draws below stay inside these ranges and needn't reach their ends.
Inputs may be any that keep to these rules, and one draw needn't show every extreme that they name: `a_cols`: each operator tile's column block lies within 2 block rows of its own block row. `aggregate`: coarse block rows come in groups of 16 consecutive ones, group g held by index g of rows; the fine block rows of one device name at most 16 rows of one group, and one group, drawn from the seed, gets exactly 16 from every device.
All inputs are finite; a program needn't handle non-finite values.
Results may differ from the reference program's by a relative error of at most 0.0041.
Values may be sent and summed in bfloat16 or wider, within the bound.
A program may use at most 128 MiB of HBM per device.

```python
import jax
import jax.numpy as jnp
from jax import lax

BLK = 64
KA = 8
KS = 2
KC = 16
HB = 2
FB = 64
CB = 4
NF = 2048
NC = 128
N_ROWS = 8
N_PAIR = 4


def draw_a_cols(key, part):
    row_ids = jnp.arange(NF, dtype=jnp.int32)
    offset = jax.random.randint(key, (NF, KA), -HB, HB + 1, dtype=jnp.int32)
    return jnp.clip(row_ids[:, None] + offset, 0, NF - 1).astype(jnp.int32)


def draw_aggregate(key, part):
    capacity = 2 * FB // N_ROWS
    group_size = CB * N_PAIR
    busy_group = jax.random.randint(jax.random.fold_in(key, 1), (), 0, N_ROWS, dtype=jnp.int32)

    def one_device(device):
        device_key = jax.random.fold_in(key, device + 7)
        slot_ids = jax.random.permutation(jax.random.fold_in(device_key, 1), (N_ROWS - 1) * capacity)[:FB - capacity]
        others = (slot_ids // capacity).astype(jnp.int32)
        others = others + (others >= busy_group).astype(jnp.int32)
        groups = jnp.concatenate([jnp.full((capacity,), busy_group, jnp.int32), others])
        order_rows = jax.random.permutation(jax.random.fold_in(device_key, 2), FB)
        groups = groups[order_rows]
        local_rows = jax.random.randint(jax.random.fold_in(device_key, 3), (FB,), 0, group_size, dtype=jnp.int32)
        return groups * group_size + local_rows
    return jax.vmap(one_device)(jnp.arange(N_ROWS * N_PAIR, dtype=jnp.int32)).reshape(-1).astype(jnp.int32)


def with_ends(drawn, key, low, high):
    extent = drawn.shape
    place = [jax.random.randint(jax.random.fold_in(key, axis), (), 0, extent[axis]) for axis in range(len(extent))]
    drawn = drawn.at[tuple(place)].set(low)
    longest = extent.index(max(extent))
    place[longest] = (place[longest] + 1) % extent[longest]
    return drawn.at[tuple(place)].set(high)


def shard_levels(own_key, dims, cuts, low, top_value):
    level = 1.0
    for dim, shards_of in cuts:
        heights = jax.random.uniform(jax.random.fold_in(jax.random.fold_in(own_key, 6), dim), (shards_of,), jnp.float32, low / len(cuts), top_value / len(cuts))
        level = level * jnp.repeat(jnp.exp(heights), dims[dim] // shards_of).reshape((-1,) + (1,) * (len(dims) - 1 - dim))
    return level


def gaussian(rng, extent, deviation, reach, pieces=(), kind=jnp.bfloat16):
    gain = shard_levels(rng, extent, pieces, -0.22, 0.18) if pieces else 1.0
    drawn = jax.random.normal(rng, extent, jnp.float32) * deviation * gain
    return jnp.minimum(jnp.maximum(drawn, -reach), reach).astype(kind)


def setup_inputs(seed: int = 0) -> dict:
    streams_of = jax.random.split(jax.random.key(seed), 7)
    a_tiles = gaussian(streams_of[0], (NF, KA, BLK * BLK), 0.35, 2.09375, ((0, 32),))
    p_tiles = gaussian(streams_of[1], (NF, BLK * BLK), BLK ** -0.5, 0.75, ((0, 32),))
    a_cols = draw_a_cols(jax.random.fold_in(streams_of[6], 71), 0)
    tile_group = with_ends(jax.random.randint(streams_of[3], (NF, KA), 0, KS), jax.random.fold_in(streams_of[3], 1), 0, KS - 1).astype(jnp.int32)
    coarse_slots = with_ends(jax.random.randint(streams_of[4], (NF, KS), 0, KC), jax.random.fold_in(streams_of[4], 1), 0, KC - 1).astype(jnp.int32)
    aggregate = draw_aggregate(jax.random.fold_in(streams_of[6], 71), 0)
    return dict(a_tiles=a_tiles, p_tiles=p_tiles, a_cols=a_cols, tile_group=tile_group, coarse_slots=coarse_slots, aggregate=aggregate)


def reshape_blocks(values):
    return values.reshape((NF // FB, FB) + values.shape[1:])


def reference(a_tiles, p_tiles, a_cols, tile_group, coarse_slots, aggregate):
    def advance(carry, inputs):
        a_block, col_block, pick_block, slot_block, agg_block, own_block = inputs
        near_tiles = p_tiles[col_block].astype(jnp.float32).reshape(FB, KA, BLK, BLK)
        a_float = a_block.astype(jnp.float32).reshape(FB, KA, BLK, BLK)
        products = jnp.einsum("tkab,tkbc->tkac", a_float, near_tiles).astype(jnp.bfloat16)
        products = products.reshape(FB, KA, BLK * BLK).astype(jnp.float32)
        selector = (pick_block[:, :, None] == jnp.arange(KS, dtype=jnp.int32)[None, None, :]).astype(jnp.float32)
        slot_sums = jnp.einsum("tks,tkf->tsf", selector, products).astype(jnp.bfloat16)
        own_float = own_block.astype(jnp.float32).reshape(FB, BLK, BLK)
        terms = jnp.einsum("tji,tsjc->tsic", own_float, slot_sums.astype(jnp.float32).reshape(FB, KS, BLK, BLK))
        terms = terms.reshape(FB * KS, BLK * BLK)
        targets = (agg_block[:, None] * KC + slot_block).reshape(-1).astype(jnp.int32)
        return carry.at[targets].add(terms), None

    start = jnp.zeros((NC * KC, BLK * BLK), jnp.float32)
    result, _ = lax.scan(advance, start, (reshape_blocks(a_tiles), reshape_blocks(a_cols), reshape_blocks(tile_group), reshape_blocks(coarse_slots), reshape_blocks(aggregate), reshape_blocks(p_tiles)))
    return result.reshape(NC, KC, BLK * BLK)
```

```python
import functools

import jax
import jax.numpy as jnp
from jax import lax
from jax.experimental import pallas as pl
from jax.experimental.pallas import tpu as pltpu
from jax.sharding import PartitionSpec as P

BLK = 64
KA = 8
KS = 2
KC = 16
HB = 2
RATIO = 16
LANES = 128
NEAR = 2 * HB + 1
CHUNK = 8
BOTH = ("rows", "pair")


def extended(array, width):
    devices, length = lax.axis_size(BOTH), array.shape[0]
    up = [(i, i + 1) for i in range(devices - 1)]
    down = [(j, i) for i, j in up]
    before = lax.ppermute(array[length - width :], BOTH, up)
    after = lax.ppermute(array[:width], BOTH, down)
    return jnp.concatenate([before, array, after], axis=0)


def iota(shape, dim):
    return lax.broadcasted_iota(jnp.int32, shape, dim)


def put_diagonal(flat, want, low):
    flat = flat.astype(jnp.float32)
    turned = pltpu.roll(flat, BLK, 1)
    zero = jnp.zeros_like(flat)
    parts = jnp.concatenate(
        [
            jnp.where(low, flat, zero),
            jnp.where(low, turned, zero),
            jnp.where(low, zero, turned),
            jnp.where(low, zero, flat),
        ],
        axis=0,
    ).astype(jnp.bfloat16)
    return jnp.dot(want, parts, preferred_element_type=jnp.float32).astype(jnp.bfloat16)


def constants():
    q = BLK // 2
    r, k = iota((LANES, LANES), 0), iota((LANES, LANES), 1)
    want = jnp.where(
        (r // BLK == k // BLK) & (r % BLK == 2 * (k % q) + (k // q) % 2), 1.0, 0.0
    ).astype(jnp.bfloat16)
    eye = jnp.where(r == k, 1.0, 0.0).astype(jnp.bfloat16)
    spread = jnp.where(
        iota((q, q * KA), 0) == iota((q, q * KA), 1) // KA, 1.0, 0.0
    ).astype(jnp.bfloat16)
    low = iota((q, LANES), 1) < BLK
    return want, eye, spread, low


def row_terms(read, code, group, near, own, eye, spread, low):
    q = BLK // 2
    tiles = jnp.concatenate([read(c).astype(jnp.float32) for c in range(q)], axis=0)
    tiles = tiles.astype(jnp.bfloat16)

    def picked(j):
        one = jnp.where(code == j, 1.0, 0.0)
        pair = jnp.concatenate([one, one], axis=0).astype(jnp.bfloat16)
        return jnp.broadcast_to(pair[None], (q // 2,) + pair.shape).reshape(tiles.shape)

    left = jnp.concatenate([tiles * picked(j) for j in range(NEAR)], axis=1)
    products = jnp.dot(left, near, preferred_element_type=jnp.float32).astype(jnp.bfloat16)
    turned = lax.dot_general(
        eye, own, (((1,), (1,)), ((), ())), preferred_element_type=jnp.float32
    ).astype(jnp.bfloat16)
    wide = jnp.dot(turned, spread, preferred_element_type=jnp.float32).astype(jnp.bfloat16)
    rows = jnp.concatenate(
        [wide * jnp.where(group == s, 1.0, 0.0).astype(jnp.bfloat16) for s in range(KS)], axis=0
    )
    full = jnp.dot(rows, products, preferred_element_type=jnp.float32)
    terms = []
    for s in range(KS):
        part = full[s * LANES : (s + 1) * LANES]
        terms.append(
            jnp.where(low, part[:q], part[3 * q :])
            + pltpu.roll(jnp.where(low, part[q : 2 * q], part[2 * q : 3 * q]), BLK, 1)
        )
    return terms


def terms_kernel(a_ref, p_ref, code_ref, group_ref, out_ref, diag, stage):
    step = pl.program_id(0)
    q = BLK // 2
    want, eye, spread, low = constants()

    @pl.when(step == 0)
    def _():
        def one(t, _):
            diag[pl.ds(pl.multiple_of(t * LANES, LANES), LANES), :] = put_diagonal(p_ref[t], want, low)
            return 0

        lax.fori_loop(0, p_ref.shape[0], one, 0, unroll=4)

    for i in range(CHUNK):
        row = step * CHUNK + i
        terms = row_terms(
            lambda c: a_ref[i, :, c * LANES : (c + 1) * LANES],
            code_ref[i],
            group_ref[i],
            diag[pl.ds(pl.multiple_of(row * LANES, LANES), NEAR * LANES), :],
            p_ref[row + HB],
            eye,
            spread,
            low,
        )
        for s in range(KS):
            stage[pl.ds(s * CHUNK + i, q, stride=KS * CHUNK), :] = terms[s]
    out_ref[...] = stage[...].astype(jnp.bfloat16).reshape(out_ref.shape)


def row_codes(a_cols, tile_group):
    fine_rows = a_cols.shape[0]
    q = BLK // 2
    own = lax.axis_index(BOTH) * fine_rows + jnp.arange(fine_rows, dtype=jnp.int32)
    offset = a_cols - own[:, None] + HB
    code = jnp.broadcast_to(offset[:, :, None], (fine_rows, KA, LANES))
    group = jnp.tile(tile_group, (1, q)).reshape(fine_rows, 1, q * KA)
    return code, group


def local_terms(a_tiles, p_tiles, a_cols, tile_group):
    fine_rows = a_tiles.shape[0]
    q = BLK // 2
    near_p = extended(p_tiles, HB).reshape(fine_rows + 2 * HB, q, LANES)
    code, group = row_codes(a_cols, tile_group)
    steps = fine_rows // CHUNK
    return pl.pallas_call(
        terms_kernel,
        grid=(steps,),
        in_specs=[
            pl.BlockSpec((CHUNK, KA, BLK * BLK), lambda g: (g, 0, 0)),
            pl.BlockSpec((fine_rows + 2 * HB, q, LANES), lambda g: (0, 0, 0)),
            pl.BlockSpec((CHUNK, KA, LANES), lambda g: (g, 0, 0)),
            pl.BlockSpec((CHUNK, 1, q * KA), lambda g: (g, 0, 0)),
        ],
        out_specs=pl.BlockSpec((q, KS * CHUNK, LANES), lambda g: (0, g, 0)),
        out_shape=jax.ShapeDtypeStruct((q, fine_rows * KS, LANES), jnp.bfloat16),
        scratch_shapes=[
            pltpu.VMEM(((fine_rows + 2 * HB) * LANES, LANES), jnp.bfloat16),
            pltpu.VMEM((q * KS * CHUNK, LANES), jnp.float32),
        ],
        compiler_params=pltpu.CompilerParams(vmem_limit_bytes=40 * 1024 * 1024),
    )(a_tiles, near_p, code, group)


HALVES = 2
GROUP = 4
PIECE = 16
SPREAD = 40
AFTER = 2


def one_if(condition):
    return jnp.where(condition, 1.0, 0.0)


def halves_kernel(
    pair_count, devices,
    a_hbm, p_hbm, cols_hbm, group_hbm, slots_hbm, aggregate_hbm, out_ref,
    a_ref, p_ref, cols_ref, groups_ref, slots_ref, agg_ref,
    tiles, diag, turned, code, pick, stage, products, sums, term_ref, got, goals, sent_sums, got_sums, own_sums, final, parts,
    a_came, p_came, small_came, halo_sent, halo_came, sent, came, goal_sent, goal_came, cross_sent, cross_came, final_sent, final_came, self_came,
):
    q = BLK // 2
    me = lax.axis_index("rows") * pair_count + lax.axis_index("pair")
    team = devices // HALVES
    half, mine = lax.div(me, team), lax.rem(me, team)
    turn = half * (team // 2)
    mirror = me ^ (devices - team // 2)
    my_slice = mine ^ turn
    fine_rows = turned.shape[0] // BLK
    wide = term_ref.shape[2]
    chunks = fine_rows // PIECE
    coarse_rows = parts.shape[0] // KC
    members = team * KC
    ahead, behind = lax.rem(me + 1, devices), lax.rem(me + devices - 1, devices)

    def at(device):
        return (lax.div(device, pair_count), lax.rem(device, pair_count))

    def copy(src, dst, send_sem, recv_sem, device):
        return pltpu.make_async_remote_copy(
            src_ref=src,
            dst_ref=dst,
            send_sem=send_sem,
            recv_sem=recv_sem,
            device_id=at(device),
            device_id_type=pl.DeviceIdType.MESH,
        )

    def whole_rows(index, count):
        return pl.ds(pl.multiple_of(index * count, count), count)

    def a_copy(order):
        rows = whole_rows(lax.rem(order + 1, chunks), PIECE)
        return pltpu.make_async_copy(a_hbm.at[rows], a_ref.at[rows], a_came.at[order])

    def p_copy(t):
        rows = whole_rows(t, 8 * q)
        return pltpu.make_async_copy(p_hbm.at[rows], p_ref.at[rows], p_came.at[t])

    small = [
        pltpu.make_async_copy(src, dst, small_came.at[i])
        for i, (src, dst) in enumerate(
            [(cols_hbm, cols_ref), (group_hbm, groups_ref), (slots_hbm, slots_ref), (aggregate_hbm, agg_ref)]
        )
    ]
    edge = HB * LANES
    inner = fine_rows * LANES
    halo_up = copy(diag.at[pl.ds(inner, edge)], diag.at[pl.ds(0, edge)], halo_sent.at[0], halo_came.at[0], ahead)
    halo_down = copy(diag.at[pl.ds(edge, edge)], diag.at[pl.ds(inner + edge, edge)], halo_sent.at[1], halo_came.at[1], behind)

    def member(k):
        return mine ^ k

    def goal_copy(k, slot):
        return copy(goals.at[mine], goals.at[slot], goal_sent.at[k], goal_came.at[slot], half * team + member(k))

    def term_part(k, slot, chunk):
        rows = whole_rows(chunk, KS * PIECE)
        return copy(
            term_ref.at[member(k) ^ turn, rows], got.at[slot, rows], sent.at[k, chunk], came.at[slot, chunk], half * team + member(k)
        )

    def cross_copy(r):
        return copy(sent_sums.at[r], got_sums.at[r], cross_sent.at[r], cross_came.at[r], mirror)

    def final_copy(k, slot, r):
        lanes = pl.ds(pl.multiple_of((slot ^ turn) * wide, wide), wide)
        return copy(
            final.at[r, whole_rows(member(k), KC)],
            parts.at[whole_rows(r, KC), lanes],
            final_sent.at[k, r],
            final_came.at[slot, r],
            half * team + member(k),
        )

    barrier = pltpu.get_barrier_semaphore()
    for device in [half * team + member(k) for k in range(1, team)] + [mirror, ahead, behind]:
        pl.semaphore_signal(barrier, inc=1, device_id=at(device), device_id_type=pl.DeviceIdType.MESH)
    for t in range(fine_rows // 8):
        p_copy(t).start()
    for transfer in small:
        transfer.start()
    for order in range(chunks):
        a_copy(order).start()

    r128, k128 = iota((LANES, LANES), 0), iota((LANES, LANES), 1)
    want = one_if((r128 // BLK == k128 // BLK) & (r128 % BLK == 2 * (k128 % q) + (k128 // q) % 2)).astype(jnp.bfloat16)
    perm = one_if((r128 // BLK == k128 // BLK) & (k128 % BLK == 2 * (r128 % q) + (r128 % BLK) // q)).astype(jnp.bfloat16)
    low = iota((q, LANES), 1) < BLK

    for transfer in small:
        transfer.wait()
    offset = cols_ref[...] - (me * fine_rows + iota((KA, fine_rows), 1)) + HB
    for i in range(fine_rows):
        code[i] = jnp.broadcast_to(offset[:, i : i + 1], (KA, LANES))
    repeat = one_if(iota((KA, q * KA), 1) % KA == iota((KA, q * KA), 0)).astype(jnp.bfloat16)
    pick[...] = lax.dot_general(
        groups_ref[...].astype(jnp.float32).astype(jnp.bfloat16),
        repeat,
        (((0,), (0,)), ((), ())),
        preferred_element_type=jnp.float32,
    )
    count = fine_rows * KS
    term, fine = iota((fine_rows, count), 1), iota((fine_rows, count), 0)
    goal_rows = []
    for s in range(KS):
        place = one_if(term == (fine // PIECE) * (KS * PIECE) + s * PIECE + fine % PIECE).astype(jnp.bfloat16)
        values = jnp.concatenate(
            [
                jnp.broadcast_to(agg_ref[...], (KA, fine_rows)),
                jnp.broadcast_to(slots_ref[s : s + 1, :], (KA, fine_rows)),
            ],
            axis=0,
        )
        values = values.astype(jnp.float32).astype(jnp.bfloat16)
        goal_rows.append(jnp.dot(values, place, preferred_element_type=jnp.float32))
    goals[mine] = goal_rows[0] + goal_rows[1]

    def prepare(t8, _):
        p_copy(t8).wait()
        tiles[...] = p_ref[whole_rows(t8, 8 * q), :].astype(jnp.float32)
        for t2 in range(4):
            flats = []
            for u in range(2):
                flat = tiles[pl.ds(2 * t2 + u, q, stride=8), :]
                t = t8 * 8 + 2 * t2 + u
                diag[whole_rows(t + HB, LANES), :] = put_diagonal(flat, want, low)
                flats.append((flat, pltpu.roll(flat, BLK, 1)))
            both = jnp.concatenate(
                [jnp.where(low, flats[0][0], flats[1][1]), jnp.where(low, flats[0][1], flats[1][0])], axis=0
            ).astype(jnp.bfloat16)
            turned[whole_rows(t8 * 4 + t2, LANES), :] = lax.dot_general(
                perm, both, (((1,), (1,)), ((), ())), preferred_element_type=jnp.float32
            ).astype(jnp.bfloat16)
        return 0

    lax.fori_loop(0, fine_rows // 8, prepare, 0)
    pl.semaphore_wait(barrier, team + 2)
    halo_up.start()
    halo_down.start()
    for k in range(1, team):
        goal_copy(k, mine).start()

    even = one_if(iota((q, q * KA), 1) // KA == iota((q, q * KA), 0)).astype(jnp.bfloat16)

    def full_mask(condition):
        one = one_if(condition)
        pair = jnp.concatenate([one, one], axis=0).astype(jnp.bfloat16)
        return jnp.broadcast_to(pair[None], (q // 2,) + pair.shape).reshape(q * KA, LANES)

    def full(condition):
        return jnp.broadcast_to(condition[None], (q, KA, LANES)).reshape(q * KA, LANES)

    def multiply(first):
        for u2 in range(GROUP // 2):
            row = first + 2 * u2
            near = [diag[whole_rows(row + j, LANES), :] for j in range(NEAR + 1)]
            zero = jnp.zeros_like(near[0])
            middle = jnp.concatenate(
                [jnp.concatenate(near[1:3], axis=1), jnp.concatenate(near[3:5], axis=1)], axis=0
            )
            outer = jnp.concatenate(
                [jnp.concatenate([near[0], zero], axis=1), jnp.concatenate([zero, near[5]], axis=1)], axis=0
            )
            rows = [a_ref[row], a_ref[row + 1]]
            edges = jnp.dot(jnp.concatenate(rows, axis=1), outer, preferred_element_type=jnp.float32)
            for u in range(2):
                which = code[row + u] + u
                upper = rows[u] * full_mask((which == 3) | (which == 4))
                inside = jnp.dot(
                    jnp.concatenate([rows[u] - upper, upper], axis=1), middle, preferred_element_type=jnp.float32
                )
                result = jnp.where(
                    full(which == NEAR * u),
                    edges[:, u * LANES : (u + 1) * LANES],
                    jnp.where(full((which == 1) | (which == 3)), inside[:, :LANES], inside[:, LANES:]),
                )
                at_row = (2 * u2 + u) * q * KA
                products[at_row : at_row + q * KA, :] = result.astype(jnp.bfloat16)

    def add_groups(first):
        for u in range(GROUP):
            one = even * jnp.broadcast_to(pick[pl.ds(first + u, 1), :], even.shape).astype(jnp.bfloat16)
            both = jnp.dot(
                jnp.concatenate([even - one, one], axis=0),
                products[u * q * KA : (u + 1) * q * KA, :],
                preferred_element_type=jnp.float32,
            )
            s0, s1 = both[:q], both[q:]
            t0, t1 = pltpu.roll(s0, BLK, 1), pltpu.roll(s1, BLK, 1)
            sums[u * BLK : (u + 1) * BLK, :] = jnp.concatenate(
                [jnp.where(low, s0, t1), jnp.where(low, t0, s1)], axis=0
            ).astype(jnp.bfloat16)

    def project(first):
        for u in range(GROUP):
            row = first + u
            both = jnp.dot(
                turned[whole_rows(row, BLK), :],
                sums[u * BLK : (u + 1) * BLK, :],
                preferred_element_type=jnp.float32,
            )
            even_rows, odd_rows = both[:q], both[q:]
            t0, t1 = pltpu.roll(even_rows, BLK, 1), pltpu.roll(odd_rows, BLK, 1)
            place = lax.rem(row, PIECE)
            stage[pl.ds(place, q, stride=SPREAD), :] = jnp.where(low, even_rows, t1)
            stage[pl.ds(PIECE + place, q, stride=SPREAD), :] = jnp.where(low, t0, odd_rows)

    groups = fine_rows // GROUP
    per = PIECE // GROUP

    def first_row(index):
        return lax.rem(index + per, groups) * GROUP

    def step(t, _):
        @pl.when((lax.rem(t, per) == 0) & (t < groups))
        def _():
            a_copy(lax.div(t, per)).wait()

        @pl.when(t == (chunks - 2) * per)
        def _():
            halo_up.wait_recv()
            halo_down.wait_recv()

        project(first_row(jnp.maximum(t - 2, 0)))
        add_groups(first_row(jnp.clip(t - 1, 0, groups - 1)))
        multiply(first_row(jnp.minimum(t, groups - 1)))

        @pl.when((t >= AFTER) & (lax.rem(t - AFTER, per) == per - 1))
        def _():
            chunk = lax.rem(lax.div(t - AFTER, per) + 1, chunks)
            rows = whole_rows(chunk, KS * PIECE)
            for pair in range(q):
                lanes = slice(pair % 2 * LANES, pair % 2 * LANES + LANES)
                term_ref[pair // 2, rows, lanes] = stage[pair * SPREAD : pair * SPREAD + KS * PIECE, :].astype(jnp.bfloat16)
            for k in range(1, team):
                term_part(k, mine, chunk).start()

        return 0

    lax.fori_loop(0, groups + AFTER, step, 0)
    keep = pltpu.make_async_copy(term_ref.at[my_slice], got.at[mine], self_came)
    keep.start()
    for k in range(1, team):
        goal_copy(k, member(k)).wait_recv()
        for chunk in range(chunks):
            term_part(k, member(k), chunk).wait_recv()
    keep.wait()

    coarse = jnp.concatenate([goals[j, :KA] for j in range(team)], axis=1)
    slot = jnp.concatenate([goals[j, KA:] for j in range(team)], axis=1)
    slot = jnp.concatenate([slot, slot], axis=0)
    slot_hot = one_if(slot == iota(slot.shape, 0).astype(jnp.float32)).astype(jnp.bfloat16)

    def half_sums(which, r):
        pieces = []
        for j in range(team):
            row = ((which * team + j) * coarse_rows + r).astype(jnp.float32)
            one = one_if(coarse == row)
            pieces.append(slot_hot * jnp.concatenate([one, one], axis=0).astype(jnp.bfloat16))
        return jnp.dot(
            jnp.concatenate(pieces, axis=0), got[...].reshape(-1, wide), preferred_element_type=jnp.float32
        )

    def cross(r, _):
        sent_sums[r] = half_sums(1 - half, r).astype(jnp.bfloat16)
        cross_copy(r).start()
        return 0

    lax.fori_loop(0, coarse_rows, cross, 0)

    def keep_own(r, _):
        own_sums[r] = half_sums(half, r)
        return 0

    lax.fori_loop(0, coarse_rows, keep_own, 0)

    def finish(r, _):
        cross_copy(r).wait_recv()
        final[r] = (own_sums[r] + got_sums[r].astype(jnp.float32)).astype(jnp.bfloat16)
        for k in range(1, team):
            final_copy(k, mine, r).start()
        lanes = pl.ds(pl.multiple_of(my_slice * wide, wide), wide)
        parts[whole_rows(r, KC), lanes] = final[r, whole_rows(mine, KC), :]
        return 0

    lax.fori_loop(0, coarse_rows, finish, 0)

    def gather(r, _):
        for k in range(1, team):
            final_copy(k, member(k), r).wait_recv()
        out_ref[whole_rows(r, KC), :] = parts[whole_rows(r, KC), :].astype(jnp.float32)
        return 0

    lax.fori_loop(0, coarse_rows, gather, 0)
    halo_up.wait_send()
    halo_down.wait_send()
    for k in range(1, team):
        goal_copy(k, mine).wait_send()
        for chunk in range(chunks):
            term_part(k, mine, chunk).wait_send()
        for r in range(coarse_rows):
            final_copy(k, mine, r).wait_send()
    for r in range(coarse_rows):
        cross_copy(r).wait_send()


def by_halves(a_tiles, p_tiles, a_cols, tile_group, coarse_slots, aggregate):
    fine_rows, _, width = a_tiles.shape
    q = BLK // 2
    devices, pair_count = lax.axis_size(BOTH), lax.axis_size("pair")
    team = devices // HALVES
    wide = width // team
    count = fine_rows * KS
    coarse_rows = fine_rows // RATIO
    chunks = fine_rows // PIECE
    members = team * KC
    a = a_tiles.reshape(fine_rows, KA, q, LANES).transpose(0, 2, 1, 3).reshape(fine_rows, q * KA, LANES)
    p = p_tiles.reshape(fine_rows // 8, 8, q, LANES).transpose(0, 2, 1, 3).reshape(fine_rows * q, LANES)
    bf16, f32, i32 = jnp.bfloat16, jnp.float32, jnp.int32
    dma = pltpu.SemaphoreType.DMA
    return pl.pallas_call(
        functools.partial(halves_kernel, pair_count, devices),
        in_specs=[pl.BlockSpec(memory_space=pltpu.HBM)] * 6,
        out_specs=pl.BlockSpec(memory_space=pltpu.VMEM),
        out_shape=jax.ShapeDtypeStruct((coarse_rows * KC, width), f32),
        scratch_shapes=[
            pltpu.VMEM(a.shape, bf16),
            pltpu.VMEM(p.shape, bf16),
            pltpu.VMEM((KA, fine_rows), i32),
            pltpu.VMEM((KA, fine_rows), i32),
            pltpu.VMEM((KS, fine_rows), i32),
            pltpu.VMEM((1, fine_rows), i32),
            pltpu.VMEM((8 * q, LANES), f32),
            pltpu.VMEM(((fine_rows + 2 * HB) * LANES, LANES), bf16),
            pltpu.VMEM((fine_rows * BLK, BLK), bf16),
            pltpu.VMEM((fine_rows, KA, LANES), i32),
            pltpu.VMEM((fine_rows, q * KA), f32),
            pltpu.VMEM((q * SPREAD, LANES), f32),
            pltpu.VMEM((GROUP * q * KA, LANES), bf16),
            pltpu.VMEM((GROUP * BLK, LANES), bf16),
            pltpu.VMEM((team, count, wide), bf16),
            pltpu.VMEM((team, count, wide), bf16),
            pltpu.VMEM((team, 2 * KA, count), f32),
            pltpu.VMEM((coarse_rows, members, wide), bf16),
            pltpu.VMEM((coarse_rows, members, wide), bf16),
            pltpu.VMEM((coarse_rows, members, wide), f32),
            pltpu.VMEM((coarse_rows, members, wide), bf16),
            pltpu.VMEM((coarse_rows * KC, width), bf16),
            dma((chunks,)),
            dma((fine_rows // 8,)),
            dma((4,)),
            dma((2,)),
            dma((2,)),
            dma((team, chunks)),
            dma((team, chunks)),
            dma((team,)),
            dma((team,)),
            dma((coarse_rows,)),
            dma((coarse_rows,)),
            dma((team, coarse_rows)),
            dma((team, coarse_rows)),
            dma,
        ],
        compiler_params=pltpu.CompilerParams(
            collective_id=0, has_side_effects=True, vmem_limit_bytes=60 * 1024 * 1024
        ),
    )(a, p, a_cols.T, tile_group.T, coarse_slots.T, aggregate.reshape(1, fine_rows))


def routed(terms, coarse_slots, aggregate):
    fine_rows = aggregate.shape[0]
    q = BLK // 2
    width = BLK * BLK
    rows_count, pair_count = lax.axis_size("rows"), lax.axis_size("pair")
    flat = terms.reshape(q, fine_rows // CHUNK, KS, CHUNK, 2, BLK)
    flat = flat.transpose(1, 3, 2, 4, 0, 5).reshape(fine_rows, KS, width)
    group_size = fine_rows // RATIO * pair_count
    capacity = 2 * fine_rows // rows_count
    dest_group = aggregate // group_size
    local_rows = aggregate - dest_group * group_size
    targets = local_rows[:, None] * KC + coarse_slots
    order = jnp.arange(fine_rows)
    same = (dest_group[:, None] == dest_group[None, :]) & (order[None, :] < order[:, None])
    position = dest_group * capacity + jnp.sum(same.astype(jnp.int32), axis=1)

    def exchange(values):
        buffer = jnp.zeros((rows_count * capacity,) + values.shape[1:], values.dtype)
        buffer = buffer.at[position].set(values)
        return lax.all_to_all(buffer, "rows", split_axis=0, concat_axis=0, tiled=True)

    got = exchange(flat).reshape(-1, width).astype(jnp.float32)
    panel = jax.ops.segment_sum(
        got, exchange(targets).reshape(-1), num_segments=group_size * KC
    )
    panel = panel.reshape(group_size, KC, width)
    return lax.psum_scatter(panel, "pair", scatter_dimension=0, tiled=True)


def body(a_tiles, p_tiles, a_cols, tile_group, coarse_slots, aggregate):
    fine_rows, width = p_tiles.shape
    devices = lax.axis_size(BOTH)
    if devices * LANES != width:
        return routed(local_terms(a_tiles, p_tiles, a_cols, tile_group), coarse_slots, aggregate)
    result = by_halves(a_tiles, p_tiles, a_cols, tile_group, coarse_slots, aggregate)
    return result.reshape(fine_rows // RATIO, KC, width)


def solution(mesh):
    return jax.shard_map(
        body,
        mesh=mesh,
        in_specs=(
            P(BOTH, None, None),
            P(BOTH, None),
            P(BOTH, None),
            P(BOTH, None),
            P(BOTH, None),
            P(BOTH),
        ),
        out_specs=P(BOTH, None, None),
        check_vma=False,
    )
```

```python
import functools

import jax
import jax.numpy as jnp
from jax import lax
from jax.experimental import pallas as pl
from jax.experimental.pallas import tpu as pltpu
from jax.sharding import PartitionSpec as P

BLK = 64
KA = 8
KS = 2
KC = 16
HB = 2
RATIO = 16
LANES = 128
NEAR = 2 * HB + 1
CHUNK = 8
BOTH = ("rows", "pair")


def extended(array, width):
    devices, length = lax.axis_size(BOTH), array.shape[0]
    up = [(i, i + 1) for i in range(devices - 1)]
    down = [(j, i) for i, j in up]
    before = lax.ppermute(array[length - width :], BOTH, up)
    after = lax.ppermute(array[:width], BOTH, down)
    return jnp.concatenate([before, array, after], axis=0)


def iota(shape, dim):
    return lax.broadcasted_iota(jnp.int32, shape, dim)


def put_diagonal(flat, want, low):
    flat = flat.astype(jnp.float32)
    turned = pltpu.roll(flat, BLK, 1)
    zero = jnp.zeros_like(flat)
    parts = jnp.concatenate(
        [
            jnp.where(low, flat, zero),
            jnp.where(low, turned, zero),
            jnp.where(low, zero, turned),
            jnp.where(low, zero, flat),
        ],
        axis=0,
    ).astype(jnp.bfloat16)
    return jnp.dot(want, parts, preferred_element_type=jnp.float32).astype(jnp.bfloat16)


def constants():
    q = BLK // 2
    r, k = iota((LANES, LANES), 0), iota((LANES, LANES), 1)
    want = jnp.where(
        (r // BLK == k // BLK) & (r % BLK == 2 * (k % q) + (k // q) % 2), 1.0, 0.0
    ).astype(jnp.bfloat16)
    eye = jnp.where(r == k, 1.0, 0.0).astype(jnp.bfloat16)
    spread = jnp.where(
        iota((q, q * KA), 0) == iota((q, q * KA), 1) // KA, 1.0, 0.0
    ).astype(jnp.bfloat16)
    low = iota((q, LANES), 1) < BLK
    return want, eye, spread, low


def row_terms(read, code, group, near, own, eye, spread, low):
    q = BLK // 2
    tiles = jnp.concatenate([read(c).astype(jnp.float32) for c in range(q)], axis=0)
    tiles = tiles.astype(jnp.bfloat16)

    def picked(j):
        one = jnp.where(code == j, 1.0, 0.0)
        pair = jnp.concatenate([one, one], axis=0).astype(jnp.bfloat16)
        return jnp.broadcast_to(pair[None], (q // 2,) + pair.shape).reshape(tiles.shape)

    left = jnp.concatenate([tiles * picked(j) for j in range(NEAR)], axis=1)
    products = jnp.dot(left, near, preferred_element_type=jnp.float32).astype(jnp.bfloat16)
    turned = lax.dot_general(
        eye, own, (((1,), (1,)), ((), ())), preferred_element_type=jnp.float32
    ).astype(jnp.bfloat16)
    wide = jnp.dot(turned, spread, preferred_element_type=jnp.float32).astype(jnp.bfloat16)
    rows = jnp.concatenate(
        [wide * jnp.where(group == s, 1.0, 0.0).astype(jnp.bfloat16) for s in range(KS)], axis=0
    )
    full = jnp.dot(rows, products, preferred_element_type=jnp.float32)
    terms = []
    for s in range(KS):
        part = full[s * LANES : (s + 1) * LANES]
        terms.append(
            jnp.where(low, part[:q], part[3 * q :])
            + pltpu.roll(jnp.where(low, part[q : 2 * q], part[2 * q : 3 * q]), BLK, 1)
        )
    return terms


def terms_kernel(a_ref, p_ref, code_ref, group_ref, out_ref, diag, stage):
    step = pl.program_id(0)
    q = BLK // 2
    want, eye, spread, low = constants()

    @pl.when(step == 0)
    def _():
        def one(t, _):
            diag[pl.ds(pl.multiple_of(t * LANES, LANES), LANES), :] = put_diagonal(p_ref[t], want, low)
            return 0

        lax.fori_loop(0, p_ref.shape[0], one, 0, unroll=4)

    for i in range(CHUNK):
        row = step * CHUNK + i
        terms = row_terms(
            lambda c: a_ref[i, :, c * LANES : (c + 1) * LANES],
            code_ref[i],
            group_ref[i],
            diag[pl.ds(pl.multiple_of(row * LANES, LANES), NEAR * LANES), :],
            p_ref[row + HB],
            eye,
            spread,
            low,
        )
        for s in range(KS):
            stage[pl.ds(s * CHUNK + i, q, stride=KS * CHUNK), :] = terms[s]
    out_ref[...] = stage[...].astype(jnp.bfloat16).reshape(out_ref.shape)


def row_codes(a_cols, tile_group):
    fine_rows = a_cols.shape[0]
    q = BLK // 2
    own = lax.axis_index(BOTH) * fine_rows + jnp.arange(fine_rows, dtype=jnp.int32)
    offset = a_cols - own[:, None] + HB
    code = jnp.broadcast_to(offset[:, :, None], (fine_rows, KA, LANES))
    group = jnp.tile(tile_group, (1, q)).reshape(fine_rows, 1, q * KA)
    return code, group


def local_terms(a_tiles, p_tiles, a_cols, tile_group):
    fine_rows = a_tiles.shape[0]
    q = BLK // 2
    near_p = extended(p_tiles, HB).reshape(fine_rows + 2 * HB, q, LANES)
    code, group = row_codes(a_cols, tile_group)
    steps = fine_rows // CHUNK
    return pl.pallas_call(
        terms_kernel,
        grid=(steps,),
        in_specs=[
            pl.BlockSpec((CHUNK, KA, BLK * BLK), lambda g: (g, 0, 0)),
            pl.BlockSpec((fine_rows + 2 * HB, q, LANES), lambda g: (0, 0, 0)),
            pl.BlockSpec((CHUNK, KA, LANES), lambda g: (g, 0, 0)),
            pl.BlockSpec((CHUNK, 1, q * KA), lambda g: (g, 0, 0)),
        ],
        out_specs=pl.BlockSpec((q, KS * CHUNK, LANES), lambda g: (0, g, 0)),
        out_shape=jax.ShapeDtypeStruct((q, fine_rows * KS, LANES), jnp.bfloat16),
        scratch_shapes=[
            pltpu.VMEM(((fine_rows + 2 * HB) * LANES, LANES), jnp.bfloat16),
            pltpu.VMEM((q * KS * CHUNK, LANES), jnp.float32),
        ],
        compiler_params=pltpu.CompilerParams(vmem_limit_bytes=40 * 1024 * 1024),
    )(a_tiles, near_p, code, group)


HALVES = 2
GROUP = 4
PIECE = 16
SPREAD = 40
AFTER = 2


def one_if(condition):
    return jnp.where(condition, 1.0, 0.0)


def halves_kernel(
    pair_count, devices,
    a_hbm, p_hbm, cols_hbm, group_hbm, slots_hbm, aggregate_hbm, out_ref,
    a_ref, p_ref, cols_ref, groups_ref, slots_ref, agg_ref,
    tiles, diag, turned, code, pick, stage, products, sums, term_ref, got, goals, sent_sums, got_sums, own_sums, final, parts,
    a_came, p_came, small_came, halo_sent, halo_came, sent, came, rest_sent, rest_came, goal_sent, goal_came, cross_sent, cross_came, final_sent, final_came, self_came,
):
    q = BLK // 2
    me = lax.axis_index("rows") * pair_count + lax.axis_index("pair")
    team = devices // HALVES
    half, mine = lax.div(me, team), lax.rem(me, team)
    turn = half * (team // 2)
    mirror = me ^ (devices - team // 2)
    my_slice = mine ^ turn
    fine_rows = turned.shape[0] // BLK
    strips = got.shape[0]
    chunks = fine_rows // PIECE
    coarse_rows = parts.shape[0] // KC
    members = team * KC
    ahead, behind = lax.rem(me + 1, devices), lax.rem(me + devices - 1, devices)

    def at(device):
        return (lax.div(device, pair_count), lax.rem(device, pair_count))

    def copy(src, dst, send_sem, recv_sem, device):
        return pltpu.make_async_remote_copy(
            src_ref=src,
            dst_ref=dst,
            send_sem=send_sem,
            recv_sem=recv_sem,
            device_id=at(device),
            device_id_type=pl.DeviceIdType.MESH,
        )

    def whole_rows(index, count):
        return pl.ds(pl.multiple_of(index * count, count), count)

    def a_copy(order):
        rows = whole_rows(lax.rem(order + 1, chunks), PIECE)
        return pltpu.make_async_copy(a_hbm.at[rows], a_ref.at[rows], a_came.at[order])

    def p_copy(t):
        rows = whole_rows(t, 8 * q)
        return pltpu.make_async_copy(p_hbm.at[rows], p_ref.at[rows], p_came.at[t])

    small = [
        pltpu.make_async_copy(src, dst, small_came.at[i])
        for i, (src, dst) in enumerate(
            [(cols_hbm, cols_ref), (group_hbm, groups_ref), (slots_hbm, slots_ref), (aggregate_hbm, agg_ref)]
        )
    ]
    edge = HB * LANES
    inner = fine_rows * LANES
    halo_up = copy(diag.at[pl.ds(inner, edge)], diag.at[pl.ds(0, edge)], halo_sent.at[0], halo_came.at[0], ahead)
    halo_down = copy(diag.at[pl.ds(edge, edge)], diag.at[pl.ds(inner + edge, edge)], halo_sent.at[1], halo_came.at[1], behind)

    def member(k):
        return mine ^ k

    def goal_copy(k, slot):
        return copy(goals.at[mine], goals.at[slot], goal_sent.at[k], goal_came.at[slot], half * team + member(k))

    def strip(slot, g):
        return (slot ^ turn) * strips + g

    def term_part(k, slot, chunk):
        rows = whole_rows(chunk, KS * PIECE)
        return copy(
            term_ref.at[strip(member(k), 0), rows],
            got.at[0, slot, rows],
            sent.at[k, chunk],
            came.at[slot, chunk],
            half * team + member(k),
        )

    def term_rest(k, slot, g):
        return copy(
            term_ref.at[strip(member(k), g)],
            got.at[g, slot],
            rest_sent.at[k, g],
            rest_came.at[slot, g],
            half * team + member(k),
        )

    def cross_copy(g, r):
        return copy(sent_sums.at[g, r], got_sums.at[g, r], cross_sent.at[g, r], cross_came.at[g, r], mirror)

    def final_copy(k, slot, g, r):
        return copy(
            final.at[g, r, whole_rows(member(k), KC)],
            parts.at[whole_rows(r, KC), whole_rows(strip(slot, g), LANES)],
            final_sent.at[k, g, r],
            final_came.at[slot, g, r],
            half * team + member(k),
        )

    barrier = pltpu.get_barrier_semaphore()
    for device in [half * team + member(k) for k in range(1, team)] + [mirror, ahead, behind]:
        pl.semaphore_signal(barrier, inc=1, device_id=at(device), device_id_type=pl.DeviceIdType.MESH)
    for t in range(fine_rows // 8):
        p_copy(t).start()
    for transfer in small:
        transfer.start()
    for order in range(chunks):
        a_copy(order).start()

    r128, k128 = iota((LANES, LANES), 0), iota((LANES, LANES), 1)
    want = one_if((r128 // BLK == k128 // BLK) & (r128 % BLK == 2 * (k128 % q) + (k128 // q) % 2)).astype(jnp.bfloat16)
    perm = one_if((r128 // BLK == k128 // BLK) & (k128 % BLK == 2 * (r128 % q) + (r128 % BLK) // q)).astype(jnp.bfloat16)
    low = iota((q, LANES), 1) < BLK

    for transfer in small:
        transfer.wait()
    offset = cols_ref[...] - (me * fine_rows + iota((KA, fine_rows), 1)) + HB
    for i in range(fine_rows):
        code[i] = jnp.broadcast_to(offset[:, i : i + 1], (KA, LANES))
    repeat = one_if(iota((KA, q * KA), 1) % KA == iota((KA, q * KA), 0)).astype(jnp.bfloat16)
    pick[...] = lax.dot_general(
        groups_ref[...].astype(jnp.float32).astype(jnp.bfloat16),
        repeat,
        (((0,), (0,)), ((), ())),
        preferred_element_type=jnp.float32,
    )
    count = fine_rows * KS
    term, fine = iota((fine_rows, count), 1), iota((fine_rows, count), 0)
    goal_rows = []
    for s in range(KS):
        place = one_if(term == (fine // PIECE) * (KS * PIECE) + s * PIECE + fine % PIECE).astype(jnp.bfloat16)
        values = jnp.concatenate(
            [
                jnp.broadcast_to(agg_ref[...], (KA, fine_rows)),
                jnp.broadcast_to(slots_ref[s : s + 1, :], (KA, fine_rows)),
            ],
            axis=0,
        )
        values = values.astype(jnp.float32).astype(jnp.bfloat16)
        goal_rows.append(jnp.dot(values, place, preferred_element_type=jnp.float32))
    goals[mine] = goal_rows[0] + goal_rows[1]

    def prepare(t16, _):
        p_copy(2 * t16).wait()
        p_copy(2 * t16 + 1).wait()
        tiles[...] = p_ref[whole_rows(t16, 16 * q), :].astype(jnp.float32)
        for t2 in range(8):
            flats = []
            for u in range(2):
                flat = tiles[pl.ds(t2 // 4 * 8 * q + t2 % 4 * 2 + u, q, stride=8), :]
                t = t16 * 16 + 2 * t2 + u
                diag[whole_rows(t + HB, LANES), :] = put_diagonal(flat, want, low)
                flats.append((flat, pltpu.roll(flat, BLK, 1)))
            both = jnp.concatenate(
                [jnp.where(low, flats[0][0], flats[1][1]), jnp.where(low, flats[0][1], flats[1][0])], axis=0
            ).astype(jnp.bfloat16)
            turned[whole_rows(t16 * 8 + t2, LANES), :] = lax.dot_general(
                perm, both, (((1,), (1,)), ((), ())), preferred_element_type=jnp.float32
            ).astype(jnp.bfloat16)
        return 0

    lax.fori_loop(0, fine_rows // 16, prepare, 0)
    pl.semaphore_wait(barrier, team + 2)
    halo_up.start()
    halo_down.start()
    for k in range(1, team):
        goal_copy(k, mine).start()

    even = one_if(iota((q, q * KA), 1) // KA == iota((q, q * KA), 0)).astype(jnp.bfloat16)

    def full_mask(condition):
        one = one_if(condition)
        pair = jnp.concatenate([one, one], axis=0).astype(jnp.bfloat16)
        return jnp.broadcast_to(pair[None], (q // 2,) + pair.shape).reshape(q * KA, LANES)

    def full(condition):
        return jnp.broadcast_to(condition[None], (q, KA, LANES)).reshape(q * KA, LANES)

    def multiply(first):
        for u2 in range(GROUP // 2):
            row = first + 2 * u2
            near = [diag[whole_rows(row + j, LANES), :] for j in range(NEAR + 1)]
            zero = jnp.zeros_like(near[0])
            middle = jnp.concatenate(
                [jnp.concatenate(near[1:3], axis=1), jnp.concatenate(near[3:5], axis=1)], axis=0
            )
            outer = jnp.concatenate(
                [jnp.concatenate([near[0], zero], axis=1), jnp.concatenate([zero, near[5]], axis=1)], axis=0
            )
            rows = [a_ref[row], a_ref[row + 1]]
            edges = jnp.dot(jnp.concatenate(rows, axis=1), outer, preferred_element_type=jnp.float32)
            for u in range(2):
                which = code[row + u] + u
                upper = rows[u] * full_mask((which == 3) | (which == 4))
                inside = jnp.dot(
                    jnp.concatenate([rows[u] - upper, upper], axis=1), middle, preferred_element_type=jnp.float32
                )
                result = jnp.where(
                    full(which == NEAR * u),
                    edges[:, u * LANES : (u + 1) * LANES],
                    jnp.where(full((which == 1) | (which == 3)), inside[:, :LANES], inside[:, LANES:]),
                )
                at_row = (2 * u2 + u) * q * KA
                products[at_row : at_row + q * KA, :] = result.astype(jnp.bfloat16)

    def add_groups(first):
        for u in range(GROUP):
            one = even * jnp.broadcast_to(pick[pl.ds(first + u, 1), :], even.shape).astype(jnp.bfloat16)
            both = jnp.dot(
                jnp.concatenate([even - one, one], axis=0),
                products[u * q * KA : (u + 1) * q * KA, :],
                preferred_element_type=jnp.float32,
            )
            s0, s1 = both[:q], both[q:]
            t0, t1 = pltpu.roll(s0, BLK, 1), pltpu.roll(s1, BLK, 1)
            sums[u * BLK : (u + 1) * BLK, :] = jnp.concatenate(
                [jnp.where(low, s0, t1), jnp.where(low, t0, s1)], axis=0
            ).astype(jnp.bfloat16)

    def project(first):
        for u in range(GROUP):
            row = first + u
            both = jnp.dot(
                turned[whole_rows(row, BLK), :],
                sums[u * BLK : (u + 1) * BLK, :],
                preferred_element_type=jnp.float32,
            )
            even_rows, odd_rows = both[:q], both[q:]
            t0, t1 = pltpu.roll(even_rows, BLK, 1), pltpu.roll(odd_rows, BLK, 1)
            place = lax.rem(row, PIECE)
            stage[pl.ds(place, q, stride=SPREAD), :] = jnp.where(low, even_rows, t1)
            stage[pl.ds(PIECE + place, q, stride=SPREAD), :] = jnp.where(low, t0, odd_rows)

    groups = fine_rows // GROUP
    per = PIECE // GROUP

    def first_row(index):
        return lax.rem(index + per, groups) * GROUP

    def step(t, _):
        @pl.when((lax.rem(t, per) == 0) & (t < groups))
        def _():
            a_copy(lax.div(t, per)).wait()

        @pl.when(t == (chunks - 2) * per)
        def _():
            halo_up.wait_recv()
            halo_down.wait_recv()

        project(first_row(jnp.maximum(t - 2, 0)))
        add_groups(first_row(jnp.clip(t - 1, 0, groups - 1)))
        multiply(first_row(jnp.minimum(t, groups - 1)))

        @pl.when((t >= AFTER) & (lax.rem(t - AFTER, per) == per - 1))
        def _():
            chunk = lax.rem(lax.div(t - AFTER, per) + 1, chunks)
            rows = whole_rows(chunk, KS * PIECE)
            for pair in range(q):
                term_ref[pair, rows, :] = stage[pair * SPREAD : pair * SPREAD + KS * PIECE, :].astype(jnp.bfloat16)
            for k in range(1, team):
                term_part(k, mine, chunk).start()

        return 0

    lax.fori_loop(0, groups + AFTER, step, 0)
    for g in range(1, strips):
        for k in range(1, team):
            term_rest(k, mine, g).start()
    keep = [pltpu.make_async_copy(term_ref.at[strip(mine, g)], got.at[g, mine], self_came.at[g]) for g in range(strips)]
    for transfer in keep:
        transfer.start()
    for k in range(1, team):
        goal_copy(k, member(k)).wait_recv()
        for chunk in range(chunks):
            term_part(k, member(k), chunk).wait_recv()

    coarse = jnp.concatenate([goals[j, :KA] for j in range(team)], axis=1)
    slot = jnp.concatenate([goals[j, KA:] for j in range(team)], axis=1)
    slot = jnp.concatenate([slot, slot], axis=0)
    slot_hot = one_if(slot == iota(slot.shape, 0).astype(jnp.float32)).astype(jnp.bfloat16)

    def half_sums(which, g, r):
        pieces = []
        for j in range(team):
            row = ((which * team + j) * coarse_rows + r).astype(jnp.float32)
            one = one_if(coarse == row)
            pieces.append(slot_hot * jnp.concatenate([one, one], axis=0).astype(jnp.bfloat16))
        return jnp.dot(
            jnp.concatenate(pieces, axis=0), got[g].reshape(-1, LANES), preferred_element_type=jnp.float32
        )

    for g in range(strips):
        keep[g].wait()
        if g > 0:
            for k in range(1, team):
                term_rest(k, member(k), g).wait_recv()

        def cross(r, _):
            sent_sums[g, r] = half_sums(1 - half, g, r).astype(jnp.bfloat16)
            cross_copy(g, r).start()
            return 0

        def keep_own(r, _):
            own_sums[g, r] = half_sums(half, g, r)
            return 0

        lax.fori_loop(0, coarse_rows, cross, 0)
        lax.fori_loop(0, coarse_rows, keep_own, 0)

    for g in range(strips):

        def finish(r, _):
            cross_copy(g, r).wait_recv()
            final[g, r] = (own_sums[g, r] + got_sums[g, r].astype(jnp.float32)).astype(jnp.bfloat16)
            for k in range(1, team):
                final_copy(k, mine, g, r).start()
            parts[whole_rows(r, KC), whole_rows(strip(mine, g), LANES)] = final[g, r, whole_rows(mine, KC), :]
            return 0

        lax.fori_loop(0, coarse_rows, finish, 0)

    def gather(r, _):
        for g in range(strips):
            for k in range(1, team):
                final_copy(k, member(k), g, r).wait_recv()
        out_ref[whole_rows(r, KC), :] = parts[whole_rows(r, KC), :]
        return 0

    lax.fori_loop(0, coarse_rows, gather, 0)
    halo_up.wait_send()
    halo_down.wait_send()
    for k in range(1, team):
        goal_copy(k, mine).wait_send()
        for chunk in range(chunks):
            term_part(k, mine, chunk).wait_send()
        for g in range(1, strips):
            term_rest(k, mine, g).wait_send()

    def sent_all(r, _):
        for g in range(strips):
            cross_copy(g, r).wait_send()
            for k in range(1, team):
                final_copy(k, mine, g, r).wait_send()
        return 0

    lax.fori_loop(0, coarse_rows, sent_all, 0)


def by_halves(a_tiles, p_tiles, a_cols, tile_group, coarse_slots, aggregate):
    fine_rows, _, width = a_tiles.shape
    q = BLK // 2
    devices, pair_count = lax.axis_size(BOTH), lax.axis_size("pair")
    team = devices // HALVES
    strips = width // team // LANES
    count = fine_rows * KS
    coarse_rows = fine_rows // RATIO
    chunks = fine_rows // PIECE
    members = team * KC
    a = a_tiles.reshape(fine_rows, KA, q, LANES).transpose(0, 2, 1, 3).reshape(fine_rows, q * KA, LANES)
    p = p_tiles.reshape(fine_rows // 8, 8, q, LANES).transpose(0, 2, 1, 3).reshape(fine_rows * q, LANES)
    bf16, f32, i32 = jnp.bfloat16, jnp.float32, jnp.int32
    dma = pltpu.SemaphoreType.DMA
    return pl.pallas_call(
        functools.partial(halves_kernel, pair_count, devices),
        in_specs=[pl.BlockSpec(memory_space=pltpu.HBM)] * 6,
        out_specs=pl.BlockSpec(memory_space=pltpu.VMEM),
        out_shape=jax.ShapeDtypeStruct((coarse_rows * KC, width), bf16),
        scratch_shapes=[
            pltpu.VMEM(a.shape, bf16),
            pltpu.VMEM(p.shape, bf16),
            pltpu.VMEM((KA, fine_rows), i32),
            pltpu.VMEM((KA, fine_rows), i32),
            pltpu.VMEM((KS, fine_rows), i32),
            pltpu.VMEM((1, fine_rows), i32),
            pltpu.VMEM((16 * q, LANES), f32),
            pltpu.VMEM(((fine_rows + 2 * HB) * LANES, LANES), bf16),
            pltpu.VMEM((fine_rows * BLK, BLK), bf16),
            pltpu.VMEM((fine_rows, KA, LANES), i32),
            pltpu.VMEM((fine_rows, q * KA), f32),
            pltpu.VMEM((q * SPREAD, LANES), f32),
            pltpu.VMEM((GROUP * q * KA, LANES), bf16),
            pltpu.VMEM((GROUP * BLK, LANES), bf16),
            pltpu.VMEM((width // LANES, count, LANES), bf16),
            pltpu.VMEM((strips, team, count, LANES), bf16),
            pltpu.VMEM((team, 2 * KA, count), f32),
            pltpu.VMEM((strips, coarse_rows, members, LANES), bf16),
            pltpu.VMEM((strips, coarse_rows, members, LANES), bf16),
            pltpu.VMEM((strips, coarse_rows, members, LANES), f32),
            pltpu.VMEM((strips, coarse_rows, members, LANES), bf16),
            pltpu.VMEM((coarse_rows * KC, width), bf16),
            dma((chunks,)),
            dma((fine_rows // 8,)),
            dma((4,)),
            dma((2,)),
            dma((2,)),
            dma((team, chunks)),
            dma((team, chunks)),
            dma((team, strips)),
            dma((team, strips)),
            dma((team,)),
            dma((team,)),
            dma((strips, coarse_rows)),
            dma((strips, coarse_rows)),
            dma((team, strips, coarse_rows)),
            dma((team, strips, coarse_rows)),
            dma((strips,)),
        ],
        compiler_params=pltpu.CompilerParams(
            collective_id=0, has_side_effects=True, vmem_limit_bytes=60 * 1024 * 1024
        ),
    )(a, p, a_cols.T, tile_group.T, coarse_slots.T, aggregate.reshape(1, fine_rows))


def routed(terms, coarse_slots, aggregate):
    fine_rows = aggregate.shape[0]
    q = BLK // 2
    width = BLK * BLK
    rows_count, pair_count = lax.axis_size("rows"), lax.axis_size("pair")
    flat = terms.reshape(q, fine_rows // CHUNK, KS, CHUNK, 2, BLK)
    flat = flat.transpose(1, 3, 2, 4, 0, 5).reshape(fine_rows, KS, width)
    group_size = fine_rows // RATIO * pair_count
    capacity = 2 * fine_rows // rows_count
    dest_group = aggregate // group_size
    local_rows = aggregate - dest_group * group_size
    targets = local_rows[:, None] * KC + coarse_slots
    order = jnp.arange(fine_rows)
    same = (dest_group[:, None] == dest_group[None, :]) & (order[None, :] < order[:, None])
    position = dest_group * capacity + jnp.sum(same.astype(jnp.int32), axis=1)

    def exchange(values):
        buffer = jnp.zeros((rows_count * capacity,) + values.shape[1:], values.dtype)
        buffer = buffer.at[position].set(values)
        return lax.all_to_all(buffer, "rows", split_axis=0, concat_axis=0, tiled=True)

    got = exchange(flat).reshape(-1, width).astype(jnp.float32)
    panel = jax.ops.segment_sum(
        got, exchange(targets).reshape(-1), num_segments=group_size * KC
    )
    panel = panel.reshape(group_size, KC, width)
    return lax.psum_scatter(panel, "pair", scatter_dimension=0, tiled=True)


def body(a_tiles, p_tiles, a_cols, tile_group, coarse_slots, aggregate):
    fine_rows, width = p_tiles.shape
    devices = lax.axis_size(BOTH)
    if devices * LANES != width:
        return routed(local_terms(a_tiles, p_tiles, a_cols, tile_group), coarse_slots, aggregate)
    result = by_halves(a_tiles, p_tiles, a_cols, tile_group, coarse_slots, aggregate)
    return result.reshape(fine_rows // RATIO, KC, width).astype(jnp.float32)


def solution(mesh):
    return jax.shard_map(
        body,
        mesh=mesh,
        in_specs=(
            P(BOTH, None, None),
            P(BOTH, None),
            P(BOTH, None),
            P(BOTH, None),
            P(BOTH, None),
            P(BOTH),
        ),
        out_specs=P(BOTH, None, None),
        check_vma=False,
    )
```

```python
import functools

import jax
import jax.numpy as jnp
from jax import lax
from jax.experimental import pallas as pl
from jax.experimental.pallas import tpu as pltpu
from jax.sharding import PartitionSpec as P

BLK = 64
KA = 8
KS = 2
KC = 16
HB = 2
RATIO = 16
LANES = 128
NEAR = 2 * HB + 1
CHUNK = 8
BOTH = ("rows", "pair")


def extended(array, width):
    devices, length = lax.axis_size(BOTH), array.shape[0]
    up = [(i, i + 1) for i in range(devices - 1)]
    down = [(j, i) for i, j in up]
    before = lax.ppermute(array[length - width :], BOTH, up)
    after = lax.ppermute(array[:width], BOTH, down)
    return jnp.concatenate([before, array, after], axis=0)


def iota(shape, dim):
    return lax.broadcasted_iota(jnp.int32, shape, dim)


def put_diagonal(flat, want, low):
    flat = flat.astype(jnp.float32)
    turned = pltpu.roll(flat, BLK, 1)
    zero = jnp.zeros_like(flat)
    parts = jnp.concatenate(
        [
            jnp.where(low, flat, zero),
            jnp.where(low, turned, zero),
            jnp.where(low, zero, turned),
            jnp.where(low, zero, flat),
        ],
        axis=0,
    ).astype(jnp.bfloat16)
    return jnp.dot(want, parts, preferred_element_type=jnp.float32).astype(jnp.bfloat16)


def constants():
    q = BLK // 2
    r, k = iota((LANES, LANES), 0), iota((LANES, LANES), 1)
    want = jnp.where(
        (r // BLK == k // BLK) & (r % BLK == 2 * (k % q) + (k // q) % 2), 1.0, 0.0
    ).astype(jnp.bfloat16)
    eye = jnp.where(r == k, 1.0, 0.0).astype(jnp.bfloat16)
    spread = jnp.where(
        iota((q, q * KA), 0) == iota((q, q * KA), 1) // KA, 1.0, 0.0
    ).astype(jnp.bfloat16)
    low = iota((q, LANES), 1) < BLK
    return want, eye, spread, low


def row_terms(read, code, group, near, own, eye, spread, low):
    q = BLK // 2
    tiles = jnp.concatenate([read(c).astype(jnp.float32) for c in range(q)], axis=0)
    tiles = tiles.astype(jnp.bfloat16)

    def picked(j):
        one = jnp.where(code == j, 1.0, 0.0)
        pair = jnp.concatenate([one, one], axis=0).astype(jnp.bfloat16)
        return jnp.broadcast_to(pair[None], (q // 2,) + pair.shape).reshape(tiles.shape)

    left = jnp.concatenate([tiles * picked(j) for j in range(NEAR)], axis=1)
    products = jnp.dot(left, near, preferred_element_type=jnp.float32).astype(jnp.bfloat16)
    turned = lax.dot_general(
        eye, own, (((1,), (1,)), ((), ())), preferred_element_type=jnp.float32
    ).astype(jnp.bfloat16)
    wide = jnp.dot(turned, spread, preferred_element_type=jnp.float32).astype(jnp.bfloat16)
    rows = jnp.concatenate(
        [wide * jnp.where(group == s, 1.0, 0.0).astype(jnp.bfloat16) for s in range(KS)], axis=0
    )
    full = jnp.dot(rows, products, preferred_element_type=jnp.float32)
    terms = []
    for s in range(KS):
        part = full[s * LANES : (s + 1) * LANES]
        terms.append(
            jnp.where(low, part[:q], part[3 * q :])
            + pltpu.roll(jnp.where(low, part[q : 2 * q], part[2 * q : 3 * q]), BLK, 1)
        )
    return terms


def terms_kernel(a_ref, p_ref, code_ref, group_ref, out_ref, diag, stage):
    step = pl.program_id(0)
    q = BLK // 2
    want, eye, spread, low = constants()

    @pl.when(step == 0)
    def _():
        def one(t, _):
            diag[pl.ds(pl.multiple_of(t * LANES, LANES), LANES), :] = put_diagonal(p_ref[t], want, low)
            return 0

        lax.fori_loop(0, p_ref.shape[0], one, 0, unroll=4)

    for i in range(CHUNK):
        row = step * CHUNK + i
        terms = row_terms(
            lambda c: a_ref[i, :, c * LANES : (c + 1) * LANES],
            code_ref[i],
            group_ref[i],
            diag[pl.ds(pl.multiple_of(row * LANES, LANES), NEAR * LANES), :],
            p_ref[row + HB],
            eye,
            spread,
            low,
        )
        for s in range(KS):
            stage[pl.ds(s * CHUNK + i, q, stride=KS * CHUNK), :] = terms[s]
    out_ref[...] = stage[...].astype(jnp.bfloat16).reshape(out_ref.shape)


def row_codes(a_cols, tile_group):
    fine_rows = a_cols.shape[0]
    q = BLK // 2
    own = lax.axis_index(BOTH) * fine_rows + jnp.arange(fine_rows, dtype=jnp.int32)
    offset = a_cols - own[:, None] + HB
    code = jnp.broadcast_to(offset[:, :, None], (fine_rows, KA, LANES))
    group = jnp.tile(tile_group, (1, q)).reshape(fine_rows, 1, q * KA)
    return code, group


def local_terms(a_tiles, p_tiles, a_cols, tile_group):
    fine_rows = a_tiles.shape[0]
    q = BLK // 2
    near_p = extended(p_tiles, HB).reshape(fine_rows + 2 * HB, q, LANES)
    code, group = row_codes(a_cols, tile_group)
    steps = fine_rows // CHUNK
    return pl.pallas_call(
        terms_kernel,
        grid=(steps,),
        in_specs=[
            pl.BlockSpec((CHUNK, KA, BLK * BLK), lambda g: (g, 0, 0)),
            pl.BlockSpec((fine_rows + 2 * HB, q, LANES), lambda g: (0, 0, 0)),
            pl.BlockSpec((CHUNK, KA, LANES), lambda g: (g, 0, 0)),
            pl.BlockSpec((CHUNK, 1, q * KA), lambda g: (g, 0, 0)),
        ],
        out_specs=pl.BlockSpec((q, KS * CHUNK, LANES), lambda g: (0, g, 0)),
        out_shape=jax.ShapeDtypeStruct((q, fine_rows * KS, LANES), jnp.bfloat16),
        scratch_shapes=[
            pltpu.VMEM(((fine_rows + 2 * HB) * LANES, LANES), jnp.bfloat16),
            pltpu.VMEM((q * KS * CHUNK, LANES), jnp.float32),
        ],
        compiler_params=pltpu.CompilerParams(vmem_limit_bytes=40 * 1024 * 1024),
    )(a_tiles, near_p, code, group)


HALVES = 2
GROUP = 4
PIECE = 16
SPREAD = 40
AFTER = 2
FLIGHT = 2


def one_if(condition):
    return jnp.where(condition, 1.0, 0.0)


def halves_kernel(
    pair_count, devices,
    a_hbm, p_hbm, cols_hbm, group_hbm, slots_hbm, aggregate_hbm, out_ref,
    a_ref, p_ref, cols_ref, groups_ref, slots_ref, agg_ref,
    tiles, diag, turned, code, pick, stage, products, sums, term_ref, got, goals, sent_sums, got_sums, final, parts,
    a_came, p_came, small_came, halo_sent, halo_came, sent, came, goal_sent, goal_came, cross_sent, cross_came, final_sent, final_came, self_came,
):
    q = BLK // 2
    me = lax.axis_index("rows") * pair_count + lax.axis_index("pair")
    team = devices // HALVES
    half, mine = lax.div(me, team), lax.rem(me, team)
    turn = half * (team // 2)
    mirror = me ^ (devices - team // 2)
    my_slice = mine ^ turn
    fine_rows = turned.shape[0] // BLK
    strips = got.shape[0]
    chunks = fine_rows // PIECE
    coarse_rows = parts.shape[0] // KC
    members = team * KC
    ahead, behind = lax.rem(me + 1, devices), lax.rem(me + devices - 1, devices)

    def at(device):
        return (lax.div(device, pair_count), lax.rem(device, pair_count))

    def copy(src, dst, send_sem, recv_sem, device):
        return pltpu.make_async_remote_copy(
            src_ref=src,
            dst_ref=dst,
            send_sem=send_sem,
            recv_sem=recv_sem,
            device_id=at(device),
            device_id_type=pl.DeviceIdType.MESH,
        )

    def whole_rows(index, count):
        return pl.ds(pl.multiple_of(index * count, count), count)

    def a_copy(order):
        rows = whole_rows(lax.rem(order + 1, chunks), PIECE)
        return pltpu.make_async_copy(a_hbm.at[rows], a_ref.at[rows], a_came.at[order])

    def p_copy(t):
        rows = whole_rows(t, 8 * q)
        return pltpu.make_async_copy(p_hbm.at[rows], p_ref.at[rows], p_came.at[t])

    small = [
        pltpu.make_async_copy(src, dst, small_came.at[i])
        for i, (src, dst) in enumerate(
            [(cols_hbm, cols_ref), (group_hbm, groups_ref), (slots_hbm, slots_ref), (aggregate_hbm, agg_ref)]
        )
    ]
    edge = HB * LANES
    inner = fine_rows * LANES
    halo_up = copy(diag.at[pl.ds(inner, edge)], diag.at[pl.ds(0, edge)], halo_sent.at[0], halo_came.at[0], ahead)
    halo_down = copy(diag.at[pl.ds(edge, edge)], diag.at[pl.ds(inner + edge, edge)], halo_sent.at[1], halo_came.at[1], behind)

    def member(k):
        return mine ^ k

    def goal_copy(k):
        return copy(goals.at[mine], goals.at[mine], goal_sent, goal_came, half * team + member(k))

    def strip(slot, g):
        return (slot ^ turn) * strips + g

    def term_part(k, chunk):
        rows = whole_rows(chunk, KS * PIECE)
        return copy(term_ref.at[strip(member(k), 0), rows], got.at[0, mine, rows], sent.at[0], came.at[0], half * team + member(k))

    def term_rest(k, g):
        return copy(term_ref.at[strip(member(k), g)], got.at[g, mine], sent.at[g], came.at[g], half * team + member(k))

    def cross_copy(n):
        return copy(sent_sums.at[n], got_sums.at[n], cross_sent.at[n], cross_came.at[n], mirror)

    def final_copy(k, n):
        g, r = lax.div(n, coarse_rows), lax.rem(n, coarse_rows)
        return copy(
            final.at[n, whole_rows(member(k), KC)],
            parts.at[whole_rows(r, KC), whole_rows(strip(mine, g), LANES)],
            final_sent,
            final_came,
            half * team + member(k),
        )

    others = pl.ds(0, team - 1)
    all_goals = copy(goals.at[others], goals.at[others], goal_sent, goal_came, mirror)
    all_terms = [copy(got.at[g, others], got.at[g, others], sent.at[g], came.at[g], mirror) for g in range(strips)]
    but_one = pl.ds(0, members - KC)
    all_final = copy(final.at[:, but_one], final.at[:, but_one], final_sent, final_came, mirror)

    barrier = pltpu.get_barrier_semaphore()
    for device in [half * team + member(k) for k in range(1, team)] + [mirror, ahead, behind]:
        pl.semaphore_signal(barrier, inc=1, device_id=at(device), device_id_type=pl.DeviceIdType.MESH)
    for t in range(fine_rows // 8):
        p_copy(t).start()
    for transfer in small:
        transfer.start()
    for order in range(chunks):
        a_copy(order).start()

    r128, k128 = iota((LANES, LANES), 0), iota((LANES, LANES), 1)
    want = one_if((r128 // BLK == k128 // BLK) & (r128 % BLK == 2 * (k128 % q) + (k128 // q) % 2)).astype(jnp.bfloat16)
    perm = one_if((r128 // BLK == k128 // BLK) & (k128 % BLK == 2 * (r128 % q) + (r128 % BLK) // q)).astype(jnp.bfloat16)
    low = iota((q, LANES), 1) < BLK

    for transfer in small:
        transfer.wait()
    offset = cols_ref[...] - (me * fine_rows + iota((KA, fine_rows), 1)) + HB
    for i in range(fine_rows):
        code[i] = jnp.broadcast_to(offset[:, i : i + 1], (KA, LANES))
    repeat = one_if(iota((KA, q * KA), 1) % KA == iota((KA, q * KA), 0)).astype(jnp.bfloat16)
    pick[...] = lax.dot_general(
        groups_ref[...].astype(jnp.float32).astype(jnp.bfloat16),
        repeat,
        (((0,), (0,)), ((), ())),
        preferred_element_type=jnp.float32,
    )
    count = fine_rows * KS
    term, fine = iota((fine_rows, count), 1), iota((fine_rows, count), 0)
    goal_rows = []
    for s in range(KS):
        place = one_if(term == (fine // PIECE) * (KS * PIECE) + s * PIECE + fine % PIECE).astype(jnp.bfloat16)
        values = jnp.where(
            iota((KA, fine_rows), 0) == 0,
            jnp.broadcast_to(agg_ref[...], (KA, fine_rows)),
            jnp.broadcast_to(slots_ref[s : s + 1, :], (KA, fine_rows)),
        )
        values = values.astype(jnp.float32).astype(jnp.bfloat16)
        goal_rows.append(jnp.dot(values, place, preferred_element_type=jnp.float32))
    goals[mine] = goal_rows[0] + goal_rows[1]

    def prepare(t16, _):
        p_copy(2 * t16).wait()
        p_copy(2 * t16 + 1).wait()
        tiles[...] = p_ref[whole_rows(t16, 16 * q), :].astype(jnp.float32)
        for t2 in range(8):
            flats = []
            for u in range(2):
                flat = tiles[pl.ds(t2 // 4 * 8 * q + t2 % 4 * 2 + u, q, stride=8), :]
                t = t16 * 16 + 2 * t2 + u
                diag[whole_rows(t + HB, LANES), :] = put_diagonal(flat, want, low)
                flats.append((flat, pltpu.roll(flat, BLK, 1)))
            both = jnp.concatenate(
                [jnp.where(low, flats[0][0], flats[1][1]), jnp.where(low, flats[0][1], flats[1][0])], axis=0
            ).astype(jnp.bfloat16)
            turned[whole_rows(t16 * 8 + t2, LANES), :] = lax.dot_general(
                perm, both, (((1,), (1,)), ((), ())), preferred_element_type=jnp.float32
            ).astype(jnp.bfloat16)
        return 0

    lax.fori_loop(0, fine_rows // 16, prepare, 0)
    pl.semaphore_wait(barrier, team + 2)
    halo_up.start()
    halo_down.start()
    for k in range(1, team):
        goal_copy(k).start()

    even = one_if(iota((q, q * KA), 1) // KA == iota((q, q * KA), 0)).astype(jnp.bfloat16)

    def full_mask(condition):
        one = one_if(condition)
        pair = jnp.concatenate([one, one], axis=0).astype(jnp.bfloat16)
        return jnp.broadcast_to(pair[None], (q // 2,) + pair.shape).reshape(q * KA, LANES)

    def full(condition):
        return jnp.broadcast_to(condition[None], (q, KA, LANES)).reshape(q * KA, LANES)

    def multiply(first):
        for u2 in range(GROUP // 2):
            row = first + 2 * u2
            near = [diag[whole_rows(row + j, LANES), :] for j in range(NEAR + 1)]
            zero = jnp.zeros_like(near[0])
            middle = jnp.concatenate(
                [jnp.concatenate(near[1:3], axis=1), jnp.concatenate(near[3:5], axis=1)], axis=0
            )
            outer = jnp.concatenate(
                [jnp.concatenate([near[0], zero], axis=1), jnp.concatenate([zero, near[5]], axis=1)], axis=0
            )
            rows = [a_ref[row], a_ref[row + 1]]
            edges = jnp.dot(jnp.concatenate(rows, axis=1), outer, preferred_element_type=jnp.float32)
            for u in range(2):
                which = code[row + u] + u
                upper = rows[u] * full_mask((which == 3) | (which == 4))
                inside = jnp.dot(
                    jnp.concatenate([rows[u] - upper, upper], axis=1), middle, preferred_element_type=jnp.float32
                )
                result = jnp.where(
                    full(which == NEAR * u),
                    edges[:, u * LANES : (u + 1) * LANES],
                    jnp.where(full((which == 1) | (which == 3)), inside[:, :LANES], inside[:, LANES:]),
                )
                at_row = (2 * u2 + u) * q * KA
                products[at_row : at_row + q * KA, :] = result.astype(jnp.bfloat16)

    def add_groups(first):
        for u in range(GROUP):
            one = even * jnp.broadcast_to(pick[pl.ds(first + u, 1), :], even.shape).astype(jnp.bfloat16)
            both = jnp.dot(
                jnp.concatenate([even - one, one], axis=0),
                products[u * q * KA : (u + 1) * q * KA, :],
                preferred_element_type=jnp.float32,
            )
            s0, s1 = both[:q], both[q:]
            t0, t1 = pltpu.roll(s0, BLK, 1), pltpu.roll(s1, BLK, 1)
            sums[u * BLK : (u + 1) * BLK, :] = jnp.concatenate(
                [jnp.where(low, s0, t1), jnp.where(low, t0, s1)], axis=0
            ).astype(jnp.bfloat16)

    def project(first):
        for u in range(GROUP):
            row = first + u
            both = jnp.dot(
                turned[whole_rows(row, BLK), :],
                sums[u * BLK : (u + 1) * BLK, :],
                preferred_element_type=jnp.float32,
            )
            even_rows, odd_rows = both[:q], both[q:]
            t0, t1 = pltpu.roll(even_rows, BLK, 1), pltpu.roll(odd_rows, BLK, 1)
            place = lax.rem(row, PIECE)
            stage[pl.ds(place, q, stride=SPREAD), :] = jnp.where(low, even_rows, t1)
            stage[pl.ds(PIECE + place, q, stride=SPREAD), :] = jnp.where(low, t0, odd_rows)

    groups = fine_rows // GROUP
    per = PIECE // GROUP

    def first_row(index):
        return lax.rem(index + per, groups) * GROUP

    def step(t, _):
        @pl.when((lax.rem(t, per) == 0) & (t < groups))
        def _():
            a_copy(lax.div(t, per)).wait()

        @pl.when(t == (chunks - 2) * per)
        def _():
            halo_up.wait_recv()
            halo_down.wait_recv()

        project(first_row(jnp.maximum(t - 2, 0)))
        add_groups(first_row(jnp.clip(t - 1, 0, groups - 1)))
        multiply(first_row(jnp.minimum(t, groups - 1)))

        @pl.when((t >= AFTER) & (lax.rem(t - AFTER, per) == per - 1))
        def _():
            chunk = lax.rem(lax.div(t - AFTER, per) + 1, chunks)
            rows = whole_rows(chunk, KS * PIECE)
            for pair in range(q):
                term_ref[pair, rows, :] = stage[pair * SPREAD : pair * SPREAD + KS * PIECE, :].astype(jnp.bfloat16)
            for k in range(1, team):
                term_part(k, chunk).start()

        return 0

    lax.fori_loop(0, groups + AFTER, step, 0)
    for g in range(1, strips):
        for k in range(1, team):
            term_rest(k, g).start()
    keep = [pltpu.make_async_copy(term_ref.at[strip(mine, g)], got.at[g, mine], self_came.at[g]) for g in range(strips)]
    for transfer in keep:
        transfer.start()
    all_goals.wait_recv()
    all_terms[0].wait_recv()
    keep[0].wait()

    def everyone(row, copies):
        return jnp.concatenate([jnp.broadcast_to(goals[j, row : row + 1, :], (copies, count)) for j in range(team)], axis=1)

    coarse = everyone(0, KA)
    slot = everyone(1, 2 * KA)
    slot_hot = one_if(slot == iota(slot.shape, 0).astype(jnp.float32)).astype(jnp.bfloat16)

    def half_sums(which, n):
        g, r = lax.div(n, coarse_rows), lax.rem(n, coarse_rows)
        pieces = []
        for j in range(team):
            row = ((which * team + j) * coarse_rows + r).astype(jnp.float32)
            one = one_if(coarse == row)
            pieces.append(slot_hot * jnp.concatenate([one, one], axis=0).astype(jnp.bfloat16))
        return jnp.dot(
            jnp.concatenate(pieces, axis=0), got[g].reshape(-1, LANES), preferred_element_type=jnp.float32
        )

    steps = strips * coarse_rows

    def cross(n, _):
        sent_sums[n] = half_sums(1 - half, n).astype(jnp.bfloat16)

        @pl.when(n < FLIGHT)
        def _():
            cross_copy(n).start()

        return 0

    lax.fori_loop(0, FLIGHT, cross, 0)

    def finish(n, _):
        @pl.when(n == coarse_rows - FLIGHT)
        def _():
            for g in range(1, strips):
                all_terms[g].wait_recv()
                keep[g].wait()

        @pl.when(n < steps - FLIGHT)
        def _():
            cross(n + FLIGHT, 0)

        own = half_sums(half, n)

        @pl.when(n < steps - FLIGHT)
        def _():
            cross_copy(n).wait_send()
            cross_copy(n + FLIGHT).start()

        cross_copy(n).wait_recv()
        final[n] = (own + got_sums[n].astype(jnp.float32)).astype(jnp.bfloat16)
        for k in range(1, team):
            final_copy(k, n).start()
        g, r = lax.div(n, coarse_rows), lax.rem(n, coarse_rows)
        parts[whole_rows(r, KC), whole_rows(strip(mine, g), LANES)] = final[n, whole_rows(mine, KC), :]
        return 0

    lax.fori_loop(0, steps, finish, 0)
    halo_up.wait_send()
    halo_down.wait_send()
    all_goals.wait_send()
    for g in range(strips):
        all_terms[g].wait_send()
    for n in range(steps - FLIGHT, steps):
        cross_copy(n).wait_send()
    all_final.wait_send()
    all_final.wait_recv()
    out_ref[...] = parts[...]


def by_halves(a_tiles, p_tiles, a_cols, tile_group, coarse_slots, aggregate):
    fine_rows, _, width = a_tiles.shape
    q = BLK // 2
    devices, pair_count = lax.axis_size(BOTH), lax.axis_size("pair")
    team = devices // HALVES
    strips = width // team // LANES
    count = fine_rows * KS
    coarse_rows = fine_rows // RATIO
    chunks = fine_rows // PIECE
    members = team * KC
    a = a_tiles.reshape(fine_rows, KA, q, LANES).transpose(0, 2, 1, 3).reshape(fine_rows, q * KA, LANES)
    p = p_tiles.reshape(fine_rows // 8, 8, q, LANES).transpose(0, 2, 1, 3).reshape(fine_rows * q, LANES)
    bf16, f32, i32 = jnp.bfloat16, jnp.float32, jnp.int32
    dma = pltpu.SemaphoreType.DMA
    return pl.pallas_call(
        functools.partial(halves_kernel, pair_count, devices),
        in_specs=[pl.BlockSpec(memory_space=pltpu.HBM)] * 6,
        out_specs=pl.BlockSpec(memory_space=pltpu.VMEM),
        out_shape=jax.ShapeDtypeStruct((coarse_rows * KC, width), bf16),
        scratch_shapes=[
            pltpu.VMEM(a.shape, bf16),
            pltpu.VMEM(p.shape, bf16),
            pltpu.VMEM((KA, fine_rows), i32),
            pltpu.VMEM((KA, fine_rows), i32),
            pltpu.VMEM((KS, fine_rows), i32),
            pltpu.VMEM((1, fine_rows), i32),
            pltpu.VMEM((16 * q, LANES), f32),
            pltpu.VMEM(((fine_rows + 2 * HB) * LANES, LANES), bf16),
            pltpu.VMEM((fine_rows * BLK, BLK), bf16),
            pltpu.VMEM((fine_rows, KA, LANES), i32),
            pltpu.VMEM((fine_rows, q * KA), f32),
            pltpu.VMEM((q * SPREAD, LANES), f32),
            pltpu.VMEM((GROUP * q * KA, LANES), bf16),
            pltpu.VMEM((GROUP * BLK, LANES), bf16),
            pltpu.VMEM((width // LANES, count, LANES), bf16),
            pltpu.VMEM((strips, team, count, LANES), bf16),
            pltpu.VMEM((team, KA, count), f32),
            pltpu.VMEM((strips * coarse_rows, members, LANES), bf16),
            pltpu.VMEM((strips * coarse_rows, members, LANES), bf16),
            pltpu.VMEM((strips * coarse_rows, members, LANES), bf16),
            pltpu.VMEM((coarse_rows * KC, width), bf16),
            dma((chunks,)),
            dma((fine_rows // 8,)),
            dma((4,)),
            dma((2,)),
            dma((2,)),
            dma((strips,)),
            dma((strips,)),
            dma,
            dma,
            dma((strips * coarse_rows,)),
            dma((strips * coarse_rows,)),
            dma,
            dma,
            dma((strips,)),
        ],
        compiler_params=pltpu.CompilerParams(
            collective_id=0, has_side_effects=True, vmem_limit_bytes=60 * 1024 * 1024
        ),
    )(a, p, a_cols.T, tile_group.T, coarse_slots.T, aggregate.reshape(1, fine_rows))


def routed(terms, coarse_slots, aggregate):
    fine_rows = aggregate.shape[0]
    q = BLK // 2
    width = BLK * BLK
    rows_count, pair_count = lax.axis_size("rows"), lax.axis_size("pair")
    flat = terms.reshape(q, fine_rows // CHUNK, KS, CHUNK, 2, BLK)
    flat = flat.transpose(1, 3, 2, 4, 0, 5).reshape(fine_rows, KS, width)
    group_size = fine_rows // RATIO * pair_count
    capacity = 2 * fine_rows // rows_count
    dest_group = aggregate // group_size
    local_rows = aggregate - dest_group * group_size
    targets = local_rows[:, None] * KC + coarse_slots
    order = jnp.arange(fine_rows)
    same = (dest_group[:, None] == dest_group[None, :]) & (order[None, :] < order[:, None])
    position = dest_group * capacity + jnp.sum(same.astype(jnp.int32), axis=1)

    def exchange(values):
        buffer = jnp.zeros((rows_count * capacity,) + values.shape[1:], values.dtype)
        buffer = buffer.at[position].set(values)
        return lax.all_to_all(buffer, "rows", split_axis=0, concat_axis=0, tiled=True)

    got = exchange(flat).reshape(-1, width).astype(jnp.float32)
    panel = jax.ops.segment_sum(
        got, exchange(targets).reshape(-1), num_segments=group_size * KC
    )
    panel = panel.reshape(group_size, KC, width)
    return lax.psum_scatter(panel, "pair", scatter_dimension=0, tiled=True)


def body(a_tiles, p_tiles, a_cols, tile_group, coarse_slots, aggregate):
    fine_rows, width = p_tiles.shape
    devices = lax.axis_size(BOTH)
    if devices * LANES != width:
        return routed(local_terms(a_tiles, p_tiles, a_cols, tile_group), coarse_slots, aggregate)
    result = by_halves(a_tiles, p_tiles, a_cols, tile_group, coarse_slots, aggregate)
    return result.reshape(fine_rows // RATIO, KC, width).astype(jnp.float32)


def solution(mesh):
    return jax.shard_map(
        body,
        mesh=mesh,
        in_specs=(
            P(BOTH, None, None),
            P(BOTH, None),
            P(BOTH, None),
            P(BOTH, None),
            P(BOTH, None),
            P(BOTH),
        ),
        out_specs=P(BOTH, None, None),
        check_vma=False,
    )
```

```python
import functools

import jax
import jax.numpy as jnp
from jax import lax
from jax.experimental import pallas as pl
from jax.experimental.pallas import tpu as pltpu
from jax.sharding import PartitionSpec as P

BLK = 64
KA = 8
KS = 2
KC = 16
HB = 2
RATIO = 16
LANES = 128
NEAR = 2 * HB + 1
CHUNK = 8
BOTH = ("rows", "pair")


def extended(array, width):
    devices, length = lax.axis_size(BOTH), array.shape[0]
    up = [(i, i + 1) for i in range(devices - 1)]
    down = [(j, i) for i, j in up]
    before = lax.ppermute(array[length - width :], BOTH, up)
    after = lax.ppermute(array[:width], BOTH, down)
    return jnp.concatenate([before, array, after], axis=0)


def iota(shape, dim):
    return lax.broadcasted_iota(jnp.int32, shape, dim)


def put_diagonal(flat, want, low):
    flat = flat.astype(jnp.float32)
    turned = pltpu.roll(flat, BLK, 1)
    zero = jnp.zeros_like(flat)
    parts = jnp.concatenate(
        [
            jnp.where(low, flat, zero),
            jnp.where(low, turned, zero),
            jnp.where(low, zero, turned),
            jnp.where(low, zero, flat),
        ],
        axis=0,
    ).astype(jnp.bfloat16)
    return jnp.dot(want, parts, preferred_element_type=jnp.float32).astype(jnp.bfloat16)


def constants():
    q = BLK // 2
    r, k = iota((LANES, LANES), 0), iota((LANES, LANES), 1)
    want = jnp.where(
        (r // BLK == k // BLK) & (r % BLK == 2 * (k % q) + (k // q) % 2), 1.0, 0.0
    ).astype(jnp.bfloat16)
    eye = jnp.where(r == k, 1.0, 0.0).astype(jnp.bfloat16)
    spread = jnp.where(
        iota((q, q * KA), 0) == iota((q, q * KA), 1) // KA, 1.0, 0.0
    ).astype(jnp.bfloat16)
    low = iota((q, LANES), 1) < BLK
    return want, eye, spread, low


def row_terms(read, code, group, near, own, eye, spread, low):
    q = BLK // 2
    tiles = jnp.concatenate([read(c).astype(jnp.float32) for c in range(q)], axis=0)
    tiles = tiles.astype(jnp.bfloat16)

    def picked(j):
        one = jnp.where(code == j, 1.0, 0.0)
        pair = jnp.concatenate([one, one], axis=0).astype(jnp.bfloat16)
        return jnp.broadcast_to(pair[None], (q // 2,) + pair.shape).reshape(tiles.shape)

    left = jnp.concatenate([tiles * picked(j) for j in range(NEAR)], axis=1)
    products = jnp.dot(left, near, preferred_element_type=jnp.float32).astype(jnp.bfloat16)
    turned = lax.dot_general(
        eye, own, (((1,), (1,)), ((), ())), preferred_element_type=jnp.float32
    ).astype(jnp.bfloat16)
    wide = jnp.dot(turned, spread, preferred_element_type=jnp.float32).astype(jnp.bfloat16)
    rows = jnp.concatenate(
        [wide * jnp.where(group == s, 1.0, 0.0).astype(jnp.bfloat16) for s in range(KS)], axis=0
    )
    full = jnp.dot(rows, products, preferred_element_type=jnp.float32)
    terms = []
    for s in range(KS):
        part = full[s * LANES : (s + 1) * LANES]
        terms.append(
            jnp.where(low, part[:q], part[3 * q :])
            + pltpu.roll(jnp.where(low, part[q : 2 * q], part[2 * q : 3 * q]), BLK, 1)
        )
    return terms


def terms_kernel(a_ref, p_ref, code_ref, group_ref, out_ref, diag, stage):
    step = pl.program_id(0)
    q = BLK // 2
    want, eye, spread, low = constants()

    @pl.when(step == 0)
    def _():
        def one(t, _):
            diag[pl.ds(pl.multiple_of(t * LANES, LANES), LANES), :] = put_diagonal(p_ref[t], want, low)
            return 0

        lax.fori_loop(0, p_ref.shape[0], one, 0, unroll=4)

    for i in range(CHUNK):
        row = step * CHUNK + i
        terms = row_terms(
            lambda c: a_ref[i, :, c * LANES : (c + 1) * LANES],
            code_ref[i],
            group_ref[i],
            diag[pl.ds(pl.multiple_of(row * LANES, LANES), NEAR * LANES), :],
            p_ref[row + HB],
            eye,
            spread,
            low,
        )
        for s in range(KS):
            stage[pl.ds(s * CHUNK + i, q, stride=KS * CHUNK), :] = terms[s]
    out_ref[...] = stage[...].astype(jnp.bfloat16).reshape(out_ref.shape)


def row_codes(a_cols, tile_group):
    fine_rows = a_cols.shape[0]
    q = BLK // 2
    own = lax.axis_index(BOTH) * fine_rows + jnp.arange(fine_rows, dtype=jnp.int32)
    offset = a_cols - own[:, None] + HB
    code = jnp.broadcast_to(offset[:, :, None], (fine_rows, KA, LANES))
    group = jnp.tile(tile_group, (1, q)).reshape(fine_rows, 1, q * KA)
    return code, group


def local_terms(a_tiles, p_tiles, a_cols, tile_group):
    fine_rows = a_tiles.shape[0]
    q = BLK // 2
    near_p = extended(p_tiles, HB).reshape(fine_rows + 2 * HB, q, LANES)
    code, group = row_codes(a_cols, tile_group)
    steps = fine_rows // CHUNK
    return pl.pallas_call(
        terms_kernel,
        grid=(steps,),
        in_specs=[
            pl.BlockSpec((CHUNK, KA, BLK * BLK), lambda g: (g, 0, 0)),
            pl.BlockSpec((fine_rows + 2 * HB, q, LANES), lambda g: (0, 0, 0)),
            pl.BlockSpec((CHUNK, KA, LANES), lambda g: (g, 0, 0)),
            pl.BlockSpec((CHUNK, 1, q * KA), lambda g: (g, 0, 0)),
        ],
        out_specs=pl.BlockSpec((q, KS * CHUNK, LANES), lambda g: (0, g, 0)),
        out_shape=jax.ShapeDtypeStruct((q, fine_rows * KS, LANES), jnp.bfloat16),
        scratch_shapes=[
            pltpu.VMEM(((fine_rows + 2 * HB) * LANES, LANES), jnp.bfloat16),
            pltpu.VMEM((q * KS * CHUNK, LANES), jnp.float32),
        ],
        compiler_params=pltpu.CompilerParams(vmem_limit_bytes=40 * 1024 * 1024),
    )(a_tiles, near_p, code, group)


HALVES = 2
GROUP = 4
PIECE = 16
SPREAD = 40
AFTER = 2
FLIGHT = 3


def one_if(condition):
    return jnp.where(condition, 1.0, 0.0)


def halves_kernel(
    pair_count, devices,
    a_hbm, p_hbm, cols_hbm, group_hbm, slots_hbm, aggregate_hbm, out_ref,
    a_ref, p_ref, cols_ref, groups_ref, slots_ref, agg_ref,
    tiles, diag, turned, code, pick, stage, products, sums, term_ref, got, goals, sent_sums, got_sums, final, parts,
    a_came, p_came, small_came, halo_sent, halo_came, sent, came, goal_sent, goal_came, cross_sent, cross_came, final_sent, final_came, self_came,
):
    q = BLK // 2
    me = lax.axis_index("rows") * pair_count + lax.axis_index("pair")
    team = devices // HALVES
    half, mine = lax.div(me, team), lax.rem(me, team)
    turn = half * (team // 2)
    mirror = me ^ (devices - team // 2)
    my_slice = mine ^ turn
    fine_rows = turned.shape[0] // BLK
    strips = got.shape[0]
    chunks = fine_rows // PIECE
    coarse_rows = parts.shape[1] // KC
    members = team * KC
    ahead, behind = lax.rem(me + 1, devices), lax.rem(me + devices - 1, devices)

    def at(device):
        return (lax.div(device, pair_count), lax.rem(device, pair_count))

    def copy(src, dst, send_sem, recv_sem, device):
        return pltpu.make_async_remote_copy(
            src_ref=src,
            dst_ref=dst,
            send_sem=send_sem,
            recv_sem=recv_sem,
            device_id=at(device),
            device_id_type=pl.DeviceIdType.MESH,
        )

    def whole_rows(index, count):
        return pl.ds(pl.multiple_of(index * count, count), count)

    def a_copy(order):
        rows = whole_rows(lax.rem(order + 1, chunks), PIECE)
        return pltpu.make_async_copy(a_hbm.at[rows], a_ref.at[rows], a_came.at[order])

    def p_copy(t):
        rows = whole_rows(t, 8 * q)
        return pltpu.make_async_copy(p_hbm.at[rows], p_ref.at[rows], p_came.at[t])

    small = [
        pltpu.make_async_copy(src, dst, small_came.at[i])
        for i, (src, dst) in enumerate(
            [(cols_hbm, cols_ref), (group_hbm, groups_ref), (slots_hbm, slots_ref), (aggregate_hbm, agg_ref)]
        )
    ]
    edge = HB * LANES
    inner = fine_rows * LANES
    halo_up = copy(diag.at[pl.ds(inner, edge)], diag.at[pl.ds(0, edge)], halo_sent.at[0], halo_came.at[0], ahead)
    halo_down = copy(diag.at[pl.ds(edge, edge)], diag.at[pl.ds(inner + edge, edge)], halo_sent.at[1], halo_came.at[1], behind)

    def member(k):
        return mine ^ k

    def goal_copy(k):
        return copy(goals.at[mine], goals.at[mine], goal_sent, goal_came, half * team + member(k))

    def strip(slot, g):
        return (slot ^ turn) * strips + g

    def term_part(k, chunk):
        rows = whole_rows(chunk, KS * PIECE)
        return copy(term_ref.at[strip(member(k), 0), rows], got.at[0, mine, rows], sent.at[0], came.at[0], half * team + member(k))

    def term_rest(k, g):
        return copy(term_ref.at[strip(member(k), g)], got.at[g, mine], sent.at[g], came.at[g], half * team + member(k))

    def cross_copy(n):
        return copy(sent_sums.at[n], got_sums.at[n], cross_sent.at[n], cross_came.at[n], mirror)

    held = coarse_rows * KC
    batch = members // held
    batches = team // batch

    def first_owner(n):
        return lax.rem(lax.rem(n, batches) + my_slice, batches) * batch

    def final_copy(n, b):
        return copy(
            final.at[n, whole_rows(b, held)],
            parts.at[strip(mine, lax.div(n, batches))],
            final_sent,
            final_came,
            half * team + first_owner(n) + b,
        )

    others = pl.ds(0, team - 1)
    all_goals = copy(goals.at[others], goals.at[others], goal_sent, goal_came, mirror)
    all_terms = [copy(got.at[g, others], got.at[g, others], sent.at[g], came.at[g], mirror) for g in range(strips)]
    but_own = pl.ds(0, strips * (team - 1))
    all_final = copy(parts.at[but_own], parts.at[but_own], final_sent, final_came, mirror)

    barrier = pltpu.get_barrier_semaphore()
    for device in [half * team + member(k) for k in range(1, team)] + [mirror, ahead, behind]:
        pl.semaphore_signal(barrier, inc=1, device_id=at(device), device_id_type=pl.DeviceIdType.MESH)
    for t in range(fine_rows // 8):
        p_copy(t).start()
    for transfer in small:
        transfer.start()
    for order in range(chunks):
        a_copy(order).start()

    r128, k128 = iota((LANES, LANES), 0), iota((LANES, LANES), 1)
    want = one_if((r128 // BLK == k128 // BLK) & (r128 % BLK == 2 * (k128 % q) + (k128 // q) % 2)).astype(jnp.bfloat16)
    perm = one_if((r128 // BLK == k128 // BLK) & (k128 % BLK == 2 * (r128 % q) + (r128 % BLK) // q)).astype(jnp.bfloat16)
    low = iota((q, LANES), 1) < BLK

    for transfer in small:
        transfer.wait()
    offset = cols_ref[...] - (me * fine_rows + iota((KA, fine_rows), 1)) + HB
    for i in range(fine_rows):
        code[i] = jnp.broadcast_to(offset[:, i : i + 1], (KA, LANES))
    repeat = one_if(iota((KA, q * KA), 1) % KA == iota((KA, q * KA), 0)).astype(jnp.bfloat16)
    pick[...] = lax.dot_general(
        groups_ref[...].astype(jnp.float32).astype(jnp.bfloat16),
        repeat,
        (((0,), (0,)), ((), ())),
        preferred_element_type=jnp.float32,
    )
    count = fine_rows * KS
    term, fine = iota((fine_rows, count), 1), iota((fine_rows, count), 0)
    goal_rows = []
    for s in range(KS):
        place = one_if(term == (fine // PIECE) * (KS * PIECE) + s * PIECE + fine % PIECE).astype(jnp.bfloat16)
        values = jnp.where(
            iota((KA, fine_rows), 0) == 0,
            jnp.broadcast_to(agg_ref[...], (KA, fine_rows)),
            jnp.broadcast_to(slots_ref[s : s + 1, :], (KA, fine_rows)),
        )
        values = values.astype(jnp.float32).astype(jnp.bfloat16)
        goal_rows.append(jnp.dot(values, place, preferred_element_type=jnp.float32))
    goals[mine] = goal_rows[0] + goal_rows[1]

    def prepare(t16, _):
        p_copy(2 * t16).wait()
        p_copy(2 * t16 + 1).wait()
        tiles[...] = p_ref[whole_rows(t16, 16 * q), :].astype(jnp.float32)
        for t2 in range(8):
            flats = []
            for u in range(2):
                flat = tiles[pl.ds(t2 // 4 * 8 * q + t2 % 4 * 2 + u, q, stride=8), :]
                t = t16 * 16 + 2 * t2 + u
                diag[whole_rows(t + HB, LANES), :] = put_diagonal(flat, want, low)
                flats.append((flat, pltpu.roll(flat, BLK, 1)))
            both = jnp.concatenate(
                [jnp.where(low, flats[0][0], flats[1][1]), jnp.where(low, flats[0][1], flats[1][0])], axis=0
            ).astype(jnp.bfloat16)
            turned[whole_rows(t16 * 8 + t2, LANES), :] = lax.dot_general(
                perm, both, (((1,), (1,)), ((), ())), preferred_element_type=jnp.float32
            ).astype(jnp.bfloat16)
        return 0

    lax.fori_loop(0, fine_rows // 16, prepare, 0)
    pl.semaphore_wait(barrier, team + 2)
    halo_up.start()
    halo_down.start()
    for k in range(1, team):
        goal_copy(k).start()

    even = one_if(iota((q, q * KA), 1) // KA == iota((q, q * KA), 0)).astype(jnp.bfloat16)

    def full_mask(condition):
        one = one_if(condition)
        pair = jnp.concatenate([one, one], axis=0).astype(jnp.bfloat16)
        return jnp.broadcast_to(pair[None], (q // 2,) + pair.shape).reshape(q * KA, LANES)

    def full(condition):
        return jnp.broadcast_to(condition[None], (q, KA, LANES)).reshape(q * KA, LANES)

    def multiply(first):
        for u2 in range(GROUP // 2):
            row = first + 2 * u2
            near = [diag[whole_rows(row + j, LANES), :] for j in range(NEAR + 1)]
            zero = jnp.zeros_like(near[0])
            middle = jnp.concatenate(
                [jnp.concatenate(near[1:3], axis=1), jnp.concatenate(near[3:5], axis=1)], axis=0
            )
            outer = jnp.concatenate(
                [jnp.concatenate([near[0], zero], axis=1), jnp.concatenate([zero, near[5]], axis=1)], axis=0
            )
            rows = [a_ref[row], a_ref[row + 1]]
            edges = jnp.dot(jnp.concatenate(rows, axis=1), outer, preferred_element_type=jnp.float32)
            for u in range(2):
                which = code[row + u] + u
                upper = rows[u] * full_mask((which == 3) | (which == 4))
                inside = jnp.dot(
                    jnp.concatenate([rows[u] - upper, upper], axis=1), middle, preferred_element_type=jnp.float32
                )
                result = jnp.where(
                    full(which == NEAR * u),
                    edges[:, u * LANES : (u + 1) * LANES],
                    jnp.where(full((which == 1) | (which == 3)), inside[:, :LANES], inside[:, LANES:]),
                )
                at_row = (2 * u2 + u) * q * KA
                products[at_row : at_row + q * KA, :] = result.astype(jnp.bfloat16)

    def add_groups(first):
        for u in range(GROUP):
            one = even * jnp.broadcast_to(pick[pl.ds(first + u, 1), :], even.shape).astype(jnp.bfloat16)
            both = jnp.dot(
                jnp.concatenate([even - one, one], axis=0),
                products[u * q * KA : (u + 1) * q * KA, :],
                preferred_element_type=jnp.float32,
            )
            s0, s1 = both[:q], both[q:]
            t0, t1 = pltpu.roll(s0, BLK, 1), pltpu.roll(s1, BLK, 1)
            sums[u * BLK : (u + 1) * BLK, :] = jnp.concatenate(
                [jnp.where(low, s0, t1), jnp.where(low, t0, s1)], axis=0
            ).astype(jnp.bfloat16)

    def project(first):
        for u in range(GROUP):
            row = first + u
            both = jnp.dot(
                turned[whole_rows(row, BLK), :],
                sums[u * BLK : (u + 1) * BLK, :],
                preferred_element_type=jnp.float32,
            )
            even_rows, odd_rows = both[:q], both[q:]
            t0, t1 = pltpu.roll(even_rows, BLK, 1), pltpu.roll(odd_rows, BLK, 1)
            place = lax.rem(row, PIECE)
            stage[pl.ds(place, q, stride=SPREAD), :] = jnp.where(low, even_rows, t1)
            stage[pl.ds(PIECE + place, q, stride=SPREAD), :] = jnp.where(low, t0, odd_rows)

    groups = fine_rows // GROUP
    per = PIECE // GROUP

    def first_row(index):
        return lax.rem(index + per, groups) * GROUP

    def step(t, _):
        @pl.when((lax.rem(t, per) == 0) & (t < groups))
        def _():
            a_copy(lax.div(t, per)).wait()

        @pl.when(t == (chunks - 2) * per)
        def _():
            halo_up.wait_recv()
            halo_down.wait_recv()

        project(first_row(jnp.maximum(t - 2, 0)))
        add_groups(first_row(jnp.clip(t - 1, 0, groups - 1)))
        multiply(first_row(jnp.minimum(t, groups - 1)))

        @pl.when((t >= AFTER) & (lax.rem(t - AFTER, per) == per - 1))
        def _():
            chunk = lax.rem(lax.div(t - AFTER, per) + 1, chunks)
            rows = whole_rows(chunk, KS * PIECE)
            for pair in range(q):
                term_ref[pair, rows, :] = stage[pair * SPREAD : pair * SPREAD + KS * PIECE, :].astype(jnp.bfloat16)
            for k in range(1, team):
                term_part(k, chunk).start()

        return 0

    lax.fori_loop(0, groups + AFTER, step, 0)
    for g in range(1, strips):
        for k in range(1, team):
            term_rest(k, g).start()
    keep = [pltpu.make_async_copy(term_ref.at[strip(mine, g)], got.at[g, mine], self_came.at[g]) for g in range(strips)]
    for transfer in keep:
        transfer.start()
    all_goals.wait_recv()
    all_terms[0].wait_recv()
    keep[0].wait()

    def everyone(row, copies):
        return jnp.concatenate([jnp.broadcast_to(goals[j, row : row + 1, :], (copies, count)) for j in range(team)], axis=1)

    coarse = everyone(0, KA)
    slot = everyone(1, 2 * KA)
    slot_hot = one_if(slot == iota(slot.shape, 0).astype(jnp.float32)).astype(jnp.bfloat16)

    def half_sums(which, n):
        first = (which * team + first_owner(n)) * coarse_rows
        pieces = []
        for j in range(batch * coarse_rows):
            one = one_if(coarse == (first + j).astype(jnp.float32))
            pieces.append(slot_hot * jnp.concatenate([one, one], axis=0).astype(jnp.bfloat16))
        return jnp.dot(
            jnp.concatenate(pieces, axis=0), got[lax.div(n, batches)].reshape(-1, LANES), preferred_element_type=jnp.float32
        )

    steps = strips * batches

    def cross(n, _):
        sent_sums[n] = half_sums(1 - half, n).astype(jnp.bfloat16)

        @pl.when(n < FLIGHT)
        def _():
            cross_copy(n).start()

        return 0

    lax.fori_loop(0, FLIGHT, cross, 0)

    def finish(n, _):
        @pl.when(n == batches - FLIGHT)
        def _():
            for g in range(1, strips):
                all_terms[g].wait_recv()
                keep[g].wait()

        @pl.when(n < steps - FLIGHT)
        def _():
            cross(n + FLIGHT, 0)

        own = half_sums(half, n)

        @pl.when(n < steps - FLIGHT)
        def _():
            cross_copy(n).wait_send()
            cross_copy(n + FLIGHT).start()

        cross_copy(n).wait_recv()
        final[n] = (own + got_sums[n].astype(jnp.float32)).astype(jnp.bfloat16)
        for b in range(batch):
            owner = first_owner(n) + b

            @pl.when(owner != mine)
            def _():
                final_copy(n, b).start()

            @pl.when(owner == mine)
            def _():
                parts[strip(mine, lax.div(n, batches))] = final[n, b * held : (b + 1) * held, :]

        return 0

    lax.fori_loop(0, steps, finish, 0)
    halo_up.wait_send()
    halo_down.wait_send()
    all_goals.wait_send()
    for g in range(strips):
        all_terms[g].wait_send()
    for n in range(steps - FLIGHT, steps):
        cross_copy(n).wait_send()
    all_final.wait_send()
    all_final.wait_recv()
    for column in range(parts.shape[0]):
        out_ref[:, column * LANES : (column + 1) * LANES] = parts[column]


def by_halves(a_tiles, p_tiles, a_cols, tile_group, coarse_slots, aggregate):
    fine_rows, _, width = a_tiles.shape
    q = BLK // 2
    devices, pair_count = lax.axis_size(BOTH), lax.axis_size("pair")
    team = devices // HALVES
    strips = width // team // LANES
    count = fine_rows * KS
    coarse_rows = fine_rows // RATIO
    chunks = fine_rows // PIECE
    members = team * KC
    a = a_tiles.reshape(fine_rows, KA, q, LANES).transpose(0, 2, 1, 3).reshape(fine_rows, q * KA, LANES)
    p = p_tiles.reshape(fine_rows // 8, 8, q, LANES).transpose(0, 2, 1, 3).reshape(fine_rows * q, LANES)
    bf16, f32, i32 = jnp.bfloat16, jnp.float32, jnp.int32
    dma = pltpu.SemaphoreType.DMA
    return pl.pallas_call(
        functools.partial(halves_kernel, pair_count, devices),
        in_specs=[pl.BlockSpec(memory_space=pltpu.HBM)] * 6,
        out_specs=pl.BlockSpec(memory_space=pltpu.VMEM),
        out_shape=jax.ShapeDtypeStruct((coarse_rows * KC, width), bf16),
        scratch_shapes=[
            pltpu.VMEM(a.shape, bf16),
            pltpu.VMEM(p.shape, bf16),
            pltpu.VMEM((KA, fine_rows), i32),
            pltpu.VMEM((KA, fine_rows), i32),
            pltpu.VMEM((KS, fine_rows), i32),
            pltpu.VMEM((1, fine_rows), i32),
            pltpu.VMEM((16 * q, LANES), f32),
            pltpu.VMEM(((fine_rows + 2 * HB) * LANES, LANES), bf16),
            pltpu.VMEM((fine_rows * BLK, BLK), bf16),
            pltpu.VMEM((fine_rows, KA, LANES), i32),
            pltpu.VMEM((fine_rows, q * KA), f32),
            pltpu.VMEM((q * SPREAD, LANES), f32),
            pltpu.VMEM((GROUP * q * KA, LANES), bf16),
            pltpu.VMEM((GROUP * BLK, LANES), bf16),
            pltpu.VMEM((width // LANES, count, LANES), bf16),
            pltpu.VMEM((strips, team, count, LANES), bf16),
            pltpu.VMEM((team, KA, count), f32),
            pltpu.VMEM((strips * coarse_rows, members, LANES), bf16),
            pltpu.VMEM((strips * coarse_rows, members, LANES), bf16),
            pltpu.VMEM((strips * coarse_rows, members, LANES), bf16),
            pltpu.VMEM((width // LANES, coarse_rows * KC, LANES), bf16),
            dma((chunks,)),
            dma((fine_rows // 8,)),
            dma((4,)),
            dma((2,)),
            dma((2,)),
            dma((strips,)),
            dma((strips,)),
            dma,
            dma,
            dma((strips * coarse_rows,)),
            dma((strips * coarse_rows,)),
            dma,
            dma,
            dma((strips,)),
        ],
        compiler_params=pltpu.CompilerParams(
            collective_id=0, has_side_effects=True, vmem_limit_bytes=60 * 1024 * 1024
        ),
    )(a, p, a_cols.T, tile_group.T, coarse_slots.T, aggregate.reshape(1, fine_rows))


def routed(terms, coarse_slots, aggregate):
    fine_rows = aggregate.shape[0]
    q = BLK // 2
    width = BLK * BLK
    rows_count, pair_count = lax.axis_size("rows"), lax.axis_size("pair")
    flat = terms.reshape(q, fine_rows // CHUNK, KS, CHUNK, 2, BLK)
    flat = flat.transpose(1, 3, 2, 4, 0, 5).reshape(fine_rows, KS, width)
    group_size = fine_rows // RATIO * pair_count
    capacity = 2 * fine_rows // rows_count
    dest_group = aggregate // group_size
    local_rows = aggregate - dest_group * group_size
    targets = local_rows[:, None] * KC + coarse_slots
    order = jnp.arange(fine_rows)
    same = (dest_group[:, None] == dest_group[None, :]) & (order[None, :] < order[:, None])
    position = dest_group * capacity + jnp.sum(same.astype(jnp.int32), axis=1)

    def exchange(values):
        buffer = jnp.zeros((rows_count * capacity,) + values.shape[1:], values.dtype)
        buffer = buffer.at[position].set(values)
        return lax.all_to_all(buffer, "rows", split_axis=0, concat_axis=0, tiled=True)

    got = exchange(flat).reshape(-1, width).astype(jnp.float32)
    panel = jax.ops.segment_sum(
        got, exchange(targets).reshape(-1), num_segments=group_size * KC
    )
    panel = panel.reshape(group_size, KC, width)
    return lax.psum_scatter(panel, "pair", scatter_dimension=0, tiled=True)


def body(a_tiles, p_tiles, a_cols, tile_group, coarse_slots, aggregate):
    fine_rows, width = p_tiles.shape
    devices = lax.axis_size(BOTH)
    if devices * LANES != width:
        return routed(local_terms(a_tiles, p_tiles, a_cols, tile_group), coarse_slots, aggregate)
    result = by_halves(a_tiles, p_tiles, a_cols, tile_group, coarse_slots, aggregate)
    return result.reshape(fine_rows // RATIO, KC, width).astype(jnp.float32)


def solution(mesh):
    return jax.shard_map(
        body,
        mesh=mesh,
        in_specs=(
            P(BOTH, None, None),
            P(BOTH, None),
            P(BOTH, None),
            P(BOTH, None),
            P(BOTH, None),
            P(BOTH),
        ),
        out_specs=P(BOTH, None, None),
        check_vma=False,
    )
```

```python
import functools

import jax
import jax.numpy as jnp
from jax import lax
from jax.experimental import pallas as pl
from jax.experimental.pallas import tpu as pltpu
from jax.sharding import PartitionSpec as P

BLK = 64
KA = 8
KS = 2
KC = 16
HB = 2
RATIO = 16
LANES = 128
NEAR = 2 * HB + 1
CHUNK = 8
BOTH = ("rows", "pair")


def extended(array, width):
    devices, length = lax.axis_size(BOTH), array.shape[0]
    up = [(i, i + 1) for i in range(devices - 1)]
    down = [(j, i) for i, j in up]
    before = lax.ppermute(array[length - width :], BOTH, up)
    after = lax.ppermute(array[:width], BOTH, down)
    return jnp.concatenate([before, array, after], axis=0)


def iota(shape, dim):
    return lax.broadcasted_iota(jnp.int32, shape, dim)


def put_diagonal(flat, want, low):
    flat = flat.astype(jnp.float32)
    turned = pltpu.roll(flat, BLK, 1)
    zero = jnp.zeros_like(flat)
    parts = jnp.concatenate(
        [
            jnp.where(low, flat, zero),
            jnp.where(low, turned, zero),
            jnp.where(low, zero, turned),
            jnp.where(low, zero, flat),
        ],
        axis=0,
    ).astype(jnp.bfloat16)
    return jnp.dot(want, parts, preferred_element_type=jnp.float32).astype(jnp.bfloat16)


def constants():
    q = BLK // 2
    r, k = iota((LANES, LANES), 0), iota((LANES, LANES), 1)
    want = jnp.where(
        (r // BLK == k // BLK) & (r % BLK == 2 * (k % q) + (k // q) % 2), 1.0, 0.0
    ).astype(jnp.bfloat16)
    eye = jnp.where(r == k, 1.0, 0.0).astype(jnp.bfloat16)
    spread = jnp.where(
        iota((q, q * KA), 0) == iota((q, q * KA), 1) // KA, 1.0, 0.0
    ).astype(jnp.bfloat16)
    low = iota((q, LANES), 1) < BLK
    return want, eye, spread, low


def row_terms(read, code, group, near, own, eye, spread, low):
    q = BLK // 2
    tiles = jnp.concatenate([read(c).astype(jnp.float32) for c in range(q)], axis=0)
    tiles = tiles.astype(jnp.bfloat16)

    def picked(j):
        one = jnp.where(code == j, 1.0, 0.0)
        pair = jnp.concatenate([one, one], axis=0).astype(jnp.bfloat16)
        return jnp.broadcast_to(pair[None], (q // 2,) + pair.shape).reshape(tiles.shape)

    left = jnp.concatenate([tiles * picked(j) for j in range(NEAR)], axis=1)
    products = jnp.dot(left, near, preferred_element_type=jnp.float32).astype(jnp.bfloat16)
    turned = lax.dot_general(
        eye, own, (((1,), (1,)), ((), ())), preferred_element_type=jnp.float32
    ).astype(jnp.bfloat16)
    wide = jnp.dot(turned, spread, preferred_element_type=jnp.float32).astype(jnp.bfloat16)
    rows = jnp.concatenate(
        [wide * jnp.where(group == s, 1.0, 0.0).astype(jnp.bfloat16) for s in range(KS)], axis=0
    )
    full = jnp.dot(rows, products, preferred_element_type=jnp.float32)
    terms = []
    for s in range(KS):
        part = full[s * LANES : (s + 1) * LANES]
        terms.append(
            jnp.where(low, part[:q], part[3 * q :])
            + pltpu.roll(jnp.where(low, part[q : 2 * q], part[2 * q : 3 * q]), BLK, 1)
        )
    return terms


def terms_kernel(a_ref, p_ref, code_ref, group_ref, out_ref, diag, stage):
    step = pl.program_id(0)
    q = BLK // 2
    want, eye, spread, low = constants()

    @pl.when(step == 0)
    def _():
        def one(t, _):
            diag[pl.ds(pl.multiple_of(t * LANES, LANES), LANES), :] = put_diagonal(p_ref[t], want, low)
            return 0

        lax.fori_loop(0, p_ref.shape[0], one, 0, unroll=4)

    for i in range(CHUNK):
        row = step * CHUNK + i
        terms = row_terms(
            lambda c: a_ref[i, :, c * LANES : (c + 1) * LANES],
            code_ref[i],
            group_ref[i],
            diag[pl.ds(pl.multiple_of(row * LANES, LANES), NEAR * LANES), :],
            p_ref[row + HB],
            eye,
            spread,
            low,
        )
        for s in range(KS):
            stage[pl.ds(s * CHUNK + i, q, stride=KS * CHUNK), :] = terms[s]
    out_ref[...] = stage[...].astype(jnp.bfloat16).reshape(out_ref.shape)


def row_codes(a_cols, tile_group):
    fine_rows = a_cols.shape[0]
    q = BLK // 2
    own = lax.axis_index(BOTH) * fine_rows + jnp.arange(fine_rows, dtype=jnp.int32)
    offset = a_cols - own[:, None] + HB
    code = jnp.broadcast_to(offset[:, :, None], (fine_rows, KA, LANES))
    group = jnp.tile(tile_group, (1, q)).reshape(fine_rows, 1, q * KA)
    return code, group


def local_terms(a_tiles, p_tiles, a_cols, tile_group):
    fine_rows = a_tiles.shape[0]
    q = BLK // 2
    near_p = extended(p_tiles, HB).reshape(fine_rows + 2 * HB, q, LANES)
    code, group = row_codes(a_cols, tile_group)
    steps = fine_rows // CHUNK
    return pl.pallas_call(
        terms_kernel,
        grid=(steps,),
        in_specs=[
            pl.BlockSpec((CHUNK, KA, BLK * BLK), lambda g: (g, 0, 0)),
            pl.BlockSpec((fine_rows + 2 * HB, q, LANES), lambda g: (0, 0, 0)),
            pl.BlockSpec((CHUNK, KA, LANES), lambda g: (g, 0, 0)),
            pl.BlockSpec((CHUNK, 1, q * KA), lambda g: (g, 0, 0)),
        ],
        out_specs=pl.BlockSpec((q, KS * CHUNK, LANES), lambda g: (0, g, 0)),
        out_shape=jax.ShapeDtypeStruct((q, fine_rows * KS, LANES), jnp.bfloat16),
        scratch_shapes=[
            pltpu.VMEM(((fine_rows + 2 * HB) * LANES, LANES), jnp.bfloat16),
            pltpu.VMEM((q * KS * CHUNK, LANES), jnp.float32),
        ],
        compiler_params=pltpu.CompilerParams(vmem_limit_bytes=40 * 1024 * 1024),
    )(a_tiles, near_p, code, group)


HALVES = 2
GROUP = 4
PIECE = 16
SPREAD = 40
AFTER = 2
FLIGHT = 3
SHARE = 2


def one_if(condition):
    return jnp.where(condition, 1.0, 0.0)


def halves_kernel(
    pair_count, devices,
    a_hbm, p_hbm, cols_hbm, group_hbm, slots_hbm, aggregate_hbm, out_ref,
    a_ref, p_ref, cols_ref, groups_ref, slots_ref, agg_ref,
    tiles, diag, turned, code, pick, stage, products, sums, term_ref, got, goals, sent_sums, got_sums, final, parts, far, far_goals, own,
    a_came, p_came, small_came, halo_sent, halo_came, sent, came, goal_sent, goal_came, cross_sent, cross_came, final_sent, final_came, self_came, far_sent, far_came, far_goal_sent, far_goal_came,
):
    q = BLK // 2
    me = lax.axis_index("rows") * pair_count + lax.axis_index("pair")
    team = devices // HALVES
    half, mine = lax.div(me, team), lax.rem(me, team)
    turn = half * (team // 2)
    mirror = me ^ (devices - team // 2)
    my_slice = mine ^ turn
    fine_rows = turned.shape[0] // BLK
    strips = got.shape[0]
    chunks = fine_rows // PIECE
    coarse_rows = parts.shape[1] // KC
    members = team * KC
    ahead, behind = lax.rem(me + 1, devices), lax.rem(me + devices - 1, devices)

    def at(device):
        return (lax.div(device, pair_count), lax.rem(device, pair_count))

    def copy(src, dst, send_sem, recv_sem, device):
        return pltpu.make_async_remote_copy(
            src_ref=src,
            dst_ref=dst,
            send_sem=send_sem,
            recv_sem=recv_sem,
            device_id=at(device),
            device_id_type=pl.DeviceIdType.MESH,
        )

    def whole_rows(index, count):
        return pl.ds(pl.multiple_of(index * count, count), count)

    def a_copy(order):
        rows = whole_rows(lax.rem(order + 1, chunks), PIECE)
        return pltpu.make_async_copy(a_hbm.at[rows], a_ref.at[rows], a_came.at[order])

    def p_copy(t):
        rows = whole_rows(t, 8 * q)
        return pltpu.make_async_copy(p_hbm.at[rows], p_ref.at[rows], p_came.at[t])

    small = [
        pltpu.make_async_copy(src, dst, small_came.at[i])
        for i, (src, dst) in enumerate(
            [(cols_hbm, cols_ref), (group_hbm, groups_ref), (slots_hbm, slots_ref), (aggregate_hbm, agg_ref)]
        )
    ]
    edge = HB * LANES
    inner = fine_rows * LANES
    halo_up = copy(diag.at[pl.ds(inner, edge)], diag.at[pl.ds(0, edge)], halo_sent.at[0], halo_came.at[0], ahead)
    halo_down = copy(diag.at[pl.ds(edge, edge)], diag.at[pl.ds(inner + edge, edge)], halo_sent.at[1], halo_came.at[1], behind)

    def member(k):
        return mine ^ k

    def goal_copy(k):
        return copy(goals.at[mine], goals.at[mine], goal_sent, goal_came, half * team + member(k))

    def strip(slot, g):
        return (slot ^ turn) * strips + g

    def term_part(k, chunk):
        rows = whole_rows(chunk, KS * PIECE)
        return copy(term_ref.at[strip(member(k), 0), rows], got.at[0, mine, rows], sent.at[0], came.at[0], half * team + member(k))

    def term_rest(k, g):
        return copy(term_ref.at[strip(member(k), g)], got.at[g, mine], sent.at[g], came.at[g], half * team + member(k))

    def cross_copy(n):
        return copy(sent_sums.at[n], got_sums.at[n], cross_sent.at[n], cross_came.at[n], mirror)

    held = coarse_rows * KC
    batch = members // held
    batches = team // batch

    def first_owner(n):
        return lax.rem(lax.rem(n, batches) + my_slice, batches) * batch

    def final_copy(n, b):
        return copy(
            final.at[n, whole_rows(b, held)],
            parts.at[strip(mine, lax.div(n, batches))],
            final_sent,
            final_came,
            half * team + first_owner(n) + b,
        )

    holders = team // SHARE
    both_hold = lax.rem(mine, SHARE) == 0
    far_team = (1 - half) * team

    def far_part(h, chunk):
        rows = whole_rows(chunk, KS * PIECE)
        to = lax.rem(h * SHARE + mine, team) // SHARE * SHARE
        place = (to ^ (team // 2 - turn)) * strips
        return copy(term_ref.at[place, rows], far.at[mine, rows], far_sent, far_came, far_team + to)

    def far_goal(h):
        return copy(goals.at[mine], far_goals.at[mine], far_goal_sent, far_goal_came, far_team + h * SHARE)

    some = pl.ds(0, holders)
    far_terms = copy(far.at[some], far.at[some], far_sent, far_came, mirror)
    far_terms_in = copy(far, far, far_sent, far_came, mirror)
    far_goals_out = copy(far_goals.at[some], far_goals.at[some], far_goal_sent, far_goal_came, mirror)
    far_goals_in = copy(far_goals, far_goals, far_goal_sent, far_goal_came, mirror)

    others = pl.ds(0, team - 1)
    all_goals = copy(goals.at[others], goals.at[others], goal_sent, goal_came, mirror)
    all_terms = [copy(got.at[g, others], got.at[g, others], sent.at[g], came.at[g], mirror) for g in range(strips)]
    but_own = pl.ds(0, strips * (team - 1))
    all_final = copy(parts.at[but_own], parts.at[but_own], final_sent, final_came, mirror)

    barrier = pltpu.get_barrier_semaphore()
    for o in range(1, devices):
        pl.semaphore_signal(
            barrier, inc=1, device_id=at(lax.rem(me + o, devices)), device_id_type=pl.DeviceIdType.MESH
        )
    for t in range(fine_rows // 8):
        p_copy(t).start()
    for transfer in small:
        transfer.start()
    for order in range(chunks):
        a_copy(order).start()

    r128, k128 = iota((LANES, LANES), 0), iota((LANES, LANES), 1)
    want = one_if((r128 // BLK == k128 // BLK) & (r128 % BLK == 2 * (k128 % q) + (k128 // q) % 2)).astype(jnp.bfloat16)
    perm = one_if((r128 // BLK == k128 // BLK) & (k128 % BLK == 2 * (r128 % q) + (r128 % BLK) // q)).astype(jnp.bfloat16)
    low = iota((q, LANES), 1) < BLK

    for transfer in small:
        transfer.wait()
    offset = cols_ref[...] - (me * fine_rows + iota((KA, fine_rows), 1)) + HB
    for i in range(fine_rows):
        code[i] = jnp.broadcast_to(offset[:, i : i + 1], (KA, LANES))
    repeat = one_if(iota((KA, q * KA), 1) % KA == iota((KA, q * KA), 0)).astype(jnp.bfloat16)
    pick[...] = lax.dot_general(
        groups_ref[...].astype(jnp.float32).astype(jnp.bfloat16),
        repeat,
        (((0,), (0,)), ((), ())),
        preferred_element_type=jnp.float32,
    )
    count = fine_rows * KS
    term, fine = iota((fine_rows, count), 1), iota((fine_rows, count), 0)
    goal_rows = []
    for s in range(KS):
        place = one_if(term == (fine // PIECE) * (KS * PIECE) + s * PIECE + fine % PIECE).astype(jnp.bfloat16)
        values = jnp.where(
            iota((KA, fine_rows), 0) == 0,
            jnp.broadcast_to(agg_ref[...], (KA, fine_rows)),
            jnp.broadcast_to(slots_ref[s : s + 1, :], (KA, fine_rows)),
        )
        values = values.astype(jnp.float32).astype(jnp.bfloat16)
        goal_rows.append(jnp.dot(values, place, preferred_element_type=jnp.float32))
    goals[mine] = goal_rows[0] + goal_rows[1]

    def prepare(t16, _):
        p_copy(2 * t16).wait()
        p_copy(2 * t16 + 1).wait()
        tiles[...] = p_ref[whole_rows(t16, 16 * q), :].astype(jnp.float32)
        for t2 in range(8):
            flats = []
            for u in range(2):
                flat = tiles[pl.ds(t2 // 4 * 8 * q + t2 % 4 * 2 + u, q, stride=8), :]
                t = t16 * 16 + 2 * t2 + u
                diag[whole_rows(t + HB, LANES), :] = put_diagonal(flat, want, low)
                flats.append((flat, pltpu.roll(flat, BLK, 1)))
            both = jnp.concatenate(
                [jnp.where(low, flats[0][0], flats[1][1]), jnp.where(low, flats[0][1], flats[1][0])], axis=0
            ).astype(jnp.bfloat16)
            turned[whole_rows(t16 * 8 + t2, LANES), :] = lax.dot_general(
                perm, both, (((1,), (1,)), ((), ())), preferred_element_type=jnp.float32
            ).astype(jnp.bfloat16)
        return 0

    lax.fori_loop(0, fine_rows // 16, prepare, 0)
    pl.semaphore_wait(barrier, devices - 1)
    halo_up.start()
    halo_down.start()
    for k in range(1, team):
        goal_copy(k).start()
    for h in range(holders):
        far_goal(h).start()

    even = one_if(iota((q, q * KA), 1) // KA == iota((q, q * KA), 0)).astype(jnp.bfloat16)

    def full_mask(condition):
        one = one_if(condition)
        pair = jnp.concatenate([one, one], axis=0).astype(jnp.bfloat16)
        return jnp.broadcast_to(pair[None], (q // 2,) + pair.shape).reshape(q * KA, LANES)

    def full(condition):
        return jnp.broadcast_to(condition[None], (q, KA, LANES)).reshape(q * KA, LANES)

    def multiply(first):
        for u2 in range(GROUP // 2):
            row = first + 2 * u2
            near = [diag[whole_rows(row + j, LANES), :] for j in range(NEAR + 1)]
            zero = jnp.zeros_like(near[0])
            middle = jnp.concatenate(
                [jnp.concatenate(near[1:3], axis=1), jnp.concatenate(near[3:5], axis=1)], axis=0
            )
            outer = jnp.concatenate(
                [jnp.concatenate([near[0], zero], axis=1), jnp.concatenate([zero, near[5]], axis=1)], axis=0
            )
            rows = [a_ref[row], a_ref[row + 1]]
            edges = jnp.dot(jnp.concatenate(rows, axis=1), outer, preferred_element_type=jnp.float32)
            for u in range(2):
                which = code[row + u] + u
                upper = rows[u] * full_mask((which == 3) | (which == 4))
                inside = jnp.dot(
                    jnp.concatenate([rows[u] - upper, upper], axis=1), middle, preferred_element_type=jnp.float32
                )
                result = jnp.where(
                    full(which == NEAR * u),
                    edges[:, u * LANES : (u + 1) * LANES],
                    jnp.where(full((which == 1) | (which == 3)), inside[:, :LANES], inside[:, LANES:]),
                )
                at_row = (2 * u2 + u) * q * KA
                products[at_row : at_row + q * KA, :] = result.astype(jnp.bfloat16)

    def add_groups(first):
        for u in range(GROUP):
            one = even * jnp.broadcast_to(pick[pl.ds(first + u, 1), :], even.shape).astype(jnp.bfloat16)
            both = jnp.dot(
                jnp.concatenate([even - one, one], axis=0),
                products[u * q * KA : (u + 1) * q * KA, :],
                preferred_element_type=jnp.float32,
            )
            s0, s1 = both[:q], both[q:]
            t0, t1 = pltpu.roll(s0, BLK, 1), pltpu.roll(s1, BLK, 1)
            sums[u * BLK : (u + 1) * BLK, :] = jnp.concatenate(
                [jnp.where(low, s0, t1), jnp.where(low, t0, s1)], axis=0
            ).astype(jnp.bfloat16)

    def project(first):
        for u in range(GROUP):
            row = first + u
            both = jnp.dot(
                turned[whole_rows(row, BLK), :],
                sums[u * BLK : (u + 1) * BLK, :],
                preferred_element_type=jnp.float32,
            )
            even_rows, odd_rows = both[:q], both[q:]
            t0, t1 = pltpu.roll(even_rows, BLK, 1), pltpu.roll(odd_rows, BLK, 1)
            place = lax.rem(row, PIECE)
            stage[pl.ds(place, q, stride=SPREAD), :] = jnp.where(low, even_rows, t1)
            stage[pl.ds(PIECE + place, q, stride=SPREAD), :] = jnp.where(low, t0, odd_rows)

    groups = fine_rows // GROUP
    per = PIECE // GROUP

    def first_row(index):
        return lax.rem(index + per, groups) * GROUP

    def step(t, _):
        @pl.when((lax.rem(t, per) == 0) & (t < groups))
        def _():
            a_copy(lax.div(t, per)).wait()

        @pl.when(t == (chunks - 2) * per)
        def _():
            halo_up.wait_recv()
            halo_down.wait_recv()

        project(first_row(jnp.maximum(t - 2, 0)))
        add_groups(first_row(jnp.clip(t - 1, 0, groups - 1)))
        multiply(first_row(jnp.minimum(t, groups - 1)))

        @pl.when((t >= AFTER) & (lax.rem(t - AFTER, per) == per - 1))
        def _():
            chunk = lax.rem(lax.div(t - AFTER, per) + 1, chunks)
            rows = whole_rows(chunk, KS * PIECE)
            for pair in range(q):
                term_ref[pair, rows, :] = stage[pair * SPREAD : pair * SPREAD + KS * PIECE, :].astype(jnp.bfloat16)
            for h in range(holders):
                far_part(h, chunk).start()
            for k in range(1, team):
                term_part(k, chunk).start()

        return 0

    lax.fori_loop(0, groups + AFTER, step, 0)
    for g in range(1, strips):
        for k in range(1, team):
            term_rest(k, g).start()
    keep = [pltpu.make_async_copy(term_ref.at[strip(mine, g)], got.at[g, mine], self_came.at[g]) for g in range(strips)]
    for transfer in keep:
        transfer.start()
    all_goals.wait_recv()
    all_terms[0].wait_recv()
    keep[0].wait()

    def everyone(rows, row, copies):
        return jnp.concatenate([jnp.broadcast_to(rows[j, row : row + 1, :], (copies, count)) for j in range(team)], axis=1)

    def hot_slots(rows):
        slot = everyone(rows, 1, 2 * KA)
        return one_if(slot == iota(slot.shape, 0).astype(jnp.float32)).astype(jnp.bfloat16)

    coarse, slot_hot = everyone(goals, 0, KA), hot_slots(goals)

    def sums_of(coarse, slot_hot, values, which, n):
        first = (which * team + first_owner(n)) * coarse_rows
        pieces = []
        for j in range(batch * coarse_rows):
            one = one_if(coarse == (first + j).astype(jnp.float32))
            pieces.append(slot_hot * jnp.concatenate([one, one], axis=0).astype(jnp.bfloat16))
        return jnp.dot(jnp.concatenate(pieces, axis=0), values, preferred_element_type=jnp.float32)

    def half_sums(which, n):
        return sums_of(coarse, slot_hot, got[lax.div(n, batches)].reshape(-1, LANES), which, n)

    def crosses(n):
        return jnp.logical_not(both_hold) | (n >= batches)

    steps = strips * batches

    def prepared(n):
        sent_sums[n] = half_sums(1 - half, n).astype(jnp.bfloat16)

    def cross(n, _):
        @pl.when(crosses(n))
        def _():
            prepared(n)
            cross_copy(n).start()

        return 0

    lax.fori_loop(0, FLIGHT, cross, 0)

    @pl.when(both_hold)
    def _():
        far_goals_in.wait_recv()
        far_terms_in.wait_recv()

    def finish(n, _):
        @pl.when(n == batches - FLIGHT)
        def _():
            for g in range(1, strips):
                all_terms[g].wait_recv()
                keep[g].wait()

        @pl.when((n < steps - FLIGHT) & crosses(n + FLIGHT))
        def _():
            prepared(n + FLIGHT)

        own[...] = half_sums(half, n)

        @pl.when((n < steps - FLIGHT) & crosses(n))
        def _():
            cross_copy(n).wait_send()

        @pl.when((n < steps - FLIGHT) & crosses(n + FLIGHT))
        def _():
            cross_copy(n + FLIGHT).start()

        @pl.when(crosses(n))
        def _():
            cross_copy(n).wait_recv()
            final[n] = (own[...] + got_sums[n].astype(jnp.float32)).astype(jnp.bfloat16)

        @pl.when(jnp.logical_not(crosses(n)))
        def _():
            more = sums_of(everyone(far_goals, 0, KA), hot_slots(far_goals), far[...].reshape(-1, LANES), half, n)
            final[n] = (own[...] + more).astype(jnp.bfloat16)

        for b in range(batch):
            owner = first_owner(n) + b

            @pl.when(owner != mine)
            def _():
                final_copy(n, b).start()

            @pl.when(owner == mine)
            def _():
                parts[strip(mine, lax.div(n, batches))] = final[n, b * held : (b + 1) * held, :]

        return 0

    lax.fori_loop(0, steps, finish, 0)
    halo_up.wait_send()
    halo_down.wait_send()
    all_goals.wait_send()
    for g in range(strips):
        all_terms[g].wait_send()
    for n in range(steps - FLIGHT, steps):
        cross_copy(n).wait_send()
    far_terms.wait_send()
    far_goals_out.wait_send()
    all_final.wait_send()
    all_final.wait_recv()
    for column in range(parts.shape[0]):
        out_ref[:, column * LANES : (column + 1) * LANES] = parts[column]


def by_halves(a_tiles, p_tiles, a_cols, tile_group, coarse_slots, aggregate):
    fine_rows, _, width = a_tiles.shape
    q = BLK // 2
    devices, pair_count = lax.axis_size(BOTH), lax.axis_size("pair")
    team = devices // HALVES
    strips = width // team // LANES
    count = fine_rows * KS
    coarse_rows = fine_rows // RATIO
    chunks = fine_rows // PIECE
    members = team * KC
    a = a_tiles.reshape(fine_rows, KA, q, LANES).transpose(0, 2, 1, 3).reshape(fine_rows, q * KA, LANES)
    p = p_tiles.reshape(fine_rows // 8, 8, q, LANES).transpose(0, 2, 1, 3).reshape(fine_rows * q, LANES)
    bf16, f32, i32 = jnp.bfloat16, jnp.float32, jnp.int32
    dma = pltpu.SemaphoreType.DMA
    return pl.pallas_call(
        functools.partial(halves_kernel, pair_count, devices),
        in_specs=[pl.BlockSpec(memory_space=pltpu.HBM)] * 6,
        out_specs=pl.BlockSpec(memory_space=pltpu.VMEM),
        out_shape=jax.ShapeDtypeStruct((coarse_rows * KC, width), bf16),
        scratch_shapes=[
            pltpu.VMEM(a.shape, bf16),
            pltpu.VMEM(p.shape, bf16),
            pltpu.VMEM((KA, fine_rows), i32),
            pltpu.VMEM((KA, fine_rows), i32),
            pltpu.VMEM((KS, fine_rows), i32),
            pltpu.VMEM((1, fine_rows), i32),
            pltpu.VMEM((16 * q, LANES), f32),
            pltpu.VMEM(((fine_rows + 2 * HB) * LANES, LANES), bf16),
            pltpu.VMEM((fine_rows * BLK, BLK), bf16),
            pltpu.VMEM((fine_rows, KA, LANES), i32),
            pltpu.VMEM((fine_rows, q * KA), f32),
            pltpu.VMEM((q * SPREAD, LANES), f32),
            pltpu.VMEM((GROUP * q * KA, LANES), bf16),
            pltpu.VMEM((GROUP * BLK, LANES), bf16),
            pltpu.VMEM((width // LANES, count, LANES), bf16),
            pltpu.VMEM((strips, team, count, LANES), bf16),
            pltpu.VMEM((team, KA, count), f32),
            pltpu.VMEM((strips * coarse_rows, members, LANES), bf16),
            pltpu.VMEM((strips * coarse_rows, members, LANES), bf16),
            pltpu.VMEM((strips * coarse_rows, members, LANES), bf16),
            pltpu.VMEM((width // LANES, coarse_rows * KC, LANES), bf16),
            pltpu.VMEM((team, count, LANES), bf16),
            pltpu.VMEM((team, KA, count), f32),
            pltpu.VMEM((members, LANES), f32),
            dma((chunks,)),
            dma((fine_rows // 8,)),
            dma((4,)),
            dma((2,)),
            dma((2,)),
            dma((strips,)),
            dma((strips,)),
            dma,
            dma,
            dma((strips * coarse_rows,)),
            dma((strips * coarse_rows,)),
            dma,
            dma,
            dma((strips,)),
            dma,
            dma,
            dma,
            dma,
        ],
        compiler_params=pltpu.CompilerParams(
            collective_id=0, has_side_effects=True, vmem_limit_bytes=60 * 1024 * 1024
        ),
    )(a, p, a_cols.T, tile_group.T, coarse_slots.T, aggregate.reshape(1, fine_rows))


def routed(terms, coarse_slots, aggregate):
    fine_rows = aggregate.shape[0]
    q = BLK // 2
    width = BLK * BLK
    rows_count, pair_count = lax.axis_size("rows"), lax.axis_size("pair")
    flat = terms.reshape(q, fine_rows // CHUNK, KS, CHUNK, 2, BLK)
    flat = flat.transpose(1, 3, 2, 4, 0, 5).reshape(fine_rows, KS, width)
    group_size = fine_rows // RATIO * pair_count
    capacity = 2 * fine_rows // rows_count
    dest_group = aggregate // group_size
    local_rows = aggregate - dest_group * group_size
    targets = local_rows[:, None] * KC + coarse_slots
    order = jnp.arange(fine_rows)
    same = (dest_group[:, None] == dest_group[None, :]) & (order[None, :] < order[:, None])
    position = dest_group * capacity + jnp.sum(same.astype(jnp.int32), axis=1)

    def exchange(values):
        buffer = jnp.zeros((rows_count * capacity,) + values.shape[1:], values.dtype)
        buffer = buffer.at[position].set(values)
        return lax.all_to_all(buffer, "rows", split_axis=0, concat_axis=0, tiled=True)

    got = exchange(flat).reshape(-1, width).astype(jnp.float32)
    panel = jax.ops.segment_sum(
        got, exchange(targets).reshape(-1), num_segments=group_size * KC
    )
    panel = panel.reshape(group_size, KC, width)
    return lax.psum_scatter(panel, "pair", scatter_dimension=0, tiled=True)


def body(a_tiles, p_tiles, a_cols, tile_group, coarse_slots, aggregate):
    fine_rows, width = p_tiles.shape
    devices = lax.axis_size(BOTH)
    if devices * LANES != width:
        return routed(local_terms(a_tiles, p_tiles, a_cols, tile_group), coarse_slots, aggregate)
    result = by_halves(a_tiles, p_tiles, a_cols, tile_group, coarse_slots, aggregate)
    return result.reshape(fine_rows // RATIO, KC, width).astype(jnp.float32)


def solution(mesh):
    return jax.shard_map(
        body,
        mesh=mesh,
        in_specs=(
            P(BOTH, None, None),
            P(BOTH, None),
            P(BOTH, None),
            P(BOTH, None),
            P(BOTH, None),
            P(BOTH),
        ),
        out_specs=P(BOTH, None, None),
        check_vma=False,
    )
```

```python
import functools

import jax
import jax.numpy as jnp
from jax import lax
from jax.experimental import pallas as pl
from jax.experimental.pallas import tpu as pltpu
from jax.sharding import PartitionSpec as P

BLK = 64
KA = 8
KS = 2
KC = 16
HB = 2
RATIO = 16
LANES = 128
NEAR = 2 * HB + 1
CHUNK = 8
BOTH = ("rows", "pair")


def extended(array, width):
    devices, length = lax.axis_size(BOTH), array.shape[0]
    up = [(i, i + 1) for i in range(devices - 1)]
    down = [(j, i) for i, j in up]
    before = lax.ppermute(array[length - width :], BOTH, up)
    after = lax.ppermute(array[:width], BOTH, down)
    return jnp.concatenate([before, array, after], axis=0)


def iota(shape, dim):
    return lax.broadcasted_iota(jnp.int32, shape, dim)


def put_diagonal(flat, want, low):
    flat = flat.astype(jnp.float32)
    turned = pltpu.roll(flat, BLK, 1)
    zero = jnp.zeros_like(flat)
    parts = jnp.concatenate(
        [
            jnp.where(low, flat, zero),
            jnp.where(low, turned, zero),
            jnp.where(low, zero, turned),
            jnp.where(low, zero, flat),
        ],
        axis=0,
    ).astype(jnp.bfloat16)
    return jnp.dot(want, parts, preferred_element_type=jnp.float32).astype(jnp.bfloat16)


def constants():
    q = BLK // 2
    r, k = iota((LANES, LANES), 0), iota((LANES, LANES), 1)
    want = jnp.where(
        (r // BLK == k // BLK) & (r % BLK == 2 * (k % q) + (k // q) % 2), 1.0, 0.0
    ).astype(jnp.bfloat16)
    eye = jnp.where(r == k, 1.0, 0.0).astype(jnp.bfloat16)
    spread = jnp.where(
        iota((q, q * KA), 0) == iota((q, q * KA), 1) // KA, 1.0, 0.0
    ).astype(jnp.bfloat16)
    low = iota((q, LANES), 1) < BLK
    return want, eye, spread, low


def row_terms(read, code, group, near, own, eye, spread, low):
    q = BLK // 2
    tiles = jnp.concatenate([read(c).astype(jnp.float32) for c in range(q)], axis=0)
    tiles = tiles.astype(jnp.bfloat16)

    def picked(j):
        one = jnp.where(code == j, 1.0, 0.0)
        pair = jnp.concatenate([one, one], axis=0).astype(jnp.bfloat16)
        return jnp.broadcast_to(pair[None], (q // 2,) + pair.shape).reshape(tiles.shape)

    left = jnp.concatenate([tiles * picked(j) for j in range(NEAR)], axis=1)
    products = jnp.dot(left, near, preferred_element_type=jnp.float32).astype(jnp.bfloat16)
    turned = lax.dot_general(
        eye, own, (((1,), (1,)), ((), ())), preferred_element_type=jnp.float32
    ).astype(jnp.bfloat16)
    wide = jnp.dot(turned, spread, preferred_element_type=jnp.float32).astype(jnp.bfloat16)
    rows = jnp.concatenate(
        [wide * jnp.where(group == s, 1.0, 0.0).astype(jnp.bfloat16) for s in range(KS)], axis=0
    )
    full = jnp.dot(rows, products, preferred_element_type=jnp.float32)
    terms = []
    for s in range(KS):
        part = full[s * LANES : (s + 1) * LANES]
        terms.append(
            jnp.where(low, part[:q], part[3 * q :])
            + pltpu.roll(jnp.where(low, part[q : 2 * q], part[2 * q : 3 * q]), BLK, 1)
        )
    return terms


def terms_kernel(a_ref, p_ref, code_ref, group_ref, out_ref, diag, stage):
    step = pl.program_id(0)
    q = BLK // 2
    want, eye, spread, low = constants()

    @pl.when(step == 0)
    def _():
        def one(t, _):
            diag[pl.ds(pl.multiple_of(t * LANES, LANES), LANES), :] = put_diagonal(p_ref[t], want, low)
            return 0

        lax.fori_loop(0, p_ref.shape[0], one, 0, unroll=4)

    for i in range(CHUNK):
        row = step * CHUNK + i
        terms = row_terms(
            lambda c: a_ref[i, :, c * LANES : (c + 1) * LANES],
            code_ref[i],
            group_ref[i],
            diag[pl.ds(pl.multiple_of(row * LANES, LANES), NEAR * LANES), :],
            p_ref[row + HB],
            eye,
            spread,
            low,
        )
        for s in range(KS):
            stage[pl.ds(s * CHUNK + i, q, stride=KS * CHUNK), :] = terms[s]
    out_ref[...] = stage[...].astype(jnp.bfloat16).reshape(out_ref.shape)


def row_codes(a_cols, tile_group):
    fine_rows = a_cols.shape[0]
    q = BLK // 2
    own = lax.axis_index(BOTH) * fine_rows + jnp.arange(fine_rows, dtype=jnp.int32)
    offset = a_cols - own[:, None] + HB
    code = jnp.broadcast_to(offset[:, :, None], (fine_rows, KA, LANES))
    group = jnp.tile(tile_group, (1, q)).reshape(fine_rows, 1, q * KA)
    return code, group


def local_terms(a_tiles, p_tiles, a_cols, tile_group):
    fine_rows = a_tiles.shape[0]
    q = BLK // 2
    near_p = extended(p_tiles, HB).reshape(fine_rows + 2 * HB, q, LANES)
    code, group = row_codes(a_cols, tile_group)
    steps = fine_rows // CHUNK
    return pl.pallas_call(
        terms_kernel,
        grid=(steps,),
        in_specs=[
            pl.BlockSpec((CHUNK, KA, BLK * BLK), lambda g: (g, 0, 0)),
            pl.BlockSpec((fine_rows + 2 * HB, q, LANES), lambda g: (0, 0, 0)),
            pl.BlockSpec((CHUNK, KA, LANES), lambda g: (g, 0, 0)),
            pl.BlockSpec((CHUNK, 1, q * KA), lambda g: (g, 0, 0)),
        ],
        out_specs=pl.BlockSpec((q, KS * CHUNK, LANES), lambda g: (0, g, 0)),
        out_shape=jax.ShapeDtypeStruct((q, fine_rows * KS, LANES), jnp.bfloat16),
        scratch_shapes=[
            pltpu.VMEM(((fine_rows + 2 * HB) * LANES, LANES), jnp.bfloat16),
            pltpu.VMEM((q * KS * CHUNK, LANES), jnp.float32),
        ],
        compiler_params=pltpu.CompilerParams(vmem_limit_bytes=40 * 1024 * 1024),
    )(a_tiles, near_p, code, group)


HALVES = 2
GROUP = 4
PIECE = 16
SPREAD = 40
AFTER = 2
FLIGHT = 2
SHARE = 2


def one_if(condition):
    return jnp.where(condition, 1.0, 0.0)


def halves_kernel(
    pair_count, devices,
    a_hbm, p_hbm, cols_hbm, group_hbm, slots_hbm, aggregate_hbm, out_ref,
    a_ref, p_ref, cols_ref, groups_ref, slots_ref, agg_ref,
    tiles, diag, turned, code, pick, stage, products, sums, term_ref, got, goals, sent_sums, got_sums, final, parts, far, far_goals, own,
    a_came, p_came, small_came, halo_sent, halo_came, sent, came, goal_sent, goal_came, cross_sent, cross_came, final_sent, final_came, self_came, far_sent, far_came, far_goal_sent, far_goal_came,
):
    q = BLK // 2
    me = lax.axis_index("rows") * pair_count + lax.axis_index("pair")
    team = devices // HALVES
    half, mine = lax.div(me, team), lax.rem(me, team)
    turn = half * (team // 2)
    mirror = me ^ (devices - team // 2)
    my_slice = mine ^ turn
    fine_rows = turned.shape[0] // BLK
    strips = got.shape[0]
    chunks = fine_rows // PIECE
    coarse_rows = parts.shape[1] // KC
    members = team * KC
    ahead, behind = lax.rem(me + 1, devices), lax.rem(me + devices - 1, devices)

    def at(device):
        return (lax.div(device, pair_count), lax.rem(device, pair_count))

    def copy(src, dst, send_sem, recv_sem, device):
        return pltpu.make_async_remote_copy(
            src_ref=src,
            dst_ref=dst,
            send_sem=send_sem,
            recv_sem=recv_sem,
            device_id=at(device),
            device_id_type=pl.DeviceIdType.MESH,
        )

    def whole_rows(index, count):
        return pl.ds(pl.multiple_of(index * count, count), count)

    def a_copy(order):
        rows = whole_rows(lax.rem(order + 1, chunks), PIECE)
        return pltpu.make_async_copy(a_hbm.at[rows], a_ref.at[rows], a_came.at[order])

    def p_copy(t):
        rows = whole_rows(t, 8 * q)
        return pltpu.make_async_copy(p_hbm.at[rows], p_ref.at[rows], p_came.at[t])

    small = [
        pltpu.make_async_copy(src, dst, small_came.at[i])
        for i, (src, dst) in enumerate(
            [(cols_hbm, cols_ref), (group_hbm, groups_ref), (slots_hbm, slots_ref), (aggregate_hbm, agg_ref)]
        )
    ]
    edge = HB * LANES
    inner = fine_rows * LANES
    halo_up = copy(diag.at[pl.ds(inner, edge)], diag.at[pl.ds(0, edge)], halo_sent.at[0], halo_came.at[0], ahead)
    halo_down = copy(diag.at[pl.ds(edge, edge)], diag.at[pl.ds(inner + edge, edge)], halo_sent.at[1], halo_came.at[1], behind)

    def member(k):
        return mine ^ k

    def goal_copy(k):
        return copy(goals.at[mine], goals.at[mine], goal_sent, goal_came, half * team + member(k))

    def strip(slot, g):
        return (slot ^ turn) * strips + g

    def term_part(k, chunk):
        rows = whole_rows(chunk, KS * PIECE)
        return copy(term_ref.at[strip(member(k), 0), rows], got.at[0, mine, rows], sent.at[0], came.at[0], half * team + member(k))

    def term_rest(k, g):
        return copy(term_ref.at[strip(member(k), g)], got.at[g, mine], sent.at[g], came.at[g], half * team + member(k))

    def cross_copy(n):
        return copy(sent_sums.at[n], got_sums.at[n], cross_sent.at[n], cross_came.at[n], mirror)

    held = coarse_rows * KC
    batch = members // held
    batches = team // batch

    def first_owner(n):
        return lax.rem(lax.rem(n, batches) + my_slice, batches) * batch

    def final_copy(n, b):
        return copy(
            final.at[n, whole_rows(b, held)],
            parts.at[strip(mine, lax.div(n, batches))],
            final_sent,
            final_came,
            half * team + first_owner(n) + b,
        )

    holders = team // SHARE
    both_hold = lax.rem(mine, SHARE) == 0
    far_team = (1 - half) * team

    def far_part(h, chunk):
        rows = whole_rows(chunk, KS * PIECE)
        to = lax.rem(h * SHARE + mine, team) // SHARE * SHARE
        place = (to ^ (team // 2 - turn)) * strips + strips - 1
        return copy(term_ref.at[place, rows], far.at[mine, rows], far_sent, far_came, far_team + to)

    def far_goal(h):
        return copy(goals.at[mine], far_goals.at[mine], far_goal_sent, far_goal_came, far_team + h * SHARE)

    some = pl.ds(0, holders)
    far_terms = copy(far.at[some], far.at[some], far_sent, far_came, mirror)
    far_terms_in = copy(far, far, far_sent, far_came, mirror)
    far_goals_out = copy(far_goals.at[some], far_goals.at[some], far_goal_sent, far_goal_came, mirror)
    far_goals_in = copy(far_goals, far_goals, far_goal_sent, far_goal_came, mirror)

    others = pl.ds(0, team - 1)
    all_goals = copy(goals.at[others], goals.at[others], goal_sent, goal_came, mirror)
    all_terms = [copy(got.at[g, others], got.at[g, others], sent.at[g], came.at[g], mirror) for g in range(strips)]
    but_own = pl.ds(0, strips * (team - 1))
    all_final = copy(parts.at[but_own], parts.at[but_own], final_sent, final_came, mirror)

    barrier = pltpu.get_barrier_semaphore()
    for o in range(1, devices):
        pl.semaphore_signal(
            barrier, inc=1, device_id=at(lax.rem(me + o, devices)), device_id_type=pl.DeviceIdType.MESH
        )
    for t in range(fine_rows // 8):
        p_copy(t).start()
    for transfer in small:
        transfer.start()
    for order in range(chunks):
        a_copy(order).start()

    r128, k128 = iota((LANES, LANES), 0), iota((LANES, LANES), 1)
    want = one_if((r128 // BLK == k128 // BLK) & (r128 % BLK == 2 * (k128 % q) + (k128 // q) % 2)).astype(jnp.bfloat16)
    perm = one_if((r128 // BLK == k128 // BLK) & (k128 % BLK == 2 * (r128 % q) + (r128 % BLK) // q)).astype(jnp.bfloat16)
    low = iota((q, LANES), 1) < BLK

    for transfer in small:
        transfer.wait()
    offset = cols_ref[...] - (me * fine_rows + iota((KA, fine_rows), 1)) + HB
    for i in range(fine_rows):
        code[i] = jnp.broadcast_to(offset[:, i : i + 1], (KA, LANES))
    repeat = one_if(iota((KA, q * KA), 1) % KA == iota((KA, q * KA), 0)).astype(jnp.bfloat16)
    pick[...] = lax.dot_general(
        groups_ref[...].astype(jnp.float32).astype(jnp.bfloat16),
        repeat,
        (((0,), (0,)), ((), ())),
        preferred_element_type=jnp.float32,
    )
    count = fine_rows * KS
    term, fine = iota((fine_rows, count), 1), iota((fine_rows, count), 0)
    goal_rows = []
    for s in range(KS):
        place = one_if(term == (fine // PIECE) * (KS * PIECE) + s * PIECE + fine % PIECE).astype(jnp.bfloat16)
        values = jnp.where(
            iota((KA, fine_rows), 0) == 0,
            jnp.broadcast_to(agg_ref[...], (KA, fine_rows)),
            jnp.broadcast_to(slots_ref[s : s + 1, :], (KA, fine_rows)),
        )
        values = values.astype(jnp.float32).astype(jnp.bfloat16)
        goal_rows.append(jnp.dot(values, place, preferred_element_type=jnp.float32))
    goals[mine] = goal_rows[0] + goal_rows[1]

    def prepare(t16, _):
        p_copy(2 * t16).wait()
        p_copy(2 * t16 + 1).wait()
        tiles[...] = p_ref[whole_rows(t16, 16 * q), :].astype(jnp.float32)
        for t2 in range(8):
            flats = []
            for u in range(2):
                flat = tiles[pl.ds(t2 // 4 * 8 * q + t2 % 4 * 2 + u, q, stride=8), :]
                t = t16 * 16 + 2 * t2 + u
                diag[whole_rows(t + HB, LANES), :] = put_diagonal(flat, want, low)
                flats.append((flat, pltpu.roll(flat, BLK, 1)))
            both = jnp.concatenate(
                [jnp.where(low, flats[0][0], flats[1][1]), jnp.where(low, flats[0][1], flats[1][0])], axis=0
            ).astype(jnp.bfloat16)
            turned[whole_rows(t16 * 8 + t2, LANES), :] = lax.dot_general(
                perm, both, (((1,), (1,)), ((), ())), preferred_element_type=jnp.float32
            ).astype(jnp.bfloat16)
        return 0

    lax.fori_loop(0, fine_rows // 16, prepare, 0)
    pl.semaphore_wait(barrier, devices - 1)
    halo_up.start()
    halo_down.start()
    for k in range(1, team):
        goal_copy(k).start()
    for h in range(holders):
        far_goal(h).start()

    even = one_if(iota((q, q * KA), 1) // KA == iota((q, q * KA), 0)).astype(jnp.bfloat16)

    def full_mask(condition):
        one = one_if(condition)
        pair = jnp.concatenate([one, one], axis=0).astype(jnp.bfloat16)
        return jnp.broadcast_to(pair[None], (q // 2,) + pair.shape).reshape(q * KA, LANES)

    def full(condition):
        return jnp.broadcast_to(condition[None], (q, KA, LANES)).reshape(q * KA, LANES)

    def multiply(first):
        for u2 in range(GROUP // 2):
            row = first + 2 * u2
            near = [diag[whole_rows(row + j, LANES), :] for j in range(NEAR + 1)]
            zero = jnp.zeros_like(near[0])
            middle = jnp.concatenate(
                [jnp.concatenate(near[1:3], axis=1), jnp.concatenate(near[3:5], axis=1)], axis=0
            )
            outer = jnp.concatenate(
                [jnp.concatenate([near[0], zero], axis=1), jnp.concatenate([zero, near[5]], axis=1)], axis=0
            )
            rows = [a_ref[row], a_ref[row + 1]]
            edges = jnp.dot(jnp.concatenate(rows, axis=1), outer, preferred_element_type=jnp.float32)
            for u in range(2):
                which = code[row + u] + u
                upper = rows[u] * full_mask((which == 3) | (which == 4))
                inside = jnp.dot(
                    jnp.concatenate([rows[u] - upper, upper], axis=1), middle, preferred_element_type=jnp.float32
                )
                result = jnp.where(
                    full(which == NEAR * u),
                    edges[:, u * LANES : (u + 1) * LANES],
                    jnp.where(full((which == 1) | (which == 3)), inside[:, :LANES], inside[:, LANES:]),
                )
                at_row = (2 * u2 + u) * q * KA
                products[at_row : at_row + q * KA, :] = result.astype(jnp.bfloat16)

    def add_groups(first):
        for u in range(GROUP):
            one = even * jnp.broadcast_to(pick[pl.ds(first + u, 1), :], even.shape).astype(jnp.bfloat16)
            both = jnp.dot(
                jnp.concatenate([even - one, one], axis=0),
                products[u * q * KA : (u + 1) * q * KA, :],
                preferred_element_type=jnp.float32,
            )
            s0, s1 = both[:q], both[q:]
            t0, t1 = pltpu.roll(s0, BLK, 1), pltpu.roll(s1, BLK, 1)
            sums[u * BLK : (u + 1) * BLK, :] = jnp.concatenate(
                [jnp.where(low, s0, t1), jnp.where(low, t0, s1)], axis=0
            ).astype(jnp.bfloat16)

    def project(first):
        for u in range(GROUP):
            row = first + u
            both = jnp.dot(
                turned[whole_rows(row, BLK), :],
                sums[u * BLK : (u + 1) * BLK, :],
                preferred_element_type=jnp.float32,
            )
            even_rows, odd_rows = both[:q], both[q:]
            t0, t1 = pltpu.roll(even_rows, BLK, 1), pltpu.roll(odd_rows, BLK, 1)
            place = lax.rem(row, PIECE)
            stage[pl.ds(place, q, stride=SPREAD), :] = jnp.where(low, even_rows, t1)
            stage[pl.ds(PIECE + place, q, stride=SPREAD), :] = jnp.where(low, t0, odd_rows)

    groups = fine_rows // GROUP
    per = PIECE // GROUP

    def first_row(index):
        return lax.rem(index + per, groups) * GROUP

    def step(t, _):
        @pl.when((lax.rem(t, per) == 0) & (t < groups))
        def _():
            a_copy(lax.div(t, per)).wait()

        @pl.when(t == (chunks - 2) * per)
        def _():
            halo_up.wait_recv()
            halo_down.wait_recv()

        project(first_row(jnp.maximum(t - 2, 0)))
        add_groups(first_row(jnp.clip(t - 1, 0, groups - 1)))
        multiply(first_row(jnp.minimum(t, groups - 1)))

        @pl.when((t >= AFTER) & (lax.rem(t - AFTER, per) == per - 1))
        def _():
            chunk = lax.rem(lax.div(t - AFTER, per) + 1, chunks)
            rows = whole_rows(chunk, KS * PIECE)
            for pair in range(q):
                term_ref[pair, rows, :] = stage[pair * SPREAD : pair * SPREAD + KS * PIECE, :].astype(jnp.bfloat16)
            for k in range(1, team):
                term_part(k, chunk).start()
            for h in range(holders):
                far_part(h, chunk).start()

        return 0

    lax.fori_loop(0, groups + AFTER, step, 0)
    for g in range(1, strips):
        for k in range(1, team):
            term_rest(k, g).start()
    keep = [pltpu.make_async_copy(term_ref.at[strip(mine, g)], got.at[g, mine], self_came.at[g]) for g in range(strips)]
    for transfer in keep:
        transfer.start()
    all_goals.wait_recv()
    all_terms[0].wait_recv()
    keep[0].wait()

    def everyone(rows, row, copies):
        return jnp.concatenate([jnp.broadcast_to(rows[j, row : row + 1, :], (copies, count)) for j in range(team)], axis=1)

    def hot_slots(rows):
        slot = everyone(rows, 1, 2 * KA)
        return one_if(slot == iota(slot.shape, 0).astype(jnp.float32)).astype(jnp.bfloat16)

    coarse, slot_hot = everyone(goals, 0, KA), hot_slots(goals)

    def sums_of(coarse, slot_hot, values, which, n):
        first = (which * team + first_owner(n)) * coarse_rows
        pieces = []
        for j in range(batch * coarse_rows):
            one = one_if(coarse == (first + j).astype(jnp.float32))
            pieces.append(slot_hot * jnp.concatenate([one, one], axis=0).astype(jnp.bfloat16))
        return jnp.dot(jnp.concatenate(pieces, axis=0), values, preferred_element_type=jnp.float32)

    def half_sums(which, n):
        return sums_of(coarse, slot_hot, got[lax.div(n, batches)].reshape(-1, LANES), which, n)

    steps = strips * batches

    def crosses(n):
        return jnp.logical_not(both_hold) | (n < steps - batches)


    def prepared(n):
        sent_sums[n] = half_sums(1 - half, n).astype(jnp.bfloat16)

    def cross(n, _):
        @pl.when(crosses(n))
        def _():
            prepared(n)
            cross_copy(n).start()

        return 0

    lax.fori_loop(0, FLIGHT, cross, 0)

    def finish(n, _):
        @pl.when(n == batches - FLIGHT)
        def _():
            for g in range(1, strips):
                all_terms[g].wait_recv()
                keep[g].wait()

        @pl.when(both_hold & (n == steps - batches))
        def _():
            far_goals_in.wait_recv()
            far_terms_in.wait_recv()

        @pl.when((n < steps - FLIGHT) & crosses(n + FLIGHT))
        def _():
            prepared(n + FLIGHT)

        own[...] = half_sums(half, n)

        @pl.when((n < steps - FLIGHT) & crosses(n))
        def _():
            cross_copy(n).wait_send()

        @pl.when((n < steps - FLIGHT) & crosses(n + FLIGHT))
        def _():
            cross_copy(n + FLIGHT).start()

        @pl.when(crosses(n))
        def _():
            cross_copy(n).wait_recv()
            final[n] = (own[...] + got_sums[n].astype(jnp.float32)).astype(jnp.bfloat16)

        @pl.when(jnp.logical_not(crosses(n)))
        def _():
            more = sums_of(everyone(far_goals, 0, KA), hot_slots(far_goals), far[...].reshape(-1, LANES), half, n)
            final[n] = (own[...] + more).astype(jnp.bfloat16)

        for b in range(batch):
            owner = first_owner(n) + b

            @pl.when(owner != mine)
            def _():
                final_copy(n, b).start()

            @pl.when(owner == mine)
            def _():
                parts[strip(mine, lax.div(n, batches))] = final[n, b * held : (b + 1) * held, :]

        return 0

    lax.fori_loop(0, steps, finish, 0)
    halo_up.wait_send()
    halo_down.wait_send()
    all_goals.wait_send()
    for g in range(strips):
        all_terms[g].wait_send()
    for n in range(steps - FLIGHT, steps):

        @pl.when(crosses(n))
        def _():
            cross_copy(n).wait_send()

    far_terms.wait_send()
    far_goals_out.wait_send()
    all_final.wait_send()
    all_final.wait_recv()
    for column in range(parts.shape[0]):
        out_ref[:, column * LANES : (column + 1) * LANES] = parts[column]


def by_halves(a_tiles, p_tiles, a_cols, tile_group, coarse_slots, aggregate):
    fine_rows, _, width = a_tiles.shape
    q = BLK // 2
    devices, pair_count = lax.axis_size(BOTH), lax.axis_size("pair")
    team = devices // HALVES
    strips = width // team // LANES
    count = fine_rows * KS
    coarse_rows = fine_rows // RATIO
    chunks = fine_rows // PIECE
    members = team * KC
    a = a_tiles.reshape(fine_rows, KA, q, LANES).transpose(0, 2, 1, 3).reshape(fine_rows, q * KA, LANES)
    p = p_tiles.reshape(fine_rows // 8, 8, q, LANES).transpose(0, 2, 1, 3).reshape(fine_rows * q, LANES)
    bf16, f32, i32 = jnp.bfloat16, jnp.float32, jnp.int32
    dma = pltpu.SemaphoreType.DMA
    return pl.pallas_call(
        functools.partial(halves_kernel, pair_count, devices),
        in_specs=[pl.BlockSpec(memory_space=pltpu.HBM)] * 6,
        out_specs=pl.BlockSpec(memory_space=pltpu.VMEM),
        out_shape=jax.ShapeDtypeStruct((coarse_rows * KC, width), bf16),
        scratch_shapes=[
            pltpu.VMEM(a.shape, bf16),
            pltpu.VMEM(p.shape, bf16),
            pltpu.VMEM((KA, fine_rows), i32),
            pltpu.VMEM((KA, fine_rows), i32),
            pltpu.VMEM((KS, fine_rows), i32),
            pltpu.VMEM((1, fine_rows), i32),
            pltpu.VMEM((16 * q, LANES), f32),
            pltpu.VMEM(((fine_rows + 2 * HB) * LANES, LANES), bf16),
            pltpu.VMEM((fine_rows * BLK, BLK), bf16),
            pltpu.VMEM((fine_rows, KA, LANES), i32),
            pltpu.VMEM((fine_rows, q * KA), f32),
            pltpu.VMEM((q * SPREAD, LANES), f32),
            pltpu.VMEM((GROUP * q * KA, LANES), bf16),
            pltpu.VMEM((GROUP * BLK, LANES), bf16),
            pltpu.VMEM((width // LANES, count, LANES), bf16),
            pltpu.VMEM((strips, team, count, LANES), bf16),
            pltpu.VMEM((team, KA, count), f32),
            pltpu.VMEM((strips * coarse_rows, members, LANES), bf16),
            pltpu.VMEM((strips * coarse_rows, members, LANES), bf16),
            pltpu.VMEM((strips * coarse_rows, members, LANES), bf16),
            pltpu.VMEM((width // LANES, coarse_rows * KC, LANES), bf16),
            pltpu.VMEM((team, count, LANES), bf16),
            pltpu.VMEM((team, KA, count), f32),
            pltpu.VMEM((members, LANES), f32),
            dma((chunks,)),
            dma((fine_rows // 8,)),
            dma((4,)),
            dma((2,)),
            dma((2,)),
            dma((strips,)),
            dma((strips,)),
            dma,
            dma,
            dma((strips * coarse_rows,)),
            dma((strips * coarse_rows,)),
            dma,
            dma,
            dma((strips,)),
            dma,
            dma,
            dma,
            dma,
        ],
        compiler_params=pltpu.CompilerParams(
            collective_id=0, has_side_effects=True, vmem_limit_bytes=60 * 1024 * 1024
        ),
    )(a, p, a_cols.T, tile_group.T, coarse_slots.T, aggregate.reshape(1, fine_rows))


def routed(terms, coarse_slots, aggregate):
    fine_rows = aggregate.shape[0]
    q = BLK // 2
    width = BLK * BLK
    rows_count, pair_count = lax.axis_size("rows"), lax.axis_size("pair")
    flat = terms.reshape(q, fine_rows // CHUNK, KS, CHUNK, 2, BLK)
    flat = flat.transpose(1, 3, 2, 4, 0, 5).reshape(fine_rows, KS, width)
    group_size = fine_rows // RATIO * pair_count
    capacity = 2 * fine_rows // rows_count
    dest_group = aggregate // group_size
    local_rows = aggregate - dest_group * group_size
    targets = local_rows[:, None] * KC + coarse_slots
    order = jnp.arange(fine_rows)
    same = (dest_group[:, None] == dest_group[None, :]) & (order[None, :] < order[:, None])
    position = dest_group * capacity + jnp.sum(same.astype(jnp.int32), axis=1)

    def exchange(values):
        buffer = jnp.zeros((rows_count * capacity,) + values.shape[1:], values.dtype)
        buffer = buffer.at[position].set(values)
        return lax.all_to_all(buffer, "rows", split_axis=0, concat_axis=0, tiled=True)

    got = exchange(flat).reshape(-1, width).astype(jnp.float32)
    panel = jax.ops.segment_sum(
        got, exchange(targets).reshape(-1), num_segments=group_size * KC
    )
    panel = panel.reshape(group_size, KC, width)
    return lax.psum_scatter(panel, "pair", scatter_dimension=0, tiled=True)


def body(a_tiles, p_tiles, a_cols, tile_group, coarse_slots, aggregate):
    fine_rows, width = p_tiles.shape
    devices = lax.axis_size(BOTH)
    if devices * LANES != width:
        return routed(local_terms(a_tiles, p_tiles, a_cols, tile_group), coarse_slots, aggregate)
    result = by_halves(a_tiles, p_tiles, a_cols, tile_group, coarse_slots, aggregate)
    return result.reshape(fine_rows // RATIO, KC, width).astype(jnp.float32)


def solution(mesh):
    return jax.shard_map(
        body,
        mesh=mesh,
        in_specs=(
            P(BOTH, None, None),
            P(BOTH, None),
            P(BOTH, None),
            P(BOTH, None),
            P(BOTH, None),
            P(BOTH),
        ),
        out_specs=P(BOTH, None, None),
        check_vma=False,
    )
```

```python
import functools

import jax
import jax.numpy as jnp
from jax import lax
from jax.experimental import pallas as pl
from jax.experimental.pallas import tpu as pltpu
from jax.sharding import PartitionSpec as P

BLK = 64
KA = 8
KS = 2
KC = 16
HB = 2
RATIO = 16
LANES = 128
NEAR = 2 * HB + 1
CHUNK = 8
BOTH = ("rows", "pair")


def extended(array, width):
    devices, length = lax.axis_size(BOTH), array.shape[0]
    up = [(i, i + 1) for i in range(devices - 1)]
    down = [(j, i) for i, j in up]
    before = lax.ppermute(array[length - width :], BOTH, up)
    after = lax.ppermute(array[:width], BOTH, down)
    return jnp.concatenate([before, array, after], axis=0)


def iota(shape, dim):
    return lax.broadcasted_iota(jnp.int32, shape, dim)


def put_diagonal(flat, want, low):
    flat = flat.astype(jnp.float32)
    turned = pltpu.roll(flat, BLK, 1)
    zero = jnp.zeros_like(flat)
    parts = jnp.concatenate(
        [
            jnp.where(low, flat, zero),
            jnp.where(low, turned, zero),
            jnp.where(low, zero, turned),
            jnp.where(low, zero, flat),
        ],
        axis=0,
    ).astype(jnp.bfloat16)
    return jnp.dot(want, parts, preferred_element_type=jnp.float32).astype(jnp.bfloat16)


def constants():
    q = BLK // 2
    r, k = iota((LANES, LANES), 0), iota((LANES, LANES), 1)
    want = jnp.where(
        (r // BLK == k // BLK) & (r % BLK == 2 * (k % q) + (k // q) % 2), 1.0, 0.0
    ).astype(jnp.bfloat16)
    eye = jnp.where(r == k, 1.0, 0.0).astype(jnp.bfloat16)
    spread = jnp.where(
        iota((q, q * KA), 0) == iota((q, q * KA), 1) // KA, 1.0, 0.0
    ).astype(jnp.bfloat16)
    low = iota((q, LANES), 1) < BLK
    return want, eye, spread, low


def row_terms(read, code, group, near, own, eye, spread, low):
    q = BLK // 2
    tiles = jnp.concatenate([read(c).astype(jnp.float32) for c in range(q)], axis=0)
    tiles = tiles.astype(jnp.bfloat16)

    def picked(j):
        one = jnp.where(code == j, 1.0, 0.0)
        pair = jnp.concatenate([one, one], axis=0).astype(jnp.bfloat16)
        return jnp.broadcast_to(pair[None], (q // 2,) + pair.shape).reshape(tiles.shape)

    left = jnp.concatenate([tiles * picked(j) for j in range(NEAR)], axis=1)
    products = jnp.dot(left, near, preferred_element_type=jnp.float32).astype(jnp.bfloat16)
    turned = lax.dot_general(
        eye, own, (((1,), (1,)), ((), ())), preferred_element_type=jnp.float32
    ).astype(jnp.bfloat16)
    wide = jnp.dot(turned, spread, preferred_element_type=jnp.float32).astype(jnp.bfloat16)
    rows = jnp.concatenate(
        [wide * jnp.where(group == s, 1.0, 0.0).astype(jnp.bfloat16) for s in range(KS)], axis=0
    )
    full = jnp.dot(rows, products, preferred_element_type=jnp.float32)
    terms = []
    for s in range(KS):
        part = full[s * LANES : (s + 1) * LANES]
        terms.append(
            jnp.where(low, part[:q], part[3 * q :])
            + pltpu.roll(jnp.where(low, part[q : 2 * q], part[2 * q : 3 * q]), BLK, 1)
        )
    return terms


def terms_kernel(a_ref, p_ref, code_ref, group_ref, out_ref, diag, stage):
    step = pl.program_id(0)
    q = BLK // 2
    want, eye, spread, low = constants()

    @pl.when(step == 0)
    def _():
        def one(t, _):
            diag[pl.ds(pl.multiple_of(t * LANES, LANES), LANES), :] = put_diagonal(p_ref[t], want, low)
            return 0

        lax.fori_loop(0, p_ref.shape[0], one, 0, unroll=4)

    for i in range(CHUNK):
        row = step * CHUNK + i
        terms = row_terms(
            lambda c: a_ref[i, :, c * LANES : (c + 1) * LANES],
            code_ref[i],
            group_ref[i],
            diag[pl.ds(pl.multiple_of(row * LANES, LANES), NEAR * LANES), :],
            p_ref[row + HB],
            eye,
            spread,
            low,
        )
        for s in range(KS):
            stage[pl.ds(s * CHUNK + i, q, stride=KS * CHUNK), :] = terms[s]
    out_ref[...] = stage[...].astype(jnp.bfloat16).reshape(out_ref.shape)


def row_codes(a_cols, tile_group):
    fine_rows = a_cols.shape[0]
    q = BLK // 2
    own = lax.axis_index(BOTH) * fine_rows + jnp.arange(fine_rows, dtype=jnp.int32)
    offset = a_cols - own[:, None] + HB
    code = jnp.broadcast_to(offset[:, :, None], (fine_rows, KA, LANES))
    group = jnp.tile(tile_group, (1, q)).reshape(fine_rows, 1, q * KA)
    return code, group


def local_terms(a_tiles, p_tiles, a_cols, tile_group):
    fine_rows = a_tiles.shape[0]
    q = BLK // 2
    near_p = extended(p_tiles, HB).reshape(fine_rows + 2 * HB, q, LANES)
    code, group = row_codes(a_cols, tile_group)
    steps = fine_rows // CHUNK
    return pl.pallas_call(
        terms_kernel,
        grid=(steps,),
        in_specs=[
            pl.BlockSpec((CHUNK, KA, BLK * BLK), lambda g: (g, 0, 0)),
            pl.BlockSpec((fine_rows + 2 * HB, q, LANES), lambda g: (0, 0, 0)),
            pl.BlockSpec((CHUNK, KA, LANES), lambda g: (g, 0, 0)),
            pl.BlockSpec((CHUNK, 1, q * KA), lambda g: (g, 0, 0)),
        ],
        out_specs=pl.BlockSpec((q, KS * CHUNK, LANES), lambda g: (0, g, 0)),
        out_shape=jax.ShapeDtypeStruct((q, fine_rows * KS, LANES), jnp.bfloat16),
        scratch_shapes=[
            pltpu.VMEM(((fine_rows + 2 * HB) * LANES, LANES), jnp.bfloat16),
            pltpu.VMEM((q * KS * CHUNK, LANES), jnp.float32),
        ],
        compiler_params=pltpu.CompilerParams(vmem_limit_bytes=40 * 1024 * 1024),
    )(a_tiles, near_p, code, group)


HALVES = 2
GROUP = 4
PIECE = 16
SPREAD = 40
AFTER = 2
FLIGHT = 2
SHARE = 2


def one_if(condition):
    return jnp.where(condition, 1.0, 0.0)


def halves_kernel(
    pair_count, devices,
    a_hbm, p_hbm, small_hbm, out_ref,
    a_ref, p_ref, small_ref,
    tiles, diag, turned, code, pick, stage, products, sums, term_ref, got, goals, sent_sums, got_sums, final, parts, far, far_goals, own,
    a_came, p_came, small_came, halo_sent, halo_came, sent, came, goal_sent, goal_came, cross_sent, cross_came, final_sent, final_came, self_came, far_sent, far_came, far_goal_sent, far_goal_came,
):
    q = BLK // 2
    me = lax.axis_index("rows") * pair_count + lax.axis_index("pair")
    team = devices // HALVES
    half, mine = lax.div(me, team), lax.rem(me, team)
    turn = half * (team // 2)
    mirror = me ^ (devices - team // 2)
    my_slice = mine ^ turn
    fine_rows = turned.shape[0] // BLK
    strips = got.shape[0]
    chunks = fine_rows // PIECE
    coarse_rows = parts.shape[1] // KC
    members = team * KC
    ahead, behind = lax.rem(me + 1, devices), lax.rem(me + devices - 1, devices)

    def at(device):
        return (lax.div(device, pair_count), lax.rem(device, pair_count))

    def copy(src, dst, send_sem, recv_sem, device):
        return pltpu.make_async_remote_copy(
            src_ref=src,
            dst_ref=dst,
            send_sem=send_sem,
            recv_sem=recv_sem,
            device_id=at(device),
            device_id_type=pl.DeviceIdType.MESH,
        )

    def whole_rows(index, count):
        return pl.ds(pl.multiple_of(index * count, count), count)

    def a_copy(order):
        rows = whole_rows(lax.rem(order + 1, chunks), PIECE)
        return pltpu.make_async_copy(a_hbm.at[rows], a_ref.at[rows], a_came.at[order])

    def p_copy(t):
        rows = whole_rows(t, 8 * q)
        return pltpu.make_async_copy(p_hbm.at[rows], p_ref.at[rows], p_came.at[t])

    small = pltpu.make_async_copy(small_hbm, small_ref, small_came)
    edge = HB * LANES
    inner = fine_rows * LANES
    halo_up = copy(diag.at[pl.ds(inner, edge)], diag.at[pl.ds(0, edge)], halo_sent.at[0], halo_came.at[0], ahead)
    halo_down = copy(diag.at[pl.ds(edge, edge)], diag.at[pl.ds(inner + edge, edge)], halo_sent.at[1], halo_came.at[1], behind)

    def member(k):
        return mine ^ k

    def goal_copy(k):
        return copy(goals.at[mine], goals.at[mine], goal_sent, goal_came, half * team + member(k))

    def strip(slot, g):
        return (slot ^ turn) * strips + g

    def term_part(k, chunk):
        rows = whole_rows(chunk, KS * PIECE)
        return copy(term_ref.at[strip(member(k), 0), rows], got.at[0, mine, rows], sent.at[0], came.at[0], half * team + member(k))

    def term_rest(k, g):
        return copy(term_ref.at[strip(member(k), g)], got.at[g, mine], sent.at[g], came.at[g], half * team + member(k))

    def cross_copy(n):
        return copy(sent_sums.at[n], got_sums.at[n], cross_sent.at[n], cross_came.at[n], mirror)

    held = coarse_rows * KC
    batch = members // held
    batches = team // batch

    def first_owner(n):
        return lax.rem(lax.rem(n, batches) + my_slice, batches) * batch

    def final_copy(n, b):
        return copy(
            final.at[n, whole_rows(b, held)],
            parts.at[strip(mine, lax.div(n, batches))],
            final_sent,
            final_came,
            half * team + first_owner(n) + b,
        )

    holders = team // SHARE
    both_hold = lax.rem(mine, SHARE) == 0
    far_team = (1 - half) * team

    def far_part(h, chunk):
        rows = whole_rows(chunk, KS * PIECE)
        to = lax.rem(h * SHARE + mine, team) // SHARE * SHARE
        place = (to ^ (team // 2 - turn)) * strips + strips - 1
        return copy(term_ref.at[place, rows], far.at[mine, rows], far_sent, far_came, far_team + to)

    def far_goal(h):
        return copy(goals.at[mine], far_goals.at[mine], far_goal_sent, far_goal_came, far_team + h * SHARE)

    some = pl.ds(0, holders)
    far_terms = copy(far.at[some], far.at[some], far_sent, far_came, mirror)
    far_terms_in = copy(far, far, far_sent, far_came, mirror)
    far_goals_out = copy(far_goals.at[some], far_goals.at[some], far_goal_sent, far_goal_came, mirror)
    far_goals_in = copy(far_goals, far_goals, far_goal_sent, far_goal_came, mirror)

    others = pl.ds(0, team - 1)
    all_goals = copy(goals.at[others], goals.at[others], goal_sent, goal_came, mirror)
    all_terms = [copy(got.at[g, others], got.at[g, others], sent.at[g], came.at[g], mirror) for g in range(strips)]
    but_own = pl.ds(0, strips * (team - 1))
    all_final = copy(parts.at[but_own], parts.at[but_own], final_sent, final_came, mirror)

    barrier = pltpu.get_barrier_semaphore()
    for o in range(1, devices):
        pl.semaphore_signal(
            barrier, inc=1, device_id=at(lax.rem(me + o, devices)), device_id_type=pl.DeviceIdType.MESH
        )
    for t in range(fine_rows // 8):
        p_copy(t).start()
    small.start()
    for order in range(chunks):
        a_copy(order).start()

    r128, k128 = iota((LANES, LANES), 0), iota((LANES, LANES), 1)
    want = one_if((r128 // BLK == k128 // BLK) & (r128 % BLK == 2 * (k128 % q) + (k128 // q) % 2)).astype(jnp.bfloat16)
    perm = one_if((r128 // BLK == k128 // BLK) & (k128 % BLK == 2 * (r128 % q) + (r128 % BLK) // q)).astype(jnp.bfloat16)
    low = iota((q, LANES), 1) < BLK

    small.wait()
    offset = small_ref[:KA, :] - (me * fine_rows + iota((KA, fine_rows), 1)) + HB
    for i in range(fine_rows):
        code[i] = jnp.broadcast_to(offset[:, i : i + 1], (KA, LANES))
    repeat = one_if(iota((KA, q * KA), 1) % KA == iota((KA, q * KA), 0)).astype(jnp.bfloat16)
    pick[...] = lax.dot_general(
        small_ref[KA : 2 * KA, :].astype(jnp.float32).astype(jnp.bfloat16),
        repeat,
        (((0,), (0,)), ((), ())),
        preferred_element_type=jnp.float32,
    )
    count = fine_rows * KS
    term, fine = iota((fine_rows, count), 1), iota((fine_rows, count), 0)
    goal_rows = []
    for s in range(KS):
        place = one_if(term == (fine // PIECE) * (KS * PIECE) + s * PIECE + fine % PIECE).astype(jnp.bfloat16)
        values = jnp.where(
            iota((KA, fine_rows), 0) == 0,
            jnp.broadcast_to(small_ref[2 * KA + KS : 2 * KA + KS + 1, :], (KA, fine_rows)),
            jnp.broadcast_to(small_ref[2 * KA + s : 2 * KA + s + 1, :], (KA, fine_rows)),
        )
        values = values.astype(jnp.float32).astype(jnp.bfloat16)
        goal_rows.append(jnp.dot(values, place, preferred_element_type=jnp.float32))
    goals[mine] = goal_rows[0] + goal_rows[1]

    def prepare(t16, _):
        p_copy(2 * t16).wait()
        p_copy(2 * t16 + 1).wait()
        tiles[...] = p_ref[whole_rows(t16, 16 * q), :].astype(jnp.float32)
        for t2 in range(8):
            flats = []
            for u in range(2):
                flat = tiles[pl.ds(t2 // 4 * 8 * q + t2 % 4 * 2 + u, q, stride=8), :]
                t = t16 * 16 + 2 * t2 + u
                diag[whole_rows(t + HB, LANES), :] = put_diagonal(flat, want, low)
                flats.append((flat, pltpu.roll(flat, BLK, 1)))
            both = jnp.concatenate(
                [jnp.where(low, flats[0][0], flats[1][1]), jnp.where(low, flats[0][1], flats[1][0])], axis=0
            ).astype(jnp.bfloat16)
            turned[whole_rows(t16 * 8 + t2, LANES), :] = lax.dot_general(
                perm, both, (((1,), (1,)), ((), ())), preferred_element_type=jnp.float32
            ).astype(jnp.bfloat16)
        return 0

    lax.fori_loop(0, fine_rows // 16, prepare, 0)
    pl.semaphore_wait(barrier, devices - 1)
    halo_up.start()
    halo_down.start()
    for k in range(1, team):
        goal_copy(k).start()
    for h in range(holders):
        far_goal(h).start()

    even = one_if(iota((q, q * KA), 1) // KA == iota((q, q * KA), 0)).astype(jnp.bfloat16)

    def full_mask(condition):
        one = one_if(condition)
        pair = jnp.concatenate([one, one], axis=0).astype(jnp.bfloat16)
        return jnp.broadcast_to(pair[None], (q // 2,) + pair.shape).reshape(q * KA, LANES)

    def full(condition):
        return jnp.broadcast_to(condition[None], (q, KA, LANES)).reshape(q * KA, LANES)

    def multiply(first):
        for u2 in range(GROUP // 2):
            row = first + 2 * u2
            near = [diag[whole_rows(row + j, LANES), :] for j in range(NEAR + 1)]
            zero = jnp.zeros_like(near[0])
            middle = jnp.concatenate(
                [jnp.concatenate(near[1:3], axis=1), jnp.concatenate(near[3:5], axis=1)], axis=0
            )
            outer = jnp.concatenate(
                [jnp.concatenate([near[0], zero], axis=1), jnp.concatenate([zero, near[5]], axis=1)], axis=0
            )
            rows = [a_ref[row], a_ref[row + 1]]
            edges = jnp.dot(jnp.concatenate(rows, axis=1), outer, preferred_element_type=jnp.float32)
            for u in range(2):
                which = code[row + u] + u
                upper = rows[u] * full_mask((which == 3) | (which == 4))
                inside = jnp.dot(
                    jnp.concatenate([rows[u] - upper, upper], axis=1), middle, preferred_element_type=jnp.float32
                )
                result = jnp.where(
                    full(which == NEAR * u),
                    edges[:, u * LANES : (u + 1) * LANES],
                    jnp.where(full((which == 1) | (which == 3)), inside[:, :LANES], inside[:, LANES:]),
                )
                at_row = (2 * u2 + u) * q * KA
                products[at_row : at_row + q * KA, :] = result.astype(jnp.bfloat16)

    def add_groups(first):
        for u in range(GROUP):
            one = even * jnp.broadcast_to(pick[pl.ds(first + u, 1), :], even.shape).astype(jnp.bfloat16)
            both = jnp.dot(
                jnp.concatenate([even - one, one], axis=0),
                products[u * q * KA : (u + 1) * q * KA, :],
                preferred_element_type=jnp.float32,
            )
            s0, s1 = both[:q], both[q:]
            t0, t1 = pltpu.roll(s0, BLK, 1), pltpu.roll(s1, BLK, 1)
            sums[u * BLK : (u + 1) * BLK, :] = jnp.concatenate(
                [jnp.where(low, s0, t1), jnp.where(low, t0, s1)], axis=0
            ).astype(jnp.bfloat16)

    def project(first):
        for u in range(GROUP):
            row = first + u
            both = jnp.dot(
                turned[whole_rows(row, BLK), :],
                sums[u * BLK : (u + 1) * BLK, :],
                preferred_element_type=jnp.float32,
            )
            even_rows, odd_rows = both[:q], both[q:]
            t0, t1 = pltpu.roll(even_rows, BLK, 1), pltpu.roll(odd_rows, BLK, 1)
            place = lax.rem(row, PIECE)
            stage[pl.ds(place, q, stride=SPREAD), :] = jnp.where(low, even_rows, t1)
            stage[pl.ds(PIECE + place, q, stride=SPREAD), :] = jnp.where(low, t0, odd_rows)

    groups = fine_rows // GROUP
    per = PIECE // GROUP

    def first_row(index):
        return lax.rem(index + per, groups) * GROUP

    def step(t, _):
        @pl.when((lax.rem(t, per) == 0) & (t < groups))
        def _():
            a_copy(lax.div(t, per)).wait()

        @pl.when(t == (chunks - 2) * per)
        def _():
            halo_up.wait_recv()
            halo_down.wait_recv()

        project(first_row(jnp.maximum(t - 2, 0)))
        add_groups(first_row(jnp.clip(t - 1, 0, groups - 1)))
        multiply(first_row(jnp.minimum(t, groups - 1)))

        @pl.when((t >= AFTER) & (lax.rem(t - AFTER, per) == per - 1))
        def _():
            chunk = lax.rem(lax.div(t - AFTER, per) + 1, chunks)
            rows = whole_rows(chunk, KS * PIECE)
            for pair in range(q):
                term_ref[pair, rows, :] = stage[pair * SPREAD : pair * SPREAD + KS * PIECE, :].astype(jnp.bfloat16)
            for k in range(team - 1, 0, -1):
                term_part(k, chunk).start()
            for h in range(holders):
                far_part(h, chunk).start()

        return 0

    lax.fori_loop(0, groups + AFTER, step, 0)
    for g in range(1, strips):
        for k in range(team - 1, 0, -1):
            term_rest(k, g).start()
    keep = [pltpu.make_async_copy(term_ref.at[strip(mine, g)], got.at[g, mine], self_came.at[g]) for g in range(strips)]
    for transfer in keep:
        transfer.start()
    all_goals.wait_recv()
    all_terms[0].wait_recv()
    keep[0].wait()

    def everyone(rows, row, copies):
        return jnp.concatenate([jnp.broadcast_to(rows[j, row : row + 1, :], (copies, count)) for j in range(team)], axis=1)

    def hot_slots(rows):
        slot = everyone(rows, 1, 2 * KA)
        return one_if(slot == iota(slot.shape, 0).astype(jnp.float32)).astype(jnp.bfloat16)

    coarse, slot_hot = everyone(goals, 0, KA), hot_slots(goals)

    def sums_of(coarse, slot_hot, values, which, n):
        first = (which * team + first_owner(n)) * coarse_rows
        pieces = []
        for j in range(batch * coarse_rows):
            one = one_if(coarse == (first + j).astype(jnp.float32))
            pieces.append(slot_hot * jnp.concatenate([one, one], axis=0).astype(jnp.bfloat16))
        return jnp.dot(jnp.concatenate(pieces, axis=0), values, preferred_element_type=jnp.float32)

    def half_sums(which, n):
        return sums_of(coarse, slot_hot, got[lax.div(n, batches)].reshape(-1, LANES), which, n)

    steps = strips * batches

    def crosses(n):
        return jnp.logical_not(both_hold) | (n < steps - batches)


    def prepared(n):
        sent_sums[n] = half_sums(1 - half, n).astype(jnp.bfloat16)

    def cross(n, _):
        @pl.when(crosses(n))
        def _():
            prepared(n)
            cross_copy(n).start()

        return 0

    lax.fori_loop(0, FLIGHT, cross, 0)

    def finish(n, _):
        @pl.when(n == batches - FLIGHT)
        def _():
            for g in range(1, strips):
                all_terms[g].wait_recv()
                keep[g].wait()

        @pl.when(both_hold & (n == steps - batches))
        def _():
            far_goals_in.wait_recv()
            far_terms_in.wait_recv()

        @pl.when((n < steps - FLIGHT) & crosses(n + FLIGHT))
        def _():
            prepared(n + FLIGHT)

        own[...] = half_sums(half, n)

        @pl.when((n < steps - FLIGHT) & crosses(n))
        def _():
            cross_copy(n).wait_send()

        @pl.when((n < steps - FLIGHT) & crosses(n + FLIGHT))
        def _():
            cross_copy(n + FLIGHT).start()

        @pl.when(crosses(n))
        def _():
            cross_copy(n).wait_recv()
            final[n] = (own[...] + got_sums[n].astype(jnp.float32)).astype(jnp.bfloat16)

        @pl.when(jnp.logical_not(crosses(n)))
        def _():
            more = sums_of(everyone(far_goals, 0, KA), hot_slots(far_goals), far[...].reshape(-1, LANES), half, n)
            final[n] = (own[...] + more).astype(jnp.bfloat16)

        for b in range(batch):
            owner = first_owner(n) + b

            @pl.when(owner != mine)
            def _():
                final_copy(n, b).start()

            @pl.when(owner == mine)
            def _():
                parts[strip(mine, lax.div(n, batches))] = final[n, b * held : (b + 1) * held, :]

        return 0

    lax.fori_loop(0, steps, finish, 0)
    halo_up.wait_send()
    halo_down.wait_send()
    all_goals.wait_send()
    for g in range(strips):
        all_terms[g].wait_send()
    for n in range(steps - FLIGHT, steps):

        @pl.when(crosses(n))
        def _():
            cross_copy(n).wait_send()

    far_terms.wait_send()
    far_goals_out.wait_send()
    all_final.wait_send()
    all_final.wait_recv()
    for column in range(parts.shape[0]):
        out_ref[:, column * LANES : (column + 1) * LANES] = parts[column]


def by_halves(a_tiles, p_tiles, a_cols, tile_group, coarse_slots, aggregate):
    fine_rows, _, width = a_tiles.shape
    q = BLK // 2
    devices, pair_count = lax.axis_size(BOTH), lax.axis_size("pair")
    team = devices // HALVES
    strips = width // team // LANES
    count = fine_rows * KS
    coarse_rows = fine_rows // RATIO
    chunks = fine_rows // PIECE
    members = team * KC
    a = a_tiles.reshape(fine_rows, KA, q, LANES).transpose(0, 2, 1, 3).reshape(fine_rows, q * KA, LANES)
    p = p_tiles.reshape(fine_rows // 8, 8, q, LANES).transpose(0, 2, 1, 3).reshape(fine_rows * q, LANES)
    small = jnp.concatenate([a_cols.T, tile_group.T, coarse_slots.T, aggregate.reshape(1, fine_rows)], axis=0)
    bf16, f32, i32 = jnp.bfloat16, jnp.float32, jnp.int32
    dma = pltpu.SemaphoreType.DMA
    return pl.pallas_call(
        functools.partial(halves_kernel, pair_count, devices),
        in_specs=[pl.BlockSpec(memory_space=pltpu.HBM)] * 3,
        out_specs=pl.BlockSpec(memory_space=pltpu.VMEM),
        out_shape=jax.ShapeDtypeStruct((coarse_rows * KC, width), bf16),
        scratch_shapes=[
            pltpu.VMEM(a.shape, bf16),
            pltpu.VMEM(p.shape, bf16),
            pltpu.VMEM((2 * KA + KS + 1, fine_rows), i32),
            pltpu.VMEM((16 * q, LANES), f32),
            pltpu.VMEM(((fine_rows + 2 * HB) * LANES, LANES), bf16),
            pltpu.VMEM((fine_rows * BLK, BLK), bf16),
            pltpu.VMEM((fine_rows, KA, LANES), i32),
            pltpu.VMEM((fine_rows, q * KA), f32),
            pltpu.VMEM((q * SPREAD, LANES), f32),
            pltpu.VMEM((GROUP * q * KA, LANES), bf16),
            pltpu.VMEM((GROUP * BLK, LANES), bf16),
            pltpu.VMEM((width // LANES, count, LANES), bf16),
            pltpu.VMEM((strips, team, count, LANES), bf16),
            pltpu.VMEM((team, KA, count), f32),
            pltpu.VMEM((strips * coarse_rows, members, LANES), bf16),
            pltpu.VMEM((strips * coarse_rows, members, LANES), bf16),
            pltpu.VMEM((strips * coarse_rows, members, LANES), bf16),
            pltpu.VMEM((width // LANES, coarse_rows * KC, LANES), bf16),
            pltpu.VMEM((team, count, LANES), bf16),
            pltpu.VMEM((team, KA, count), f32),
            pltpu.VMEM((members, LANES), f32),
            dma((chunks,)),
            dma((fine_rows // 8,)),
            dma,
            dma((2,)),
            dma((2,)),
            dma((strips,)),
            dma((strips,)),
            dma,
            dma,
            dma((strips * coarse_rows,)),
            dma((strips * coarse_rows,)),
            dma,
            dma,
            dma((strips,)),
            dma,
            dma,
            dma,
            dma,
        ],
        compiler_params=pltpu.CompilerParams(
            collective_id=0, has_side_effects=True, vmem_limit_bytes=53 * 1024 * 1024
        ),
    )(a, p, small)


def routed(terms, coarse_slots, aggregate):
    fine_rows = aggregate.shape[0]
    q = BLK // 2
    width = BLK * BLK
    rows_count, pair_count = lax.axis_size("rows"), lax.axis_size("pair")
    flat = terms.reshape(q, fine_rows // CHUNK, KS, CHUNK, 2, BLK)
    flat = flat.transpose(1, 3, 2, 4, 0, 5).reshape(fine_rows, KS, width)
    group_size = fine_rows // RATIO * pair_count
    capacity = 2 * fine_rows // rows_count
    dest_group = aggregate // group_size
    local_rows = aggregate - dest_group * group_size
    targets = local_rows[:, None] * KC + coarse_slots
    order = jnp.arange(fine_rows)
    same = (dest_group[:, None] == dest_group[None, :]) & (order[None, :] < order[:, None])
    position = dest_group * capacity + jnp.sum(same.astype(jnp.int32), axis=1)

    def exchange(values):
        buffer = jnp.zeros((rows_count * capacity,) + values.shape[1:], values.dtype)
        buffer = buffer.at[position].set(values)
        return lax.all_to_all(buffer, "rows", split_axis=0, concat_axis=0, tiled=True)

    got = exchange(flat).reshape(-1, width).astype(jnp.float32)
    panel = jax.ops.segment_sum(
        got, exchange(targets).reshape(-1), num_segments=group_size * KC
    )
    panel = panel.reshape(group_size, KC, width)
    return lax.psum_scatter(panel, "pair", scatter_dimension=0, tiled=True)


def body(a_tiles, p_tiles, a_cols, tile_group, coarse_slots, aggregate):
    fine_rows, width = p_tiles.shape
    devices = lax.axis_size(BOTH)
    if devices * LANES != width:
        return routed(local_terms(a_tiles, p_tiles, a_cols, tile_group), coarse_slots, aggregate)
    result = by_halves(a_tiles, p_tiles, a_cols, tile_group, coarse_slots, aggregate)
    return result.reshape(fine_rows // RATIO, KC, width).astype(jnp.float32)


def solution(mesh):
    return jax.shard_map(
        body,
        mesh=mesh,
        in_specs=(
            P(BOTH, None, None),
            P(BOTH, None),
            P(BOTH, None),
            P(BOTH, None),
            P(BOTH, None),
            P(BOTH),
        ),
        out_specs=P(BOTH, None, None),
        check_vma=False,
    )
```
